256 devices in a mesh: ctx: 8 (over y_lo, x), exp: 32 (over z, y_hi, core).
Axes of the slice: x: 4, y: 4 (y_hi: 2, y_lo: 2; y = y_hi * 2 + y_lo), z: 8, core: 2. Of those that a mesh axis runs over, the one named last changes fastest.
Arguments:
- queries: bfloat16 [2, 256, 64, 576], P(None, 'exp'), may hold values from -512 to 512
- prompt_cache: bfloat16 [32, 4096, 576], P('exp', 'ctx'), may hold values from -6 to 6
- new_latent: bfloat16 [2, 256, 576], P(None, 'exp'), may hold values from -12 to 12
- parents: int32 [32, 8], P('exp'), may hold values from 0 to 7
- lengths: int32 [32], P('exp'), may hold values from 2048 to 4096, as said below
- value_weight: bfloat16 [64, 512, 128], P('exp'), may hold values from -2 to 2
- output_weight: bfloat16 [8192, 7168], P('exp'), may hold values from -0.0625 to 0.0625
- residual: bfloat16 [2, 256, 7168], P(None, 'exp'), may hold values from -6 to 6
- norm_gain: float32 [7168], replicated, may hold values from 0.5 to 1.5
- expert_ids: int32 [2, 256, 8], P(None, 'exp'), may hold values from 0 to 31, all different within a row; in each aligned block of 8 rows (0 to 7, 8 to 15, ..., all dimensions but the last counted through in order) at most 4 rows name the same one
- expert_weights: float32 [2, 256, 8], P(None, 'exp'), may hold values from 0.1 to 1
- expert_gate: bfloat16 [32, 7168, 1024], P('exp', None, 'ctx'), may hold values from -0.0625 to 0.0625
- expert_up: bfloat16 [32, 7168, 1024], P('exp', None, 'ctx'), may hold values from -0.0625 to 0.0625
- expert_down: bfloat16 [32, 1024, 7168], P('exp', 'ctx'), may hold values from -0.1875 to 0.1875
Outputs:
- layer_out: bfloat16 [2, 256, 7168], P(None, 'exp', 'ctx')
The draws below stay inside these ranges and needn't reach their ends.
Inputs may be any that keep to these rules, and one draw needn't show every extreme that they name: `lengths`: some request uses all 4096 positions. `expert_ids`: each row names 8 different experts; in each aligned block of 8 rows of one step (the rows of one index of exp) no expert is named more than 4 times, a bound that some block reaches.
All inputs are finite; a program needn't handle non-finite values.
Results may differ from the reference program's by a relative error of at most 0.018.
Values may be sent and summed in bfloat16 or wider, within the bound.
A program may use at most 128 MiB of HBM per device.

```python
import math
import jax
import jax.numpy as jnp
import numpy as np
from jax import lax

D = 7168
LAT = 512
VDIM = 128
TOPK = 8
H = 64
FFN_E = 1024
BEAMS = 8
STEPS = 2
KDIM = 576
EXPERTS = 32
REQS = 32
ROWS = 8
NROWS = 256
PROMPT = 4096
HEADS_DEV = 2
HSLICE = 128
CAP = 4
N_CTX = 8
N_EXP = 32


SCALE = 0.07216878364870322


def cache_base(key):
    base_draw = jnp.clip(jax.random.normal(key, (REQS, PROMPT, KDIM), jnp.float32), -6.0, 6.0)
    request = jnp.arange(REQS)
    first_pos = request * 7 % (PROMPT // 4)
    second_pos = first_pos + PROMPT // 4
    source = base_draw[request, first_pos]
    turned = jnp.concatenate([jnp.roll(source[:, :LAT], 1, axis=-1), source[:, LAT:]], axis=-1)
    return (base_draw.at[request, second_pos].set(turned), first_pos, second_pos)


def draw_prompt_cache(key, part):
    base_draw = cache_base(key)[0]
    return base_draw.astype(jnp.bfloat16)


def draw_queries(key, part):
    own_key = jax.random.fold_in(key, 5)
    noise = jnp.clip(jax.random.normal(own_key, (STEPS, NROWS, H, KDIM), jnp.float32), -6.0, 6.0)
    base_draw, first_pos, second_pos = cache_base(key)
    request = jnp.arange(REQS)
    first_key = base_draw[request, first_pos]
    second_key = base_draw[request, second_pos]
    unit = 1.0 / (KDIM * SCALE)
    boost = 1.0
    step_list = [0]
    beam_list = [0]
    for step_index in step_list:
        for beam_index in beam_list:
            for head_index in range(3):
                strength = boost * (200.0 + 100.0 * head_index) * unit
                aligned = strength * 0.5 * (first_key + second_key) + 2.0 * unit * first_key
                noise = noise.at[step_index, request * BEAMS + beam_index, head_index].set(jnp.clip(aligned, -512.0, 512.0))
    return noise.astype(jnp.bfloat16)


def draw_lengths(key, part):
    own_key = jax.random.fold_in(key, 7)
    drawn = jax.random.randint(own_key, (REQS,), PROMPT // 2, PROMPT + 1)
    chosen = jax.random.randint(jax.random.fold_in(own_key, 1), (), 0, REQS)
    return jnp.where(jnp.arange(REQS) == chosen, PROMPT, drawn).astype(jnp.int32)


def plant(values, key, low, high):
    extent = values.shape
    place = [jax.random.randint(jax.random.fold_in(key, axis), (), 0, extent[axis]) for axis in range(len(extent))]
    values = values.at[tuple(place)].set(low)
    longest = extent.index(max(extent))
    place[longest] = (place[longest] + 1) % extent[longest]
    return values.at[tuple(place)].set(high)


def levels(rng, shape, split, low, high):
    def one(axis_at, shards_of):
        heights = jax.random.uniform(jax.random.fold_in(jax.random.fold_in(rng, 6), axis_at), (shards_of,), jnp.float32, low / len(split), high / len(split))
        return jnp.repeat(jnp.exp(heights), shape[axis_at] // shards_of).reshape((-1,) + (1,) * (len(shape) - axis_at - 1))

    loudness = one(*split[0])
    for cut in split[1:]:
        loudness = loudness * one(*cut)
    return loudness


def assign_block(key, own, number, rows, amount, top, most, lean):
    sequence = jax.random.permutation(key, amount)
    heavy_load, usual = portions_of(amount, rows * top, most, lean, True), portions_of(amount, rows * top, most, lean, False)
    places = jnp.arange(amount)

    def named(sizes, rotation):
        used = int((sizes > 0).sum())
        fixed = max(1, used // 4)
        passed = fixed + (places - fixed + rotation * (used - fixed)) % max(1, amount - fixed)
        return jnp.zeros((amount,), jnp.int32).at[sequence[jnp.where(places < fixed, places, passed)]].set(jnp.asarray(sizes, jnp.int32))

    sizes = jnp.where(number % 4 == 0, named(heavy_load, number // 4), named(usual, number - number // 4 - 1))
    mixed = jax.random.permutation(jax.random.fold_in(own, 3), amount)
    source_of, sink = mixed[0:amount // 2 * 2:2], mixed[1:amount // 2 * 2:2]
    margin = jnp.minimum(sizes[source_of] - 1, most - sizes[sink]) // 2
    margin = jnp.where((source_of == sequence[0]) | (sink == sequence[0]) | (sizes[sink] == 0), 0, jnp.maximum(margin, 0))
    passed = jax.random.randint(jax.random.fold_in(own, 4), (amount // 2,), 0, 1 << 20) % (margin + 1)
    sizes = sizes.at[source_of].add(-passed).at[sink].add(passed)
    items = jnp.searchsorted(jnp.cumsum(sizes), jnp.arange(rows * top), side="right").astype(jnp.int32)
    table = items.reshape(top, rows).T
    table = table[jax.random.permutation(jax.random.fold_in(own, 1), rows)]
    rotation = jax.random.randint(jax.random.fold_in(own, 2), (rows, 1), 0, top)
    return jnp.take_along_axis(table, (jnp.arange(top)[None, :] + rotation) % top, axis=1)


def portions_of(amount, total, most, skew, full):
    loads = [(1 << 20) // math.isqrt(standing ** skew) + 1 for standing in range(1, amount + 1)]
    largest = most if full else min(most, max(-(-total // amount), total * loads[0] // sum(loads)))
    least = 1 if total - largest >= amount - 1 else 0
    given, surplus = [largest] + [least] * (amount - 1), total - largest - least * (amount - 1)
    while surplus > 0:
        movable = [i for i in range(1, amount) if given[i] < largest] or [i for i in range(1, amount) if given[i] < most]
        whole, left = sum([loads[i] for i in movable]), surplus
        for i in movable:
            more = min(most - given[i], max(1, left * loads[i] // whole), surplus)
            given[i] = given[i] + more
            surplus = surplus - more
    return np.array(given)


def centred(key, shape, spread, bound, cuts=(), kind=jnp.bfloat16):
    level = levels(key, shape, cuts, -0.22, 0.18) if cuts else 1.0
    entries = jax.random.normal(key, shape, jnp.float32) * spread * level
    return jnp.minimum(jnp.maximum(entries, -bound), bound).astype(kind)


def setup_inputs(seed: int = 0) -> dict:
    key_list = jax.random.split(jax.random.key(seed), 15)
    queries = draw_queries(jax.random.fold_in(key_list[14], 71), 0)
    prompt_cache = draw_prompt_cache(jax.random.fold_in(key_list[14], 71), 0)
    new_latent = centred(key_list[2], (STEPS, NROWS, KDIM), 2.5, 12.0, ((1, 32),))
    parents = plant(jax.random.randint(key_list[3], (REQS, BEAMS), 0, BEAMS), jax.random.fold_in(key_list[3], 1), 0, BEAMS - 1).astype(jnp.int32)
    lengths = draw_lengths(jax.random.fold_in(key_list[14], 71), 0)
    value_weight = centred(key_list[5], (H, LAT, VDIM), (LAT // 64) ** -0.5, 2.0, ((0, 32),))
    output_weight = centred(key_list[6], (H * VDIM, D), (H * VDIM) ** -0.5, 0.0625, ((0, 32),))
    residual = centred(key_list[7], (STEPS, NROWS, D), 1.0, 6.0, ((1, 32),))
    norm_gain = jnp.clip(1.0 + 0.1 * jax.random.normal(key_list[8], (D,), jnp.float32), 0.5, 1.5)
    expert_ids_keys = jax.random.split(jax.random.fold_in(key_list[9], 1), STEPS * NROWS // ROWS)
    expert_ids_turns = jax.random.permutation(jax.random.fold_in(key_list[9], 3), STEPS * NROWS // ROWS)
    expert_ids = jax.vmap(lambda own, number: assign_block(jax.random.fold_in(key_list[9], 2), own, number, ROWS, EXPERTS, TOPK, CAP, 2))(expert_ids_keys, expert_ids_turns).reshape((STEPS, NROWS, TOPK))
    expert_weights = jnp.clip(jnp.exp(math.log(1.0) - 2.3025851 * jax.random.uniform(key_list[10], (STEPS, NROWS, TOPK), jnp.float32) ** levels(key_list[10], (STEPS, NROWS, TOPK), ((1, 32),), -0.2, 0.2)), 0.1, 1.0)
    expert_gate = centred(key_list[11], (EXPERTS, D, FFN_E), D ** -0.5, 0.0625, ((0, 32), (2, 8)))
    expert_up = centred(key_list[12], (EXPERTS, D, FFN_E), D ** -0.5, 0.0625, ((0, 32), (2, 8)))
    expert_down = centred(key_list[13], (EXPERTS, FFN_E, D), FFN_E ** -0.5, 0.1875, ((0, 32), (1, 8)))
    return dict(queries=queries, prompt_cache=prompt_cache, new_latent=new_latent, parents=parents, lengths=lengths, value_weight=value_weight, output_weight=output_weight, residual=residual, norm_gain=norm_gain, expert_ids=expert_ids, expert_weights=expert_weights, expert_gate=expert_gate, expert_up=expert_up, expert_down=expert_down)


SCALE = 0.07216878364870322
NEGATIVE = -1e+30

def rounded(value):
    return lax.optimization_barrier(value.astype(jnp.bfloat16)).astype(jnp.float32)

def attend_request(request_index, queries, prompt_cache, new_latent, parents, lengths):
    first_row = request_index * BEAMS
    query_rows = lax.dynamic_slice_in_dim(queries, first_row, BEAMS, 1)
    query_wide = query_rows.astype(jnp.float32)
    new_rows = lax.dynamic_slice_in_dim(new_latent, first_row, BEAMS, 1).astype(jnp.float32)
    cache_rows = lax.dynamic_index_in_dim(prompt_cache, request_index, 0, keepdims=False)
    parent_rows = lax.dynamic_index_in_dim(parents, request_index, 0, keepdims=False)
    length = lax.dynamic_index_in_dim(lengths, request_index, 0, keepdims=False)
    flat_queries = query_rows.reshape(STEPS * BEAMS * H, KDIM)
    scores = jnp.dot(flat_queries, cache_rows.T, preferred_element_type=jnp.float32) * SCALE
    scores = scores.reshape(STEPS, BEAMS, H, PROMPT)
    live_mask = jnp.arange(PROMPT) < length
    own_scores = jnp.einsum('sbhk,sbk->sbh', query_wide, new_rows) * SCALE
    parent_keys = jnp.take(new_rows[0], parent_rows, axis=0)
    tail_later = jnp.einsum('bhk,bk->bh', query_wide[1], parent_keys) * SCALE
    tail_scores = jnp.stack([jnp.full_like(tail_later, NEGATIVE), tail_later])
    tail_values = jnp.stack([jnp.zeros_like(parent_keys), parent_keys])[:, :, :LAT]
    prompt_peak = lax.optimization_barrier(jnp.max(jnp.where(live_mask, scores, NEGATIVE), axis=-1))
    peak_score = jnp.maximum(prompt_peak, jnp.maximum(own_scores, tail_scores))
    weights = jnp.where(live_mask, jnp.exp(scores - peak_score[..., None]), 0.0)
    own_weight = jnp.exp(own_scores - peak_score)
    tail_weight = jnp.exp(tail_scores - peak_score)
    weight_total = lax.optimization_barrier(jnp.sum(weights, axis=-1)) + own_weight + tail_weight
    numerator = jnp.dot(weights.reshape(STEPS * BEAMS * H, PROMPT).astype(jnp.bfloat16), cache_rows[:, :LAT], preferred_element_type=jnp.float32)
    numerator = numerator.reshape(STEPS, BEAMS, H, LAT)
    numerator = numerator + rounded(own_weight)[..., None] * new_rows[:, :, None, :LAT]
    numerator = numerator + rounded(tail_weight)[..., None] * tail_values[:, :, None, :]
    return (numerator / weight_total[..., None]).astype(jnp.bfloat16)

def reference(queries, prompt_cache, new_latent, parents, lengths, value_weight, output_weight, residual, norm_gain, expert_ids, expert_weights, expert_gate, expert_up, expert_down):

    def per_request(request_index):
        return attend_request(request_index, queries, prompt_cache, new_latent, parents, lengths)
    attended = lax.map(per_request, jnp.arange(REQS, dtype=jnp.int32))
    attended = jnp.transpose(attended, (1, 0, 2, 3, 4)).reshape(STEPS, NROWS, H, LAT)
    head_values = jnp.einsum('snhl,hlv->snhv', attended.astype(jnp.float32), value_weight.astype(jnp.float32)).astype(jnp.bfloat16)
    grouped = jnp.transpose(head_values.reshape(STEPS * NROWS, N_EXP, HEADS_DEV * VDIM), (1, 0, 2))
    weight_groups = output_weight.reshape(N_EXP, HEADS_DEV * VDIM, D)

    def add_group(carry, pair):
        return (carry + rounded(jnp.dot(pair[0], pair[1], preferred_element_type=jnp.float32)), None)
    attention_out = lax.scan(add_group, jnp.zeros((STEPS * NROWS, D), jnp.float32), (grouped, weight_groups))[0]
    layer_state = residual.reshape(STEPS * NROWS, D).astype(jnp.float32) + attention_out
    scale_row = lax.rsqrt(lax.optimization_barrier(jnp.mean(layer_state * layer_state, axis=-1, keepdims=True)) + 1e-06)
    normed = (layer_state * scale_row * norm_gain).astype(jnp.bfloat16)
    flat_ids = expert_ids.reshape(STEPS * NROWS, TOPK)
    flat_weights = expert_weights.reshape(STEPS * NROWS, TOPK)
    most_rows = STEPS * N_EXP * CAP

    def run_expert(carry, inputs):
        expert_index, gate_matrix, up_matrix, down_matrix = inputs
        hit_mask = flat_ids == expert_index
        row_weight = lax.optimization_barrier(jnp.sum(jnp.where(hit_mask, flat_weights, 0.0), axis=1))
        missed = 1 - jnp.any(hit_mask, axis=1).astype(jnp.int32)
        row_order = jnp.argsort(missed, stable=True)[:most_rows]
        picked = normed[row_order]
        gate_out = jnp.dot(picked, gate_matrix, preferred_element_type=jnp.float32)
        up_out = jnp.dot(picked, up_matrix, preferred_element_type=jnp.float32)
        hidden = (jax.nn.silu(gate_out) * up_out).astype(jnp.bfloat16)
        expert_out = jnp.zeros((most_rows, D), jnp.float32)
        for block_index in range(N_CTX):
            lower = block_index * HSLICE
            upper = lower + HSLICE
            expert_out = expert_out + rounded(jnp.dot(hidden[:, lower:upper], down_matrix[lower:upper], preferred_element_type=jnp.float32))
        return (carry.at[row_order].add(row_weight[row_order][:, None] * expert_out), None)
    mixture = lax.scan(run_expert, jnp.zeros((STEPS * NROWS, D), jnp.float32), (jnp.arange(EXPERTS, dtype=jnp.int32), expert_gate, expert_up, expert_down))[0]
    return (layer_state + mixture).astype(jnp.bfloat16).reshape(STEPS, NROWS, D)
```

```python
import jax
import jax.numpy as jnp
from jax import lax
from jax.sharding import PartitionSpec as P

SCALE = 0.07216878364870322
NEGATIVE = -1e30


def rounded(value):
    return lax.optimization_barrier(value.astype(jnp.bfloat16)).astype(jnp.float32)


def per_device(
    queries,
    prompt_cache,
    new_latent,
    parents,
    lengths,
    value_weight,
    output_weight,
    residual,
    norm_gain,
    expert_ids,
    expert_weights,
    expert_gate,
    expert_up,
    expert_down,
):
    steps, beams, heads, key_width = queries.shape
    latent = value_weight.shape[1]
    positions = prompt_cache.shape[1]
    width = residual.shape[2]
    ctx_count = lax.axis_size("ctx")
    exp_count = lax.axis_size("exp")
    ctx_index = lax.axis_index("ctx")
    rows = steps * beams
    mine = rows // ctx_count
    heads_dev = heads // exp_count
    col_width = width // ctx_count
    scores = (
        jnp.dot(
            queries.reshape(rows * heads, key_width),
            prompt_cache[0].T,
            preferred_element_type=jnp.float32,
        )
        * SCALE
    )
    position = ctx_index * positions + lax.broadcasted_iota(jnp.int32, (1, positions), 1)
    live = position < lengths[0]
    local_top = jnp.max(jnp.where(live, scores, NEGATIVE), axis=-1)
    weights = jnp.where(live, jnp.exp(scores - local_top[:, None]), 0.0)
    local_total = jnp.sum(weights, axis=-1)
    local_sum = jnp.dot(
        weights.astype(jnp.bfloat16), prompt_cache[0, :, :latent], preferred_element_type=jnp.float32
    ).astype(jnp.bfloat16)
    stats = jnp.stack([local_top, local_total]).reshape(2, ctx_count, mine * heads)
    stats = lax.all_to_all(stats, "ctx", split_axis=1, concat_axis=1, tiled=True)
    sums = lax.all_to_all(
        local_sum.reshape(ctx_count, mine * heads, latent),
        "ctx",
        split_axis=0,
        concat_axis=0,
        tiled=True,
    )
    flat_new = new_latent.reshape(rows, key_width)
    parent_keys = jnp.take(new_latent[0], parents[0], axis=0)
    flat_tail = jnp.concatenate([jnp.zeros_like(parent_keys), parent_keys])
    first = ctx_index * mine
    my_queries = lax.dynamic_slice_in_dim(queries.reshape(rows, heads, key_width), first, mine, 0)
    my_new = lax.dynamic_slice_in_dim(flat_new, first, mine, 0)
    my_tail = lax.dynamic_slice_in_dim(flat_tail, first, mine, 0)
    own = jnp.einsum("rhk,rk->rh", my_queries, my_new, preferred_element_type=jnp.float32) * SCALE
    tail = jnp.einsum("rhk,rk->rh", my_queries, my_tail, preferred_element_type=jnp.float32) * SCALE
    has_tail = (first + lax.broadcasted_iota(jnp.int32, (mine, 1), 0)) >= beams
    tail = jnp.where(has_tail, tail, NEGATIVE)
    own, tail = own.reshape(mine * heads), tail.reshape(mine * heads)
    peak = jnp.maximum(jnp.max(stats[0], axis=0), jnp.maximum(own, tail))
    factor = jnp.exp(stats[0] - peak)
    own_weight, tail_weight = jnp.exp(own - peak), jnp.exp(tail - peak)
    total = jnp.sum(stats[1] * factor, axis=0) + own_weight + tail_weight
    summed = jnp.sum(sums.astype(jnp.float32) * factor[..., None], axis=0).reshape(
        mine, heads, latent
    )
    own_weight = rounded(own_weight).reshape(mine, heads, 1)
    tail_weight = rounded(tail_weight).reshape(mine, heads, 1)
    summed = summed + own_weight * my_new[:, None, :latent].astype(jnp.float32)
    summed = summed + tail_weight * my_tail[:, None, :latent].astype(jnp.float32)
    attended = (summed / total.reshape(mine, heads, 1)).astype(jnp.bfloat16)
    by_head = lax.all_to_all(
        attended.reshape(mine, exp_count, heads_dev, latent),
        "exp",
        split_axis=1,
        concat_axis=0,
        tiled=True,
    ).reshape(exp_count * mine, heads_dev, latent)
    values = jnp.einsum(
        "nhl,hlv->nhv", by_head, value_weight, preferred_element_type=jnp.float32
    ).astype(jnp.bfloat16)
    shares = jnp.dot(
        values.reshape(exp_count * mine, -1), output_weight, preferred_element_type=jnp.float32
    ).astype(jnp.bfloat16)
    attention_out = lax.psum_scatter(shares, "exp", scatter_dimension=0, tiled=True)
    my_residual = lax.dynamic_slice_in_dim(residual.reshape(rows, width), first, mine, 0)
    state = my_residual.astype(jnp.float32) + attention_out.astype(jnp.float32)
    scale_row = lax.rsqrt(jnp.mean(state * state, axis=-1, keepdims=True) + 1e-06)
    normed = (state * scale_row * norm_gain).astype(jnp.bfloat16)
    chosen = expert_ids.reshape(rows, -1)[..., None] == lax.broadcasted_iota(
        jnp.int32, (1, 1, exp_count), 2
    )
    routing = jnp.sum(
        jnp.where(chosen, expert_weights.reshape(rows, -1)[..., None], 0.0), axis=1
    )
    routing = lax.all_gather(routing, "exp", tiled=True)
    mine_of = lax.dynamic_slice_in_dim(routing, lax.axis_index("exp"), 1, 1)
    every = lax.all_gather(normed, "exp")
    every = lax.all_gather(every, "ctx", axis=1).reshape(exp_count * rows, width)
    gate = jnp.dot(every, expert_gate[0], preferred_element_type=jnp.float32)
    up = jnp.dot(every, expert_up[0], preferred_element_type=jnp.float32)
    hidden = (jax.nn.silu(gate) * up).astype(jnp.bfloat16)
    partial = jnp.dot(hidden, expert_down[0], preferred_element_type=jnp.float32) * mine_of
    partial = partial.astype(jnp.bfloat16)
    mixture = lax.psum_scatter(partial, "ctx", scatter_dimension=1, tiled=True)
    mixture = lax.psum_scatter(mixture, "exp", scatter_dimension=0, tiled=True)
    state_cols = lax.all_to_all(
        state.reshape(mine, ctx_count, col_width), "ctx", split_axis=1, concat_axis=0, tiled=True
    )
    out = state_cols.reshape(rows, col_width) + mixture.astype(jnp.float32)
    return out.astype(jnp.bfloat16).reshape(steps, beams, col_width)


def solution(mesh):
    in_specs = (
        P(None, "exp", None, None),
        P("exp", "ctx", None),
        P(None, "exp", None),
        P("exp", None),
        P("exp"),
        P("exp", None, None),
        P("exp", None),
        P(None, "exp", None),
        P(),
        P(None, "exp", None),
        P(None, "exp", None),
        P("exp", None, "ctx"),
        P("exp", None, "ctx"),
        P("exp", "ctx", None),
    )
    out_specs = P(None, "exp", "ctx")
    return jax.shard_map(
        per_device, mesh=mesh, in_specs=in_specs, out_specs=out_specs, check_vma=False
    )
```

```python
import functools

import jax
import jax.numpy as jnp
from jax import lax
from jax.experimental import pallas as pl
from jax.experimental.pallas import tpu as pltpu
from jax.sharding import PartitionSpec as P

SCALE = 0.07216878364870322
NEGATIVE = -1e30
BF16 = jnp.bfloat16
F32 = jnp.float32
N_CTX = 8
N_EXP = 32
ROWS = 16
MINE = 2
HEADS = 64
LAT = 512
COLS = 896
VMEM_LIMIT = 56 * 1024 * 1024


def coordinates():
    c, e = lax.axis_index("ctx"), lax.axis_index("exp")
    x, y_lo = lax.rem(c, 4), c // 4
    z, y_hi, core = e // 4, lax.rem(e // 2, 2), lax.rem(e, 2)
    return c, e, x, y_hi * 2 + y_lo, z, core


def device(x, y, z, core):
    return (lax.rem(y, 2) * 4 + x, z * 4 + (y // 2) * 2 + core)


def greet(barrier, target):
    pl.semaphore_signal(
        barrier, inc=1, device_id=target, device_id_type=pl.DeviceIdType.MESH
    )


def remote(source, target_ref, send_sem, recv_sem, target):
    return pltpu.make_async_remote_copy(
        src_ref=source,
        dst_ref=target_ref,
        send_sem=send_sem,
        recv_sem=recv_sem,
        device_id=target,
        device_id_type=pl.DeviceIdType.MESH,
    )


def one_hot(wanted, columns):
    return jnp.where(
        lax.broadcasted_iota(jnp.int32, (wanted.shape[0], columns), 1) == wanted, 1.0, 0.0
    ).astype(BF16)


def row_index(count):
    return lax.broadcasted_iota(jnp.int32, (count, 1), 0)


def dot(a, b):
    return jnp.dot(a, b, preferred_element_type=F32)


def dot_t(a, b):
    return lax.dot_general(a, b, (((1,), (1,)), ((), ())), preferred_element_type=F32)


def attend_kernel(
    length_ref,
    parents_ref,
    q_ref,
    cache_ref,
    new_ref,
    ids_ref,
    gates_ref,
    out_ref,
    routed_ref,
    part,
    stat,
    got,
    got_stat,
    routes,
    part_send,
    part_recv,
    stat_send,
    stat_recv,
    route_send,
    route_recv,
):
    c, e, x, y, z, core = coordinates()
    barrier = pltpu.get_barrier_semaphore()
    for step in range(1, N_CTX):
        greet(barrier, (lax.rem(c + step, N_CTX), e))

    @pl.loop(1, N_EXP)
    def _(step):
        greet(barrier, (c, lax.rem(e + step, N_EXP)))

    lane = lax.broadcasted_iota(jnp.int32, (ROWS, 128), 1)
    dense = jnp.zeros((ROWS, 128), F32)
    for k in range(8):
        dense = jnp.where(lane == ids_ref[:, k : k + 1], gates_ref[:, k : k + 1], dense)
    spot = core * 16 + (y // 2) * 8 + z
    routes[spot] = dense

    length = length_ref[0]
    positions = cache_ref.shape[0]
    live = (
        c * positions + lax.broadcasted_iota(jnp.int32, (1, positions), 1)
    ) < length
    wide_lane = lax.broadcasted_iota(jnp.int32, (128, 128), 1)

    def partial(target, sums, stats):
        scores = dot_t(q_ref[target], cache_ref[...]) * SCALE
        scores = jnp.where(live, scores, NEGATIVE)
        top = jnp.max(scores, axis=-1, keepdims=True)
        weights = jnp.where(live, jnp.exp(scores - top), 0.0)
        total = jnp.sum(weights, axis=-1, keepdims=True)
        sums[...] = dot(weights.astype(BF16), cache_ref[:, :LAT]).astype(BF16)
        both = jnp.where(wide_lane == 0, top, jnp.where(wide_lane == 1, total, 0.0))
        stats[...] = both.T[:8]

    def copies(target):
        where = (target, e)
        return (
            remote(part.at[target], got.at[c], part_send.at[target], part_recv.at[c], where),
            remote(stat.at[target], got_stat.at[c], stat_send.at[target], stat_recv.at[c], where),
        )

    def route_copy(step):
        target = lax.rem(e + step, N_EXP)
        return remote(
            routes.at[spot],
            routes.at[spot],
            route_send.at[target],
            route_recv.at[spot],
            (c, target),
        )

    first = lax.rem(c + 1, N_CTX)
    partial(first, part.at[first], stat.at[first])
    pl.semaphore_wait(barrier, N_CTX - 1 + N_EXP - 1)
    for copy in copies(first):
        copy.start()

    @pl.loop(2, N_CTX)
    def _(step):
        target = lax.rem(c + step, N_CTX)
        partial(target, part.at[target], stat.at[target])
        for copy in copies(target):
            copy.start()

    @pl.loop(1, N_EXP)
    def _(step):
        route_copy(step).start()

    partial(c, got.at[c], got_stat.at[c])

    row = row_index(128)
    base = lax.rem(c, 4) * MINE
    wanted = jnp.where(
        row == 0,
        c * MINE,
        jnp.where(
            row == 1,
            c * MINE + 1,
            jnp.where(
                row == 2, parents_ref[base], jnp.where(row == 3, parents_ref[base + 1], -1)
            ),
        ),
    )
    keys = dot(one_hot(wanted, ROWS), new_ref[...]).astype(BF16)
    scores = dot_t(q_ref[c], keys) * SCALE
    second = jnp.where(row >= HEADS, 1, 0)
    tail_at = jnp.where(c >= 4, second + 2, -1)
    valid = (wide_lane == second) | (wide_lane == tail_at)
    scores = jnp.where(valid, scores, NEGATIVE)
    top = jnp.max(scores, axis=-1, keepdims=True)
    weights = jnp.where(valid, jnp.exp(scores - top), 0.0)
    own_total = jnp.sum(weights, axis=-1, keepdims=True)
    own_sum = dot(weights.astype(BF16), keys[:, :LAT])

    for step in range(1, N_CTX):
        source = lax.rem(c + N_CTX - step, N_CTX)
        where = (source, e)
        remote(part.at[source], got.at[source], part_send.at[source], part_recv.at[source], where).wait_recv()
        remote(stat.at[source], got_stat.at[source], stat_send.at[source], stat_recv.at[source], where).wait_recv()

    stats = got_stat[...].reshape(N_CTX * 8, 128).T
    peak = top
    for source in range(N_CTX):
        peak = jnp.maximum(peak, stats[:, 8 * source : 8 * source + 1])
    factor = jnp.exp(top - peak)
    total = own_total * factor
    summed = own_sum * factor
    for source in range(N_CTX):
        factor = jnp.exp(stats[:, 8 * source : 8 * source + 1] - peak)
        total = total + stats[:, 8 * source + 1 : 8 * source + 2] * factor
        summed = summed + got[source].astype(F32) * factor
    attended = (summed / total).astype(BF16)
    stacked = jnp.concatenate([attended[:, 128 * k : 128 * k + 128] for k in range(4)], axis=0)
    row = row_index(512)
    source = ((row >> 2) & 3) * 128 + ((row >> 1) & 1) * HEADS + (row >> 4) * 2 + (row & 1)
    out_ref[...] = dot(one_hot(source, 512), stacked).astype(BF16)

    @pl.loop(1, N_EXP)
    def _(step):
        source = lax.rem(e + step, N_EXP)
        at = lax.rem(source, 2) * 16 + lax.rem(source // 2, 2) * 8 + source // 4
        remote(
            routes.at[at], routes.at[at], route_send.at[source], route_recv.at[at], (c, source)
        ).wait_recv()

    everyone = routes[...].reshape(N_EXP * ROWS, 128)
    here = lax.broadcasted_iota(jnp.int32, (N_EXP * ROWS, 128), 1) == e
    weight = jnp.sum(jnp.where(here, everyone, 0.0), axis=-1, keepdims=True)
    routed_ref[...] = jnp.broadcast_to(weight, (N_EXP * ROWS, 128))

    for step in range(1, N_CTX):
        for copy in copies(lax.rem(c + step, N_CTX)):
            copy.wait_send()

    @pl.loop(1, N_EXP)
    def _(step):
        route_copy(step).wait_send()


def project_kernel(
    att_ref,
    wv_ref,
    wo_ref,
    residual_ref,
    gain_ref,
    state_ref,
    normed_ref,
    by_head,
    wo_cols,
    values,
    ordered,
    crossing,
    from_core,
    shares,
    got,
    squares,
    wo_sem,
    head_send,
    head_recv,
    value_send,
    value_recv,
    core_send,
    core_recv,
    share_send,
    share_recv,
    square_send,
    square_recv,
):
    c, e, x, y, z, core = coordinates()
    pair = e // 2
    other_core = (c, e + 1 - 2 * core)
    barrier = pltpu.get_barrier_semaphore()
    for step in range(1, N_CTX):
        greet(barrier, (lax.rem(c + step, N_CTX), e))

    @pl.loop(1, N_EXP)
    def _(step):
        greet(barrier, (c, lax.rem(e + step, N_EXP)))

    columns = pl.ds(pl.multiple_of(c * COLS, 128), COLS)
    fetch = pltpu.make_async_copy(wo_ref.at[:, columns], wo_cols, wo_sem)
    fetch.start()
    by_head[e] = att_ref[e]

    def head_copy(step):
        target = lax.rem(e + step, N_EXP)
        return remote(
            att_ref.at[target], by_head.at[e], head_send.at[target], head_recv.at[e], (c, target)
        )

    pl.semaphore_wait(barrier, N_CTX - 1 + N_EXP - 1)

    @pl.loop(1, N_EXP)
    def _(step):
        head_copy(step).start()

    @pl.loop(1, N_EXP)
    def _(step):
        source = lax.rem(e + step, N_EXP)
        remote(
            att_ref.at[source], by_head.at[source], head_send.at[source], head_recv.at[source], (c, source)
        ).wait_recv()

    row = row_index(512)
    source = (
        ((row >> 1) & 31) * 16 + ((row >> 6) & 3) * 4 + (row & 1) * 2 + (row >> 8)
    )
    latents = dot(one_hot(source, 512), by_head[...].reshape(512, 128)).astype(BF16)
    halves = []
    for parity in range(2):
        total = jnp.zeros((64, 128), F32)
        for quarter in range(4):
            at = (parity * 4 + quarter) * 64
            total = total + dot(
                latents[at : at + 64], wv_ref[parity, 128 * quarter : 128 * quarter + 128, :]
            )
        halves.append(total.astype(BF16))
    values[c] = jnp.concatenate(halves, axis=1)

    def value_copy(target):
        return remote(
            values.at[c], values.at[c], value_send.at[target], value_recv.at[c], (target, e)
        )

    for step in range(1, N_CTX):
        value_copy(lax.rem(c + step, N_CTX)).start()
    for step in range(1, N_CTX):
        source = lax.rem(c + N_CTX - step, N_CTX)
        remote(
            values.at[source], values.at[source], value_send.at[source], value_recv.at[source], (source, e)
        ).wait_recv()
    source = (
        ((row >> 1) & 7) * 64 + ((row >> 4) & 15) * 4 + (row >> 8) * 2 + (row & 1)
    )
    ordered[...] = (
        dot(one_hot(source, 512), values[...].reshape(512, 256)).astype(BF16).reshape(2, 256, 256)
    )
    fetch.wait()
    crossing[...] = dot(ordered[1 - core], wo_cols[...]).astype(BF16).reshape(16, ROWS, COLS)
    across = remote(crossing, from_core, core_send, core_recv, other_core)
    across.start()
    own = dot(ordered[core], wo_cols[...])
    across.wait_recv()
    shares[...] = (
        (own + from_core[...].reshape(256, COLS).astype(F32)).astype(BF16).reshape(16, ROWS, COLS)
    )

    def share_copy(step):
        target = lax.rem(pair + step, 16)
        return remote(
            shares.at[target],
            got.at[pair],
            share_send.at[target],
            share_recv.at[pair],
            (c, target * 2 + core),
        )

    @pl.loop(1, 16)
    def _(step):
        share_copy(step).start()

    got[pair] = shares[pair]

    @pl.loop(1, 16)
    def _(step):
        source = lax.rem(pair + step, 16)
        remote(
            shares.at[source],
            got.at[source],
            share_send.at[source],
            share_recv.at[source],
            (c, source * 2 + core),
        ).wait_recv()

    state = residual_ref[:, columns].astype(F32)
    state = state + jnp.sum(got[...].astype(F32), axis=0)
    state_ref[...] = state
    square = jnp.sum(state * state, axis=-1, keepdims=True)
    squares[c] = jnp.broadcast_to(square, (ROWS, 128))

    def square_copy(target):
        return remote(
            squares.at[c], squares.at[c], square_send.at[target], square_recv.at[c], (target, e)
        )

    for step in range(1, N_CTX):
        square_copy(lax.rem(c + step, N_CTX)).start()
    for step in range(1, N_CTX):
        source = lax.rem(c + N_CTX - step, N_CTX)
        remote(
            squares.at[source], squares.at[source], square_send.at[source], square_recv.at[source], (source, e)
        ).wait_recv()
    mean = jnp.sum(squares[...], axis=0)[:, :1] * (1.0 / (N_CTX * COLS))
    normed_ref[...] = (state * lax.rsqrt(mean + 1e-06) * gain_ref[pl.ds(c, 1), :]).astype(BF16)

    across.wait_send()
    for step in range(1, N_CTX):
        value_copy(lax.rem(c + step, N_CTX)).wait_send()
        square_copy(lax.rem(c + step, N_CTX)).wait_send()

    @pl.loop(1, N_EXP)
    def _(step):
        head_copy(step).wait_send()

    @pl.loop(1, 16)
    def _(step):
        share_copy(step).wait_send()


def expert_kernel(
    normed_ref,
    state_ref,
    routed_ref,
    gate_ref,
    up_ref,
    down_ref,
    out_ref,
    rows,
    sums,
    from_core,
    half_one,
    whole_one,
    half_two,
    whole_two,
    last,
    hidden,
    both,
    down,
    weight_sems,
    z_send,
    z_recv,
    two_send,
    two_recv,
    relay_two_send,
    relay_two_recv,
    three_send,
    three_recv,
    relay_three_send,
    relay_three_recv,
    share_send,
    share_recv,
    cross_send,
    cross_recv,
    half_one_send,
    half_one_recv,
    whole_one_send,
    whole_one_recv,
    half_two_send,
    half_two_recv,
    whole_two_send,
    whole_two_recv,
    last_send,
    last_recv,
):
    c, e, x, y, z, core = coordinates()
    y_hi = y // 2

    def plus(a, k):
        return lax.rem(a + k, 4)

    neighbours = {
        ("x", 0): device(plus(x, 1), y, z, core),
        ("x", 1): device(plus(x, 3), y, z, core),
        ("y", 0): device(x, plus(y, 1), z, core),
        ("y", 1): device(x, plus(y, 3), z, core),
    }
    other_core = device(x, y, z, 1 - core)
    wide_axis, narrow_axis = ("x", "y"), ("y", "x")
    wide_at, narrow_at = (x, y), (y, x)

    barrier = pltpu.get_barrier_semaphore()
    for target in neighbours.values():
        greet(barrier, target)
    greet(barrier, other_core)
    for step in range(1, 8):
        greet(barrier, device(x, y, lax.rem(z + step, 8), core))

    fetches = [
        pltpu.make_async_copy(gate_ref, both.at[:, :, pl.ds(0, 128)], weight_sems.at[0]),
        pltpu.make_async_copy(up_ref, both.at[:, :, pl.ds(128, 128)], weight_sems.at[1]),
        pltpu.make_async_copy(down_ref, down, weight_sems.at[2]),
    ]
    for fetch in fetches:
        fetch.start()
    rows[c, core, y_hi, z] = normed_ref[...]
    pl.semaphore_wait(barrier, 12)

    sent = []

    def send(source, target_ref, send_sem, recv_sem, target):
        copy = remote(source, target_ref, send_sem, recv_sem, target)
        copy.start()
        sent.append(copy)

    def arrive(ref, send_sem, recv_sem, target):
        remote(ref, ref, send_sem, recv_sem, target).wait_recv()

    def chunk(ref, part, wide, narrow, start=0, count=4):
        at_x, at_y = (wide, narrow) if part == 0 else (narrow, wide)
        return ref.at[
            lax.rem(at_y, 2) * 4 + at_x, core, at_y // 2, pl.ds(part * 4 + start, count)
        ]

    for step in range(1, 8):
        to = lax.rem(z + step, 8)
        block = rows.at[c, core, y_hi, z]
        send(block, block, z_send.at[to], z_recv.at[z], device(x, y, to, core))
    for step in range(1, 8):
        source = lax.rem(z + step, 8)
        arrive(
            rows.at[c, core, y_hi, source],
            z_send.at[source],
            z_recv.at[source],
            device(x, y, source, core),
        )

    def share(part, wide, narrow):
        block = chunk(rows, part, wide, narrow)
        sem = (part, wide, narrow)
        send(block, block, share_send.at[sem], share_recv.at[sem], other_core)

    def spread(part, narrow):
        block = chunk(rows, part, wide_at[part], narrow)
        for side in range(2):
            sem = (part, side, narrow)
            send(
                block,
                block,
                three_send.at[sem],
                three_recv.at[sem],
                neighbours[wide_axis[part], side],
            )
        share(part, wide_at[part], narrow)

    for part in range(2):
        block = chunk(rows, part, wide_at[part], narrow_at[part])
        for side in range(2):
            send(
                block,
                block,
                two_send.at[part, side],
                two_recv.at[part, side],
                neighbours[narrow_axis[part], side],
            )
    for part in range(2):
        spread(part, narrow_at[part])
    for part in range(2):
        for side in range(2):
            near = plus(narrow_at[part], 3 if side == 0 else 1)
            target = neighbours[narrow_axis[part], side]
            arrive(
                chunk(rows, part, wide_at[part], near),
                two_send.at[part, side],
                two_recv.at[part, side],
                target,
            )
            block = chunk(rows, part, wide_at[part], near, 2 * side, 2)
            send(
                block,
                block,
                relay_two_send.at[part, side],
                relay_two_recv.at[part, side],
                target,
            )
            spread(part, near)
    for part in range(2):
        far = plus(narrow_at[part], 2)
        for side in range(2):
            arrive(
                chunk(rows, part, wide_at[part], far, 2 * side, 2),
                relay_two_send.at[part, side],
                relay_two_recv.at[part, side],
                neighbours[narrow_axis[part], side],
            )
        spread(part, far)
    for step in range(4):
        for part in range(2):
            narrow = plus(narrow_at[part], (0, 1, 3, 2)[step])
            for side in range(2):
                near = plus(wide_at[part], 3 if side == 0 else 1)
                target = neighbours[wide_axis[part], side]
                sem = (part, side, narrow)
                arrive(
                    chunk(rows, part, near, narrow), three_send.at[sem], three_recv.at[sem], target
                )
                share(part, near, narrow)

                @pl.when((narrow >= 2) == (side == 1))
                def _():
                    block = chunk(rows, part, near, narrow)
                    remote(
                        block,
                        block,
                        relay_three_send.at[part, narrow],
                        relay_three_recv.at[part, narrow],
                        target,
                    ).start()

    for part in range(2):
        for narrow in range(4):
            side = narrow // 2
            far = plus(wide_at[part], 2)
            arrive(
                chunk(rows, part, far, narrow),
                relay_three_send.at[part, narrow],
                relay_three_recv.at[part, narrow],
                neighbours[wide_axis[part], side],
            )
            share(part, far, narrow)
    for part in range(2):
        for wide in range(4):
            for narrow in range(4):
                at_x, at_y = (wide, narrow) if part == 0 else (narrow, wide)
                sem = (part, wide, narrow)
                block = rows.at[
                    (at_y % 2) * 4 + at_x, 1 - core, at_y // 2, pl.ds(part * 4, 4)
                ]
                arrive(block, share_send.at[sem], share_recv.at[sem], other_core)

    for fetch in fetches:
        fetch.wait()
    total = jnp.zeros((512, 256), F32)
    for k in range(N_CTX):
        total = total + dot(rows[k].reshape(512, COLS), both[k])
    gate, up = total[:, :128], total[:, 128:]
    silu = gate / (1.0 + jnp.exp(-gate))
    hidden[...] = (silu * up * routed_ref[...]).astype(BF16).reshape(2, 256, 128)

    for k in range(N_CTX):
        at = pl.ds(k * COLS, COLS)
        sums[k, 1 - core] = (
            dot(hidden[1 - core], down[:, at]).astype(BF16).reshape(2, 8, ROWS, COLS)
        )
        send(
            sums.at[k, 1 - core], from_core.at[k], cross_send.at[k], cross_recv.at[k], other_core
        )
    for k in range(N_CTX):
        at = pl.ds(k * COLS, COLS)
        own = dot(hidden[core], down[:, at])
        arrive(from_core.at[k], cross_send.at[k], cross_recv.at[k], other_core)
        sums[k, core] = (
            (own + from_core[k].reshape(256, COLS).astype(F32))
            .astype(BF16)
            .reshape(2, 8, ROWS, COLS)
        )

    def add(ref, *others):
        value = ref[...].astype(F32)
        for other in others:
            value = value + other[...].astype(F32)
        ref[...] = value.astype(BF16)

    def wide_send(part, side, narrow):
        near = plus(wide_at[part], 1 if side == 0 else 3)
        sem = (part, side, narrow)
        send(
            chunk(sums, part, near, narrow),
            whole_one.at[sem],
            whole_one_send.at[sem],
            whole_one_recv.at[sem],
            neighbours[wide_axis[part], side],
        )

    for part in range(2):
        far = plus(wide_at[part], 2)
        for side in range(2):
            for k in range(2):
                sem = (part, side, k)
                send(
                    chunk(sums, part, far, 2 * side + k),
                    half_one.at[sem],
                    half_one_send.at[sem],
                    half_one_recv.at[sem],
                    neighbours[wide_axis[part], side],
                )
    for part in range(2):
        for side in range(2):
            for k in range(2):
                wide_send(part, side, 2 * (1 - side) + k)
    for part in range(2):
        for side in range(2):
            near = plus(wide_at[part], 1 if side == 0 else 3)
            for k in range(2):
                sem = (part, side, k)
                arrive(
                    half_one.at[sem],
                    half_one_send.at[sem],
                    half_one_recv.at[sem],
                    neighbours[wide_axis[part], side],
                )
                add(chunk(sums, part, near, 2 * side + k), half_one.at[sem])
                wide_send(part, side, 2 * side + k)

    def narrow_send(part, side):
        near = plus(narrow_at[part], 1 if side == 0 else 3)
        sem = (part, side)
        send(
            chunk(sums, part, wide_at[part], near),
            whole_two.at[sem],
            whole_two_send.at[sem],
            whole_two_recv.at[sem],
            neighbours[narrow_axis[part], side],
        )

    for step in (2, 1, 3, 0):
        for part in range(2):
            narrow = plus(narrow_at[part], step)
            for side in range(2):
                sem = (part, side, narrow)
                arrive(
                    whole_one.at[sem],
                    whole_one_send.at[sem],
                    whole_one_recv.at[sem],
                    neighbours[wide_axis[part], side],
                )
            add(
                chunk(sums, part, wide_at[part], narrow),
                whole_one.at[part, 0, narrow],
                whole_one.at[part, 1, narrow],
            )
            if step == 2:
                for side in range(2):
                    sem = (part, side)
                    send(
                        chunk(sums, part, wide_at[part], narrow, 2 * side, 2),
                        half_two.at[sem],
                        half_two_send.at[sem],
                        half_two_recv.at[sem],
                        neighbours[narrow_axis[part], side],
                    )
    for part in range(2):
        for side in range(2):
            near = plus(narrow_at[part], 1 if side == 0 else 3)
            sem = (part, side)
            arrive(
                half_two.at[sem],
                half_two_send.at[sem],
                half_two_recv.at[sem],
                neighbours[narrow_axis[part], side],
            )
            add(chunk(sums, part, wide_at[part], near, 2 * side, 2), half_two.at[sem])
            narrow_send(part, side)
    for part in range(2):
        for side in range(2):
            sem = (part, side)
            arrive(
                whole_two.at[sem],
                whole_two_send.at[sem],
                whole_two_recv.at[sem],
                neighbours[narrow_axis[part], side],
            )
        add(
            chunk(sums, part, wide_at[part], narrow_at[part]),
            whole_two.at[part, 0],
            whole_two.at[part, 1],
        )
    for step in range(1, 8):
        to = lax.rem(z + step, 8)
        send(
            sums.at[c, core, y_hi, to],
            last.at[z],
            last_send.at[to],
            last_recv.at[z],
            device(x, y, to, core),
        )
    last[z] = sums[c, core, y_hi, z]
    for step in range(1, 8):
        source = lax.rem(z + step, 8)
        arrive(
            last.at[source],
            last_send.at[source],
            last_recv.at[source],
            device(x, y, source, core),
        )
    result = state_ref[...]
    for k in range(8):
        result = result + last[k].astype(F32)
    out_ref[...] = result.astype(BF16)

    for copy in sent:
        copy.wait_send()
    for part in range(2):
        for narrow in range(4):
            block = chunk(rows, part, wide_at[part], narrow)
            remote(
                block,
                block,
                relay_three_send.at[part, narrow],
                relay_three_recv.at[part, narrow],
                neighbours[wide_axis[part], narrow // 2],
            ).wait_send()


VMEM = pl.BlockSpec(memory_space=pltpu.VMEM)
SMEM = pl.BlockSpec(memory_space=pltpu.SMEM)
ANY = pl.BlockSpec(memory_space=pl.ANY)
DMA = pltpu.SemaphoreType.DMA


def params(number):
    return pltpu.CompilerParams(
        collective_id=number, has_side_effects=True, vmem_limit_bytes=VMEM_LIMIT
    )


def per_device(
    queries,
    prompt_cache,
    new_latent,
    parents,
    lengths,
    value_weight,
    output_weight,
    residual,
    norm_gain,
    expert_ids,
    expert_weights,
    expert_gate,
    expert_up,
    expert_down,
):
    key_width = queries.shape[3]
    attended, routed = pl.pallas_call(
        attend_kernel,
        out_shape=(
            jax.ShapeDtypeStruct((512, 128), BF16),
            jax.ShapeDtypeStruct((N_EXP * ROWS, 128), F32),
        ),
        in_specs=[SMEM, SMEM] + [VMEM] * 5,
        out_specs=(VMEM, VMEM),
        scratch_shapes=[
            pltpu.VMEM((N_CTX, 128, LAT), BF16),
            pltpu.VMEM((N_CTX, 8, 128), F32),
            pltpu.VMEM((N_CTX, 128, LAT), BF16),
            pltpu.VMEM((N_CTX, 8, 128), F32),
            pltpu.VMEM((N_EXP, ROWS, 128), F32),
            DMA((N_CTX,)),
            DMA((N_CTX,)),
            DMA((N_CTX,)),
            DMA((N_CTX,)),
            DMA((N_EXP,)),
            DMA((N_EXP,)),
        ],
        compiler_params=params(0),
        name="attend",
    )(
        lengths,
        parents.reshape(8),
        queries.reshape(N_CTX, 128, key_width),
        prompt_cache[0],
        new_latent.reshape(ROWS, key_width),
        expert_ids.reshape(ROWS, 8),
        expert_weights.reshape(ROWS, 8),
    )
    state, normed = pl.pallas_call(
        project_kernel,
        out_shape=(
            jax.ShapeDtypeStruct((ROWS, COLS), F32),
            jax.ShapeDtypeStruct((ROWS, COLS), BF16),
        ),
        in_specs=[VMEM, VMEM, ANY, VMEM, VMEM],
        out_specs=(VMEM, VMEM),
        scratch_shapes=[
            pltpu.VMEM((N_EXP, ROWS, 128), BF16),
            pltpu.VMEM((256, COLS), BF16),
            pltpu.VMEM((N_CTX, 64, 256), BF16),
            pltpu.VMEM((2, 256, 256), BF16),
            pltpu.VMEM((16, ROWS, COLS), BF16),
            pltpu.VMEM((16, ROWS, COLS), BF16),
            pltpu.VMEM((16, ROWS, COLS), BF16),
            pltpu.VMEM((16, ROWS, COLS), BF16),
            pltpu.VMEM((N_CTX, ROWS, 128), F32),
            DMA,
            DMA((N_EXP,)),
            DMA((N_EXP,)),
            DMA((N_CTX,)),
            DMA((N_CTX,)),
            DMA,
            DMA,
            DMA((16,)),
            DMA((16,)),
            DMA((N_CTX,)),
            DMA((N_CTX,)),
        ],
        compiler_params=params(1),
        name="project",
    )(
        attended.reshape(N_EXP, ROWS, 128),
        value_weight,
        output_weight,
        residual.reshape(ROWS, N_CTX * COLS),
        norm_gain.reshape(N_CTX, COLS),
    )
    out = pl.pallas_call(
        expert_kernel,
        out_shape=jax.ShapeDtypeStruct((ROWS, COLS), BF16),
        in_specs=[VMEM, VMEM, VMEM, ANY, ANY, ANY],
        out_specs=VMEM,
        scratch_shapes=[
            pltpu.VMEM((N_CTX, 2, 2, 8, ROWS, COLS), BF16),
            pltpu.VMEM((N_CTX, 2, 2, 8, ROWS, COLS), BF16),
            pltpu.VMEM((N_CTX, 2, 8, ROWS, COLS), BF16),
            pltpu.VMEM((2, 2, 2, 4, ROWS, COLS), BF16),
            pltpu.VMEM((2, 2, 4, 4, ROWS, COLS), BF16),
            pltpu.VMEM((2, 2, 2, ROWS, COLS), BF16),
            pltpu.VMEM((2, 2, 4, ROWS, COLS), BF16),
            pltpu.VMEM((8, ROWS, COLS), BF16),
            pltpu.VMEM((2, 256, 128), BF16),
            pltpu.VMEM((N_CTX, COLS, 256), BF16),
            pltpu.VMEM((128, N_CTX * COLS), BF16),
            DMA((3,)),
            DMA((8,)),
            DMA((8,)),
            DMA((2, 2)),
            DMA((2, 2)),
            DMA((2, 2)),
            DMA((2, 2)),
            DMA((2, 2, 4)),
            DMA((2, 2, 4)),
            DMA((2, 4)),
            DMA((2, 4)),
            DMA((2, 4, 4)),
            DMA((2, 4, 4)),
            DMA((8,)),
            DMA((8,)),
            DMA((2, 2, 2)),
            DMA((2, 2, 2)),
            DMA((2, 2, 4)),
            DMA((2, 2, 4)),
            DMA((2, 2)),
            DMA((2, 2)),
            DMA((2, 2)),
            DMA((2, 2)),
            DMA((8,)),
            DMA((8,)),
        ],
        compiler_params=params(2),
        name="experts",
    )(
        normed,
        state,
        routed,
        expert_gate.reshape(N_CTX, COLS, 128),
        expert_up.reshape(N_CTX, COLS, 128),
        expert_down[0],
    )
    return out.reshape(2, 8, COLS)


def solution(mesh):
    in_specs = (
        P(None, "exp", None, None),
        P("exp", "ctx", None),
        P(None, "exp", None),
        P("exp", None),
        P("exp"),
        P("exp", None, None),
        P("exp", None),
        P(None, "exp", None),
        P(),
        P(None, "exp", None),
        P(None, "exp", None),
        P("exp", None, "ctx"),
        P("exp", None, "ctx"),
        P("exp", "ctx", None),
    )
    out_specs = P(None, "exp", "ctx")
    return jax.shard_map(
        per_device, mesh=mesh, in_specs=in_specs, out_specs=out_specs, check_vma=False
    )
```

```python
import functools

import jax
import jax.numpy as jnp
from jax import lax
from jax.experimental import pallas as pl
from jax.experimental.pallas import tpu as pltpu
from jax.sharding import PartitionSpec as P

SCALE = 0.07216878364870322
NEGATIVE = -1e30
BF16 = jnp.bfloat16
F32 = jnp.float32
N_CTX = 8
N_EXP = 32
ROWS = 16
MINE = 2
HEADS = 64
LAT = 512
COLS = 896
VMEM_LIMIT = 56 * 1024 * 1024


def coordinates():
    c, e = lax.axis_index("ctx"), lax.axis_index("exp")
    x, y_lo = lax.rem(c, 4), c // 4
    z, y_hi, core = e // 4, lax.rem(e // 2, 2), lax.rem(e, 2)
    return c, e, x, y_hi * 2 + y_lo, z, core


def device(x, y, z, core):
    return (lax.rem(y, 2) * 4 + x, z * 4 + (y // 2) * 2 + core)


def greet(barrier, target):
    pl.semaphore_signal(
        barrier, inc=1, device_id=target, device_id_type=pl.DeviceIdType.MESH
    )


def remote(source, target_ref, send_sem, recv_sem, target):
    return pltpu.make_async_remote_copy(
        src_ref=source,
        dst_ref=target_ref,
        send_sem=send_sem,
        recv_sem=recv_sem,
        device_id=target,
        device_id_type=pl.DeviceIdType.MESH,
    )


def one_hot(wanted, columns):
    return jnp.where(
        lax.broadcasted_iota(jnp.int32, (wanted.shape[0], columns), 1) == wanted, 1.0, 0.0
    ).astype(BF16)


def row_index(count):
    return lax.broadcasted_iota(jnp.int32, (count, 1), 0)


def dot(a, b):
    return jnp.dot(a, b, preferred_element_type=F32)


def dot_t(a, b):
    return lax.dot_general(a, b, (((1,), (1,)), ((), ())), preferred_element_type=F32)


def layer_kernel(
    length_ref,
    parents_ref,
    q_ref,
    cache_ref,
    new_ref,
    ids_ref,
    gates_ref,
    wv_ref,
    wo_ref,
    residual_ref,
    gain_ref,
    gate_ref,
    up_ref,
    down_ref,
    out_ref,
    part,
    stat,
    got,
    got_stat,
    orders,
    heads,
    by_head,
    wo_cols,
    values,
    ordered,
    crossing,
    crossed,
    shares,
    from_y,
    from_z,
    squares,
    state,
    notes,
    noted,
    rows,
    sums,
    from_core,
    half_one,
    whole_one,
    half_two,
    whole_two,
    last,
    hidden,
    both,
    down,
    weight_sems,
    part_send,
    part_recv,
    stat_send,
    stat_recv,
    head_send,
    head_recv,
    value_send,
    value_recv,
    crossing_send,
    crossing_recv,
    y_send,
    y_recv,
    zsum_send,
    zsum_recv,
    square_send,
    square_recv,
    note_send,
    note_recv,
    z_send,
    z_recv,
    two_send,
    two_recv,
    relay_two_send,
    relay_two_recv,
    three_send,
    three_recv,
    relay_three_send,
    relay_three_recv,
    share_send,
    share_recv,
    cross_send,
    cross_recv,
    half_one_send,
    half_one_recv,
    whole_one_send,
    whole_one_recv,
    half_two_send,
    half_two_recv,
    whole_two_send,
    whole_two_recv,
    last_send,
    last_recv,
):
    c, e, x, y, z, core = coordinates()
    y_hi, y_lo = y // 2, lax.rem(y, 2)

    def plus(a, k):
        return lax.rem(a + k, 4)

    neighbours = {
        ("x", 0): device(plus(x, 1), y, z, core),
        ("x", 1): device(plus(x, 3), y, z, core),
        ("y", 0): device(x, plus(y, 1), z, core),
        ("y", 1): device(x, plus(y, 3), z, core),
    }
    other_core = device(x, y, z, 1 - core)
    wide_axis, narrow_axis = ("x", "y"), ("y", "x")
    wide_at, narrow_at = (x, y), (y, x)

    barrier = pltpu.get_barrier_semaphore()
    for step in range(1, N_CTX):
        greet(barrier, (lax.rem(c + step, N_CTX), e))

    @pl.loop(1, N_EXP)
    def _(step):
        greet(barrier, (c, lax.rem(e + step, N_EXP)))

    greet(barrier, device(x, 3 - y, z, core))

    columns = pl.ds(pl.multiple_of(c * COLS, 128), COLS)
    fetches = [
        pltpu.make_async_copy(wo_ref.at[:, columns], wo_cols, weight_sems.at[0]),
        pltpu.make_async_copy(gate_ref, both.at[:, :, pl.ds(0, 128)], weight_sems.at[1]),
        pltpu.make_async_copy(up_ref, both.at[:, :, pl.ds(128, 128)], weight_sems.at[2]),
        pltpu.make_async_copy(down_ref, down, weight_sems.at[3]),
    ]
    for fetch in fetches:
        fetch.start()

    sent = []

    def send(source, target_ref, send_sem, recv_sem, target):
        copy = remote(source, target_ref, send_sem, recv_sem, target)
        copy.start()
        sent.append(copy)

    def arrive(ref, send_sem, recv_sem, target):
        remote(ref, ref, send_sem, recv_sem, target).wait_recv()

    length = length_ref[0]
    positions = cache_ref.shape[1]
    live = (
        c * positions + lax.broadcasted_iota(jnp.int32, (1, positions), 1)
    ) < length
    wide_lane = lax.broadcasted_iota(jnp.int32, (128, 128), 1)

    def partial(target, sums_ref, stats_ref):
        scores = dot(q_ref[target], cache_ref[...]) * SCALE
        scores = jnp.where(live, scores, NEGATIVE)
        top = jnp.max(scores, axis=-1, keepdims=True)
        weights = jnp.where(live, jnp.exp(scores - top), 0.0)
        total = jnp.sum(weights, axis=-1, keepdims=True)
        sums_ref[...] = dot_t(weights.astype(BF16), cache_ref[:LAT, :]).astype(BF16)
        stats_ref[...] = jnp.where(
            wide_lane == 0, top, jnp.where(wide_lane == 1, total, 0.0)
        ).T[:8]

    def peer(flip, step):
        return lax.rem(y_lo + flip, 2) * 4 + plus(x, step)

    def send_partial(target):
        where = (target, e)
        send(part.at[target], got.at[c], part_send.at[target], part_recv.at[c], where)
        send(stat.at[target], got_stat.at[c], stat_send.at[target], stat_recv.at[c], where)

    peers = [peer(*k) for k in ((1, 2), (0, 2), (1, 1), (0, 1), (1, 3), (0, 3), (1, 0))]
    partial(peers[0], part.at[peers[0]], stat.at[peers[0]])
    pl.semaphore_wait(barrier, N_CTX - 1 + N_EXP - 1 + 1)
    send_partial(peers[0])
    for target in peers[1:]:
        partial(target, part.at[target], stat.at[target])
        send_partial(target)
    partial(c, got.at[c], got_stat.at[c])

    row = row_index(512)
    orders[0] = one_hot(
        ((row >> 2) & 3) * 128 + ((row >> 1) & 1) * HEADS + (row >> 4) * 2 + (row & 1), 512
    )
    orders[1] = one_hot(
        ((row >> 1) & 31) * 16 + ((row >> 6) & 3) * 4 + (row & 1) * 2 + (row >> 8), 512
    )
    orders[2] = one_hot(
        ((row >> 1) & 7) * 64
        + ((row >> 4) & 7) * 8
        + ((row >> 7) & 1) * 4
        + (row >> 8) * 2
        + (row & 1),
        512,
    )

    row = row_index(128)
    base = lax.rem(c, 4) * MINE
    wanted = jnp.where(
        row == 0,
        c * MINE,
        jnp.where(
            row == 1,
            c * MINE + 1,
            jnp.where(
                row == 2, parents_ref[base], jnp.where(row == 3, parents_ref[base + 1], -1)
            ),
        ),
    )
    keys = dot(one_hot(wanted, ROWS), new_ref[...]).astype(BF16)
    scores = dot_t(q_ref[c], keys) * SCALE
    second = jnp.where(row >= HEADS, 1, 0)
    tail_at = jnp.where(c >= 4, second + 2, -1)
    valid = (wide_lane == second) | (wide_lane == tail_at)
    scores = jnp.where(valid, scores, NEGATIVE)
    top = jnp.max(scores, axis=-1, keepdims=True)
    weights = jnp.where(valid, jnp.exp(scores - top), 0.0)
    own_total = jnp.sum(weights, axis=-1, keepdims=True)
    own_sum = dot(weights.astype(BF16), keys[:, :LAT])

    lane = lax.broadcasted_iota(jnp.int32, (ROWS, 128), 1)
    dense = jnp.zeros((ROWS, 128), F32)
    for k in range(8):
        dense = jnp.where(lane == ids_ref[:, k : k + 1], gates_ref[:, k : k + 1], dense)

    for source in peers:
        where = (source, e)
        arrive(got_stat.at[source], stat_send.at[source], stat_recv.at[source], where)
    stats = got_stat[...].reshape(N_CTX * 8, 128).T
    peak = top
    for source in range(N_CTX):
        peak = jnp.maximum(peak, stats[:, 8 * source : 8 * source + 1])
    factor = jnp.exp(top - peak)
    total = own_total * factor
    summed = own_sum * factor
    for source in range(N_CTX):
        factor = jnp.exp(stats[:, 8 * source : 8 * source + 1] - peak)
        total = total + stats[:, 8 * source + 1 : 8 * source + 2] * factor
    for source in peers:
        arrive(got.at[source], part_send.at[source], part_recv.at[source], (source, e))
    for source in range(N_CTX):
        factor = jnp.exp(stats[:, 8 * source : 8 * source + 1] - peak)
        summed = summed + got[source].astype(F32) * factor
    attended = (summed / total).astype(BF16)
    stacked = jnp.concatenate([attended[:, 128 * k : 128 * k + 128] for k in range(4)], axis=0)
    heads[...] = dot(orders[0], stacked).astype(BF16).reshape(N_EXP, ROWS, 128)

    def head_copy(step):
        target = lax.rem(e + step, N_EXP)
        return remote(
            heads.at[target], by_head.at[e], head_send.at[target], head_recv.at[e], (c, target)
        )

    @pl.loop(1, N_EXP)
    def _(step):
        head_copy(step).start()

    by_head[e] = heads[e]

    @pl.loop(1, N_EXP)
    def _(step):
        source = lax.rem(e + step, N_EXP)
        remote(
            heads.at[source],
            by_head.at[source],
            head_send.at[source],
            head_recv.at[source],
            (c, source),
        ).wait_recv()

    latents = dot(orders[1], by_head[...].reshape(512, 128)).astype(BF16)
    halves = []
    for parity in range(2):
        value = jnp.zeros((64, 128), F32)
        for quarter in range(4):
            at = (parity * 4 + quarter) * 64
            value = value + dot(
                latents[at : at + 64], wv_ref[parity, 128 * quarter : 128 * quarter + 128, :]
            )
        halves.append(value.astype(BF16))
    values[c] = jnp.concatenate(halves, axis=1)

    for target in peers:
        send(values.at[c], values.at[c], value_send.at[target], value_recv.at[c], (target, e))
    for source in peers:
        arrive(values.at[source], value_send.at[source], value_recv.at[source], (source, e))
    ordered[...] = dot(orders[2], values[...].reshape(512, 256)).astype(BF16).reshape(2, 256, 256)
    fetches[0].wait()
    crossing[...] = dot(ordered[1 - core], wo_cols[...]).astype(BF16).reshape(2, 8, ROWS, COLS)
    for half in (1, 0):
        at = lax.rem(y_hi + half, 2)
        send(
            crossing.at[at],
            crossed.at[at],
            crossing_send.at[at],
            crossing_recv.at[at],
            other_core,
        )
    other_y = device(x, plus(y, 2), z, core)
    for half in (1, 0):
        at = lax.rem(y_hi + half, 2)
        own = dot(ordered[core, pl.ds(pl.multiple_of(at * 128, 128), 128)], wo_cols[...])
        arrive(crossed.at[at], crossing_send.at[at], crossing_recv.at[at], other_core)
        own = own + crossed[at].reshape(128, COLS).astype(F32)
        shares[at] = own.astype(BF16).reshape(8, ROWS, COLS)
        if half:
            for step in (4, 3, 5, 2, 6, 1, 7, 0):
                to = lax.rem(z + step, 8)
                send(shares.at[at, to], from_y.at[to], y_send.at[to], y_recv.at[to], other_y)
    for step in (4, 3, 5, 2, 6, 1, 7, 0):
        to = lax.rem(z + step, 8)
        arrive(from_y.at[to], y_send.at[to], y_recv.at[to], other_y)
        both_y = shares[y_hi, to].astype(F32) + from_y[to].astype(F32)
        if step:
            shares[y_hi, to] = both_y.astype(BF16)
            send(
                shares.at[y_hi, to],
                from_z.at[z],
                zsum_send.at[to],
                zsum_recv.at[z],
                device(x, y, to, core),
            )
    value = residual_ref[:, columns].astype(F32) + both_y
    for step in range(1, 8):
        source = lax.rem(z + step, 8)
        arrive(
            from_z.at[source],
            zsum_send.at[source],
            zsum_recv.at[source],
            device(x, y, source, core),
        )
        value = value + from_z[source].astype(F32)
    state[...] = value
    rows[c, core, y_hi, z] = (value * gain_ref[pl.ds(c, 1), :]).astype(BF16)
    squares[c] = jnp.broadcast_to(jnp.sum(value * value, axis=-1, keepdims=True), (ROWS, 128))
    for target in peers:
        send(squares.at[c], squares.at[c], square_send.at[target], square_recv.at[c], (target, e))

    def note_copy(step):
        target = lax.rem(e + step, N_EXP)
        spot = core * 16 + y_hi * 8 + z
        return remote(
            notes.at[target], noted.at[spot], note_send.at[target], note_recv.at[spot], (c, target)
        )

    def send_notes():
        for source in peers:
            arrive(squares.at[source], square_send.at[source], square_recv.at[source], (source, e))
        mean = jnp.sum(squares[...], axis=0) * (1.0 / (N_CTX * COLS))
        scale = lax.rsqrt(mean + 1e-06)
        block = jnp.concatenate([dense, scale, jnp.zeros((96, 128), F32)], axis=0).T
        notes[...] = block[:N_EXP].reshape(N_EXP, 1, 128)
        noted[core * 16 + y_hi * 8 + z] = notes[e]

        @pl.loop(1, N_EXP)
        def _(step):
            note_copy(step).start()

    def chunk(ref, part, wide, narrow, start=0, count=4):
        at_x, at_y = (wide, narrow) if part == 0 else (narrow, wide)
        return ref.at[
            lax.rem(at_y, 2) * 4 + at_x, core, at_y // 2, pl.ds(part * 4 + start, count)
        ]

    for step in range(1, 8):
        to = lax.rem(z + step, 8)
        block = rows.at[c, core, y_hi, z]
        send(block, block, z_send.at[to], z_recv.at[z], device(x, y, to, core))
    for step in range(1, 8):
        source = lax.rem(z + step, 8)
        arrive(
            rows.at[c, core, y_hi, source],
            z_send.at[source],
            z_recv.at[source],
            device(x, y, source, core),
        )

    def share(part, wide, narrow):
        block = chunk(rows, part, wide, narrow)
        sem = (part, wide, narrow)
        send(block, block, share_send.at[sem], share_recv.at[sem], other_core)

    def spread(part, narrow):
        block = chunk(rows, part, wide_at[part], narrow)
        for side in range(2):
            sem = (part, side, narrow)
            send(
                block,
                block,
                three_send.at[sem],
                three_recv.at[sem],
                neighbours[wide_axis[part], side],
            )
        share(part, wide_at[part], narrow)

    for part in range(2):
        block = chunk(rows, part, wide_at[part], narrow_at[part])
        for side in range(2):
            send(
                block,
                block,
                two_send.at[part, side],
                two_recv.at[part, side],
                neighbours[narrow_axis[part], side],
            )
    for part in range(2):
        spread(part, narrow_at[part])
    send_notes()
    for part in range(2):
        for side in range(2):
            near = plus(narrow_at[part], 3 if side == 0 else 1)
            target = neighbours[narrow_axis[part], side]
            arrive(
                chunk(rows, part, wide_at[part], near),
                two_send.at[part, side],
                two_recv.at[part, side],
                target,
            )
            block = chunk(rows, part, wide_at[part], near, 2 * side, 2)
            send(
                block,
                block,
                relay_two_send.at[part, side],
                relay_two_recv.at[part, side],
                target,
            )
            spread(part, near)
    for part in range(2):
        far = plus(narrow_at[part], 2)
        for side in range(2):
            arrive(
                chunk(rows, part, wide_at[part], far, 2 * side, 2),
                relay_two_send.at[part, side],
                relay_two_recv.at[part, side],
                neighbours[narrow_axis[part], side],
            )
        spread(part, far)
    for step in range(4):
        for part in range(2):
            narrow = plus(narrow_at[part], (0, 1, 3, 2)[step])
            for side in range(2):
                near = plus(wide_at[part], 3 if side == 0 else 1)
                target = neighbours[wide_axis[part], side]
                sem = (part, side, narrow)
                arrive(
                    chunk(rows, part, near, narrow), three_send.at[sem], three_recv.at[sem], target
                )
                share(part, near, narrow)

                @pl.when((narrow >= 2) == (side == 1))
                def _():
                    block = chunk(rows, part, near, narrow)
                    remote(
                        block,
                        block,
                        relay_three_send.at[part, narrow],
                        relay_three_recv.at[part, narrow],
                        target,
                    ).start()

    for part in range(2):
        for narrow in range(4):
            side = narrow // 2
            far = plus(wide_at[part], 2)
            arrive(
                chunk(rows, part, far, narrow),
                relay_three_send.at[part, narrow],
                relay_three_recv.at[part, narrow],
                neighbours[wide_axis[part], side],
            )
            share(part, far, narrow)
    for part in range(2):
        for wide in range(4):
            for narrow in range(4):
                at_x, at_y = (wide, narrow) if part == 0 else (narrow, wide)
                sem = (part, wide, narrow)
                block = rows.at[
                    (at_y % 2) * 4 + at_x, 1 - core, at_y // 2, pl.ds(part * 4, 4)
                ]
                arrive(block, share_send.at[sem], share_recv.at[sem], other_core)

    for fetch in fetches[1:]:
        fetch.wait()

    @pl.loop(1, N_EXP)
    def _(step):
        source = lax.rem(e + step, N_EXP)
        spot = lax.rem(source, 2) * 16 + lax.rem(source // 2, 2) * 8 + source // 4
        remote(
            notes.at[source], noted.at[spot], note_send.at[source], note_recv.at[spot], (c, source)
        ).wait_recv()

    note = jnp.broadcast_to(noted[...], (N_EXP, ROWS, 128)).reshape(N_EXP * ROWS, 128)
    lane = lax.broadcasted_iota(jnp.int32, (N_EXP * ROWS, 128), 1)
    beam = row_index(N_EXP * ROWS) & 15
    routed = jnp.sum(jnp.where(lane == beam, note, 0.0), axis=-1, keepdims=True)
    scale = jnp.sum(jnp.where(lane == beam + 16, note, 0.0), axis=-1, keepdims=True)
    total = jnp.zeros((512, 256), F32)
    for k in range(N_CTX):
        total = total + dot(rows[k].reshape(512, COLS), both[k])
    total = total * scale
    gate, up = total[:, :128], total[:, 128:]
    silu = gate / (1.0 + jnp.exp(-gate))
    hidden[...] = (silu * up * routed).astype(BF16).reshape(2, 256, 128)

    def far_send(part):
        far = plus(wide_at[part], 2)
        for side in range(2):
            for k in range(2):
                sem = (part, side, k)
                send(
                    chunk(sums, part, far, 2 * side + k),
                    half_one.at[sem],
                    half_one_send.at[sem],
                    half_one_recv.at[sem],
                    neighbours[wide_axis[part], side],
                )

    blocks = [
        peer(*k) for k in ((0, 2), (1, 2), (0, 1), (0, 3), (0, 0), (1, 1), (1, 3), (1, 0))
    ]
    for k in blocks:
        at = pl.ds(pl.multiple_of(k * COLS, 128), COLS)
        sums[k, 1 - core] = (
            dot(hidden[1 - core], down[:, at]).astype(BF16).reshape(2, 8, ROWS, COLS)
        )
        send(
            sums.at[k, 1 - core], from_core.at[k], cross_send.at[k], cross_recv.at[k], other_core
        )
    for number, k in enumerate(blocks):
        at = pl.ds(pl.multiple_of(k * COLS, 128), COLS)
        own = dot(hidden[core], down[:, at])
        arrive(from_core.at[k], cross_send.at[k], cross_recv.at[k], other_core)
        sums[k, core] = (
            (own + from_core[k].reshape(256, COLS).astype(F32))
            .astype(BF16)
            .reshape(2, 8, ROWS, COLS)
        )
        if number == 1:
            far_send(0)
        if number == 4:
            far_send(1)

    def add(ref, *others):
        value = ref[...].astype(F32)
        for other in others:
            value = value + other[...].astype(F32)
        ref[...] = value.astype(BF16)

    def wide_send(part, side, narrow):
        near = plus(wide_at[part], 1 if side == 0 else 3)
        sem = (part, side, narrow)
        send(
            chunk(sums, part, near, narrow),
            whole_one.at[sem],
            whole_one_send.at[sem],
            whole_one_recv.at[sem],
            neighbours[wide_axis[part], side],
        )

    for part in range(2):
        for side in range(2):
            for k in range(2):
                wide_send(part, side, 2 * (1 - side) + k)
    for part in range(2):
        for side in range(2):
            near = plus(wide_at[part], 1 if side == 0 else 3)
            for k in range(2):
                sem = (part, side, k)
                arrive(
                    half_one.at[sem],
                    half_one_send.at[sem],
                    half_one_recv.at[sem],
                    neighbours[wide_axis[part], side],
                )
                add(chunk(sums, part, near, 2 * side + k), half_one.at[sem])
                wide_send(part, side, 2 * side + k)

    def narrow_send(part, side):
        near = plus(narrow_at[part], 1 if side == 0 else 3)
        sem = (part, side)
        send(
            chunk(sums, part, wide_at[part], near),
            whole_two.at[sem],
            whole_two_send.at[sem],
            whole_two_recv.at[sem],
            neighbours[narrow_axis[part], side],
        )

    for step in (2, 1, 3, 0):
        for part in range(2):
            narrow = plus(narrow_at[part], step)
            for side in range(2):
                sem = (part, side, narrow)
                arrive(
                    whole_one.at[sem],
                    whole_one_send.at[sem],
                    whole_one_recv.at[sem],
                    neighbours[wide_axis[part], side],
                )
            add(
                chunk(sums, part, wide_at[part], narrow),
                whole_one.at[part, 0, narrow],
                whole_one.at[part, 1, narrow],
            )
            if step == 2:
                for side in range(2):
                    sem = (part, side)
                    send(
                        chunk(sums, part, wide_at[part], narrow, 2 * side, 2),
                        half_two.at[sem],
                        half_two_send.at[sem],
                        half_two_recv.at[sem],
                        neighbours[narrow_axis[part], side],
                    )
    for part in range(2):
        for side in range(2):
            near = plus(narrow_at[part], 1 if side == 0 else 3)
            sem = (part, side)
            arrive(
                half_two.at[sem],
                half_two_send.at[sem],
                half_two_recv.at[sem],
                neighbours[narrow_axis[part], side],
            )
            add(chunk(sums, part, wide_at[part], near, 2 * side, 2), half_two.at[sem])
            narrow_send(part, side)
    for part in range(2):
        for side in range(2):
            sem = (part, side)
            arrive(
                whole_two.at[sem],
                whole_two_send.at[sem],
                whole_two_recv.at[sem],
                neighbours[narrow_axis[part], side],
            )
        add(
            chunk(sums, part, wide_at[part], narrow_at[part]),
            whole_two.at[part, 0],
            whole_two.at[part, 1],
        )
    for step in range(1, 8):
        to = lax.rem(z + step, 8)
        send(
            sums.at[c, core, y_hi, to],
            last.at[z],
            last_send.at[to],
            last_recv.at[z],
            device(x, y, to, core),
        )
    last[z] = sums[c, core, y_hi, z]
    for step in range(1, 8):
        source = lax.rem(z + step, 8)
        arrive(
            last.at[source],
            last_send.at[source],
            last_recv.at[source],
            device(x, y, source, core),
        )
    result = state[...]
    for k in range(8):
        result = result + last[k].astype(F32)
    out_ref[...] = result.astype(BF16)

    for copy in sent:
        copy.wait_send()
    for part in range(2):
        for narrow in range(4):
            block = chunk(rows, part, wide_at[part], narrow)
            remote(
                block,
                block,
                relay_three_send.at[part, narrow],
                relay_three_recv.at[part, narrow],
                neighbours[wide_axis[part], narrow // 2],
            ).wait_send()

    @pl.loop(1, N_EXP)
    def _(step):
        head_copy(step).wait_send()
        note_copy(step).wait_send()


VMEM = pl.BlockSpec(memory_space=pltpu.VMEM)
SMEM = pl.BlockSpec(memory_space=pltpu.SMEM)
ANY = pl.BlockSpec(memory_space=pl.ANY)
DMA = pltpu.SemaphoreType.DMA


def per_device(
    queries,
    prompt_cache,
    new_latent,
    parents,
    lengths,
    value_weight,
    output_weight,
    residual,
    norm_gain,
    expert_ids,
    expert_weights,
    expert_gate,
    expert_up,
    expert_down,
):
    key_width = queries.shape[3]
    pairs = [(N_CTX,), (N_CTX,), (N_EXP,), (N_CTX,), (2,), (8,), (8,), (N_CTX,), (N_EXP,)]
    pairs += [(8,), (2, 2), (2, 2), (2, 2, 4), (2, 4), (2, 4, 4)]
    pairs += [(8,), (2, 2, 2), (2, 2, 4), (2, 2), (2, 2), (8,)]
    out = pl.pallas_call(
        layer_kernel,
        out_shape=jax.ShapeDtypeStruct((ROWS, COLS), BF16),
        in_specs=[SMEM, SMEM] + [VMEM] * 6 + [ANY, VMEM, VMEM, ANY, ANY, ANY],
        out_specs=VMEM,
        scratch_shapes=[
            pltpu.VMEM((N_CTX, 128, LAT), BF16),
            pltpu.VMEM((N_CTX, 8, 128), F32),
            pltpu.VMEM((N_CTX, 128, LAT), BF16),
            pltpu.VMEM((N_CTX, 8, 128), F32),
            pltpu.VMEM((3, 512, 512), BF16),
            pltpu.VMEM((N_EXP, ROWS, 128), BF16),
            pltpu.VMEM((N_EXP, ROWS, 128), BF16),
            pltpu.VMEM((256, COLS), BF16),
            pltpu.VMEM((N_CTX, 64, 256), BF16),
            pltpu.VMEM((2, 256, 256), BF16),
            pltpu.VMEM((2, 8, ROWS, COLS), BF16),
            pltpu.VMEM((2, 8, ROWS, COLS), BF16),
            pltpu.VMEM((2, 8, ROWS, COLS), BF16),
            pltpu.VMEM((8, ROWS, COLS), BF16),
            pltpu.VMEM((8, ROWS, COLS), BF16),
            pltpu.VMEM((N_CTX, ROWS, 128), F32),
            pltpu.VMEM((ROWS, COLS), F32),
            pltpu.VMEM((N_EXP, 1, 128), F32),
            pltpu.VMEM((N_EXP, 1, 128), F32),
            pltpu.VMEM((N_CTX, 2, 2, 8, ROWS, COLS), BF16),
            pltpu.VMEM((N_CTX, 2, 2, 8, ROWS, COLS), BF16),
            pltpu.VMEM((N_CTX, 2, 8, ROWS, COLS), BF16),
            pltpu.VMEM((2, 2, 2, 4, ROWS, COLS), BF16),
            pltpu.VMEM((2, 2, 4, 4, ROWS, COLS), BF16),
            pltpu.VMEM((2, 2, 2, ROWS, COLS), BF16),
            pltpu.VMEM((2, 2, 4, ROWS, COLS), BF16),
            pltpu.VMEM((8, ROWS, COLS), BF16),
            pltpu.VMEM((2, 256, 128), BF16),
            pltpu.VMEM((N_CTX, COLS, 256), BF16),
            pltpu.VMEM((128, N_CTX * COLS), BF16),
            DMA((4,)),
        ]
        + [DMA(shape) for shape in pairs for _ in range(2)],
        compiler_params=pltpu.CompilerParams(
            collective_id=0, has_side_effects=True, vmem_limit_bytes=VMEM_LIMIT
        ),
        name="layer",
    )(
        lengths,
        parents.reshape(8),
        queries.reshape(N_CTX, 128, key_width),
        prompt_cache[0].T,
        new_latent.reshape(ROWS, key_width),
        expert_ids.reshape(ROWS, 8),
        expert_weights.reshape(ROWS, 8),
        value_weight,
        output_weight,
        residual.reshape(ROWS, N_CTX * COLS),
        norm_gain.reshape(N_CTX, COLS),
        expert_gate.reshape(N_CTX, COLS, 128),
        expert_up.reshape(N_CTX, COLS, 128),
        expert_down[0],
    )
    return out.reshape(2, 8, COLS)


def solution(mesh):
    in_specs = (
        P(None, "exp", None, None),
        P("exp", "ctx", None),
        P(None, "exp", None),
        P("exp", None),
        P("exp"),
        P("exp", None, None),
        P("exp", None),
        P(None, "exp", None),
        P(),
        P(None, "exp", None),
        P(None, "exp", None),
        P("exp", None, "ctx"),
        P("exp", None, "ctx"),
        P("exp", "ctx", None),
    )
    out_specs = P(None, "exp", "ctx")
    return jax.shard_map(
        per_device, mesh=mesh, in_specs=in_specs, out_specs=out_specs, check_vma=False
    )
```

```python
import functools

import jax
import jax.numpy as jnp
from jax import lax
from jax.experimental import pallas as pl
from jax.experimental.pallas import tpu as pltpu
from jax.sharding import PartitionSpec as P

SCALE = 0.07216878364870322
NEGATIVE = -1e30
BF16 = jnp.bfloat16
F32 = jnp.float32
N_CTX = 8
N_EXP = 32
ROWS = 16
MINE = 2
HEADS = 64
LAT = 512
COLS = 896
PARTS = ((0, 384), (384, 256), (640, 256))
HALVES = ((2, 1), (3, 0))
VMEM_LIMIT = 56 * 1024 * 1024


def coordinates():
    c, e = lax.axis_index("ctx"), lax.axis_index("exp")
    x, y_lo = lax.rem(c, 4), c // 4
    z, y_hi, core = e // 4, lax.rem(e // 2, 2), lax.rem(e, 2)
    return c, e, x, y_hi * 2 + y_lo, z, core


def device(x, y, z, core):
    return (lax.rem(y, 2) * 4 + x, z * 4 + (y // 2) * 2 + core)


def greet(barrier, target):
    pl.semaphore_signal(
        barrier, inc=1, device_id=target, device_id_type=pl.DeviceIdType.MESH
    )


def remote(source, target_ref, send_sem, recv_sem, target):
    return pltpu.make_async_remote_copy(
        src_ref=source,
        dst_ref=target_ref,
        send_sem=send_sem,
        recv_sem=recv_sem,
        device_id=target,
        device_id_type=pl.DeviceIdType.MESH,
    )


def one_hot(wanted, columns):
    return jnp.where(
        lax.broadcasted_iota(jnp.int32, (wanted.shape[0], columns), 1) == wanted, 1.0, 0.0
    ).astype(BF16)


def row_index(count):
    return lax.broadcasted_iota(jnp.int32, (count, 1), 0)


def dot(a, b):
    return jnp.dot(a, b, preferred_element_type=F32)


def dot_t(a, b):
    return lax.dot_general(a, b, (((1,), (1,)), ((), ())), preferred_element_type=F32)


def layer_kernel(
    length_ref,
    parents_ref,
    q_ref,
    cache_ref,
    new_ref,
    ids_ref,
    gates_ref,
    wv_ref,
    wo_ref,
    residual_ref,
    gain_ref,
    gate_ref,
    up_ref,
    down_ref,
    out_ref,
    part,
    stat,
    got,
    got_stat,
    orders,
    heads,
    by_head,
    wo_cols,
    values,
    ordered,
    crossing,
    crossed,
    shares,
    from_y,
    from_z,
    squares,
    state,
    notes,
    noted,
    rows,
    sums,
    from_core,
    half_one,
    whole_one,
    half_two,
    whole_two,
    ring_sums,
    y_sums,
    x_sums,
    last,
    hidden,
    both,
    down,
    weight_sems,
    part_send,
    part_recv,
    stat_send,
    stat_recv,
    head_send,
    head_recv,
    value_send,
    value_recv,
    crossing_send,
    crossing_recv,
    y_send,
    y_recv,
    zsum_send,
    zsum_recv,
    square_send,
    square_recv,
    note_send,
    note_recv,
    z_send,
    z_recv,
    x_send,
    x_recv,
    y_row_send,
    y_row_recv,
    two_send,
    two_recv,
    relay_two_send,
    relay_two_recv,
    three_send,
    three_recv,
    relay_three_send,
    relay_three_recv,
    ring_send,
    ring_recv,
    share_send,
    share_recv,
    share_z_send,
    share_z_recv,
    cross_send,
    cross_recv,
    half_one_send,
    half_one_recv,
    whole_one_send,
    whole_one_recv,
    half_two_send,
    half_two_recv,
    whole_two_send,
    whole_two_recv,
    ring_sum_send,
    ring_sum_recv,
    y_sum_send,
    y_sum_recv,
    x_sum_send,
    x_sum_recv,
    last_send,
    last_recv,
):
    c, e, x, y, z, core = coordinates()
    y_hi, y_lo = y // 2, lax.rem(y, 2)

    def plus(a, k):
        return lax.rem(a + k, 4)

    neighbours = {
        ("x", 0): device(plus(x, 1), y, z, core),
        ("x", 1): device(plus(x, 3), y, z, core),
        ("y", 0): device(x, plus(y, 1), z, core),
        ("y", 1): device(x, plus(y, 3), z, core),
    }
    other_core = device(x, y, z, 1 - core)
    wide_axis, narrow_axis = ("x", "y"), ("y", "x")
    wide_at, narrow_at = (x, y), (y, x)

    barrier = pltpu.get_barrier_semaphore()
    for step in range(1, N_CTX):
        greet(barrier, (lax.rem(c + step, N_CTX), e))

    @pl.loop(1, N_EXP)
    def _(step):
        greet(barrier, (c, lax.rem(e + step, N_EXP)))

    greet(barrier, device(x, 3 - y, z, core))

    columns = pl.ds(pl.multiple_of(c * COLS, 128), COLS)
    fetches = [
        pltpu.make_async_copy(wo_ref.at[:, columns], wo_cols, weight_sems.at[0]),
        pltpu.make_async_copy(gate_ref, both.at[:, :, pl.ds(0, 128)], weight_sems.at[1]),
        pltpu.make_async_copy(up_ref, both.at[:, :, pl.ds(128, 128)], weight_sems.at[2]),
        pltpu.make_async_copy(down_ref, down, weight_sems.at[3]),
    ]
    for fetch in fetches:
        fetch.start()

    sent = []

    def send(source, target_ref, send_sem, recv_sem, target):
        copy = remote(source, target_ref, send_sem, recv_sem, target)
        copy.start()
        sent.append(copy)

    def arrive(ref, send_sem, recv_sem, target):
        remote(ref, ref, send_sem, recv_sem, target).wait_recv()

    length = length_ref[0]
    positions = cache_ref.shape[1]
    live = (
        c * positions + lax.broadcasted_iota(jnp.int32, (1, positions), 1)
    ) < length
    wide_lane = lax.broadcasted_iota(jnp.int32, (128, 128), 1)

    def partial(target, sums_ref, stats_ref):
        scores = dot(q_ref[target], cache_ref[...]) * SCALE
        scores = jnp.where(live, scores, NEGATIVE)
        top = jnp.max(scores, axis=-1, keepdims=True)
        weights = jnp.where(live, jnp.exp(scores - top), 0.0)
        total = jnp.sum(weights, axis=-1, keepdims=True)
        sums_ref[...] = dot_t(weights.astype(BF16), cache_ref[:LAT, :]).astype(BF16)
        stats_ref[...] = jnp.where(
            wide_lane == 0, top, jnp.where(wide_lane == 1, total, 0.0)
        ).T[:8]

    def peer(flip, step):
        return lax.rem(y_lo + flip, 2) * 4 + plus(x, step)

    def send_partial(target):
        where = (target, e)
        send(part.at[target], got.at[c], part_send.at[target], part_recv.at[c], where)
        send(stat.at[target], got_stat.at[c], stat_send.at[target], stat_recv.at[c], where)

    peers = [peer(*k) for k in ((1, 2), (0, 2), (1, 1), (0, 1), (1, 3), (0, 3), (1, 0))]
    partial(peers[0], part.at[peers[0]], stat.at[peers[0]])
    pl.semaphore_wait(barrier, N_CTX - 1 + N_EXP - 1 + 1)
    send_partial(peers[0])
    for target in peers[1:]:
        partial(target, part.at[target], stat.at[target])
        send_partial(target)
    partial(c, got.at[c], got_stat.at[c])

    row = row_index(512)
    orders[0] = one_hot(
        ((row >> 2) & 3) * 128 + ((row >> 1) & 1) * HEADS + (row >> 4) * 2 + (row & 1), 512
    )
    orders[1] = one_hot(
        ((row >> 1) & 31) * 16 + ((row >> 6) & 3) * 4 + (row & 1) * 2 + (row >> 8), 512
    )
    orders[2] = one_hot(
        ((row >> 1) & 7) * 64
        + ((row >> 4) & 7) * 8
        + ((row >> 7) & 1) * 4
        + (row >> 8) * 2
        + (row & 1),
        512,
    )

    row = row_index(128)
    base = lax.rem(c, 4) * MINE
    wanted = jnp.where(
        row == 0,
        c * MINE,
        jnp.where(
            row == 1,
            c * MINE + 1,
            jnp.where(
                row == 2, parents_ref[base], jnp.where(row == 3, parents_ref[base + 1], -1)
            ),
        ),
    )
    keys = dot(one_hot(wanted, ROWS), new_ref[...]).astype(BF16)
    scores = dot_t(q_ref[c], keys) * SCALE
    second = jnp.where(row >= HEADS, 1, 0)
    tail_at = jnp.where(c >= 4, second + 2, -1)
    valid = (wide_lane == second) | (wide_lane == tail_at)
    scores = jnp.where(valid, scores, NEGATIVE)
    top = jnp.max(scores, axis=-1, keepdims=True)
    weights = jnp.where(valid, jnp.exp(scores - top), 0.0)
    own_total = jnp.sum(weights, axis=-1, keepdims=True)
    own_sum = dot(weights.astype(BF16), keys[:, :LAT])

    lane = lax.broadcasted_iota(jnp.int32, (ROWS, 128), 1)
    dense = jnp.zeros((ROWS, 128), F32)
    for k in range(8):
        dense = jnp.where(lane == ids_ref[:, k : k + 1], gates_ref[:, k : k + 1], dense)

    for source in peers:
        where = (source, e)
        arrive(got_stat.at[source], stat_send.at[source], stat_recv.at[source], where)
    stats = got_stat[...].reshape(N_CTX * 8, 128).T
    peak = top
    for source in range(N_CTX):
        peak = jnp.maximum(peak, stats[:, 8 * source : 8 * source + 1])
    factor = jnp.exp(top - peak)
    total = own_total * factor
    summed = own_sum * factor
    for source in range(N_CTX):
        factor = jnp.exp(stats[:, 8 * source : 8 * source + 1] - peak)
        total = total + stats[:, 8 * source + 1 : 8 * source + 2] * factor
    for source in peers:
        arrive(got.at[source], part_send.at[source], part_recv.at[source], (source, e))
    for source in range(N_CTX):
        factor = jnp.exp(stats[:, 8 * source : 8 * source + 1] - peak)
        summed = summed + got[source].astype(F32) * factor
    attended = (summed / total).astype(BF16)
    stacked = jnp.concatenate([attended[:, 128 * k : 128 * k + 128] for k in range(4)], axis=0)
    heads[...] = dot(orders[0], stacked).astype(BF16).reshape(N_EXP, ROWS, 128)

    def head_copy(step):
        target = lax.rem(e + step, N_EXP)
        return remote(
            heads.at[target], by_head.at[e], head_send.at[target], head_recv.at[e], (c, target)
        )

    @pl.loop(1, N_EXP)
    def _(step):
        head_copy(step).start()

    by_head[e] = heads[e]

    @pl.loop(1, N_EXP)
    def _(step):
        source = lax.rem(e + step, N_EXP)
        remote(
            heads.at[source],
            by_head.at[source],
            head_send.at[source],
            head_recv.at[source],
            (c, source),
        ).wait_recv()

    latents = dot(orders[1], by_head[...].reshape(512, 128)).astype(BF16)
    halves = []
    for parity in range(2):
        value = jnp.zeros((64, 128), F32)
        for quarter in range(4):
            at = (parity * 4 + quarter) * 64
            value = value + dot(
                latents[at : at + 64], wv_ref[parity, 128 * quarter : 128 * quarter + 128, :]
            )
        halves.append(value.astype(BF16))
    values[c] = jnp.concatenate(halves, axis=1)

    for target in peers:
        send(values.at[c], values.at[c], value_send.at[target], value_recv.at[c], (target, e))
    for source in peers:
        arrive(values.at[source], value_send.at[source], value_recv.at[source], (source, e))
    ordered[...] = dot(orders[2], values[...].reshape(512, 256)).astype(BF16).reshape(2, 256, 256)
    fetches[0].wait()
    crossing[...] = dot(ordered[1 - core], wo_cols[...]).astype(BF16).reshape(2, 8, ROWS, COLS)
    for half in (1, 0):
        at = lax.rem(y_hi + half, 2)
        send(
            crossing.at[at],
            crossed.at[at],
            crossing_send.at[at],
            crossing_recv.at[at],
            other_core,
        )
    other_y = device(x, plus(y, 2), z, core)
    for half in (1, 0):
        at = lax.rem(y_hi + half, 2)
        own = dot(ordered[core, pl.ds(pl.multiple_of(at * 128, 128), 128)], wo_cols[...])
        arrive(crossed.at[at], crossing_send.at[at], crossing_recv.at[at], other_core)
        own = own + crossed[at].reshape(128, COLS).astype(F32)
        shares[at] = own.astype(BF16).reshape(8, ROWS, COLS)
        if half:
            for step in (4, 3, 5, 2, 6, 1, 7, 0):
                to = lax.rem(z + step, 8)
                send(shares.at[at, to], from_y.at[to], y_send.at[to], y_recv.at[to], other_y)
    for step in (4, 3, 5, 2, 6, 1, 7, 0):
        to = lax.rem(z + step, 8)
        arrive(from_y.at[to], y_send.at[to], y_recv.at[to], other_y)
        both_y = shares[y_hi, to].astype(F32) + from_y[to].astype(F32)
        if step:
            shares[y_hi, to] = both_y.astype(BF16)
            send(
                shares.at[y_hi, to],
                from_z.at[z],
                zsum_send.at[to],
                zsum_recv.at[z],
                device(x, y, to, core),
            )
    value = residual_ref[:, columns].astype(F32) + both_y
    for step in range(1, 8):
        source = lax.rem(z + step, 8)
        arrive(
            from_z.at[source],
            zsum_send.at[source],
            zsum_recv.at[source],
            device(x, y, source, core),
        )
        value = value + from_z[source].astype(F32)
    state[...] = value
    rows[c, core, y_hi, z] = (value * gain_ref[pl.ds(c, 1), :]).astype(BF16)
    squares[c] = jnp.broadcast_to(jnp.sum(value * value, axis=-1, keepdims=True), (ROWS, 128))
    for target in peers:
        send(squares.at[c], squares.at[c], square_send.at[target], square_recv.at[c], (target, e))

    def note_copy(step):
        target = lax.rem(e + step, N_EXP)
        spot = core * 16 + y_hi * 8 + z
        return remote(
            notes.at[target], noted.at[spot], note_send.at[target], note_recv.at[spot], (c, target)
        )

    def send_notes():
        for source in peers:
            arrive(squares.at[source], square_send.at[source], square_recv.at[source], (source, e))
        mean = jnp.sum(squares[...], axis=0) * (1.0 / (N_CTX * COLS))
        scale = lax.rsqrt(mean + 1e-06)
        block = jnp.concatenate([dense, scale, jnp.zeros((96, 128), F32)], axis=0).T
        notes[...] = block[:N_EXP].reshape(N_EXP, 1, 128)
        noted[core * 16 + y_hi * 8 + z] = notes[e]

        @pl.loop(1, N_EXP)
        def _(step):
            note_copy(step).start()

    def chunk(ref, part, wide, narrow, start=0, count=8):
        at_x, at_y = (wide, narrow) if part == 0 else (narrow, wide)
        first_lane, lanes = PARTS[part]
        return ref.at[
            lax.rem(at_y, 2) * 4 + at_x,
            core,
            at_y // 2,
            pl.ds(start, count),
            :,
            pl.ds(first_lane, lanes),
        ]

    def layer(ref, at_z, at_y):
        return ref.at[pl.ds(lax.rem(at_y, 2) * 4, 4), core, at_y // 2, at_z, :, pl.ds(*PARTS[2])]

    along_z = (device(x, y, lax.rem(z + 1, 8), core), device(x, y, lax.rem(z + 7, 8), core))

    def behind(side, hop):
        return lax.rem(z + (8 - hop if side == 0 else hop), 8)

    for step in (4, 3, 5, 2, 6, 1, 7):
        to = lax.rem(z + step, 8)
        block = rows.at[c, core, y_hi, z, :, pl.ds(0, PARTS[2][0])]
        send(block, block, z_send.at[to], z_recv.at[z], device(x, y, to, core))
    block = rows.at[c, core, y_hi, z, :, pl.ds(*PARTS[2])]
    for step in (2, 1, 3):
        send(
            block,
            block,
            x_send.at[step],
            x_recv.at[step],
            device(plus(x, step), y, z, core),
        )

    def share(part, wide, narrow, step, hop):
        block = chunk(rows, part, wide, narrow)
        sem = (part, step, hop)
        send(block, block, share_send.at[sem], share_recv.at[sem], other_core)

    def spread(part, step):
        narrow = plus(narrow_at[part], step)
        block = chunk(rows, part, wide_at[part], narrow)
        for side in range(2):
            sem = (part, side, step)
            send(
                block,
                block,
                three_send.at[sem],
                three_recv.at[sem],
                neighbours[wide_axis[part], side],
            )
        share(part, wide_at[part], narrow, step, 0)

    def spread_z(step):
        block = layer(rows, z, plus(y, step))
        for side in range(2):
            sem = (side, 0, step)
            send(block, block, ring_send.at[sem], ring_recv.at[sem], along_z[side])

    def share_z(at_z, hop):
        block = rows.at[:, core, :, at_z, :, pl.ds(*PARTS[2])]
        send(block, block, share_z_send.at[hop], share_z_recv.at[hop], other_core)

    for step in (1, 3, 2):
        source = plus(x, 4 - step)
        arrive(
            rows.at[y_lo * 4 + source, core, y_hi, z, :, pl.ds(*PARTS[2])],
            x_send.at[step],
            x_recv.at[step],
            device(source, y, z, core),
        )
    block = layer(rows, z, y)
    for step in (2, 1, 3):
        send(
            block,
            block,
            y_row_send.at[step],
            y_row_recv.at[step],
            device(x, plus(y, step), z, core),
        )
    spread_z(0)
    for step in range(1, 8):
        source = lax.rem(z + step, 8)
        arrive(
            rows.at[c, core, y_hi, source, :, pl.ds(0, PARTS[2][0])],
            z_send.at[source],
            z_recv.at[source],
            device(x, y, source, core),
        )
    for part in range(2):
        block = chunk(rows, part, wide_at[part], narrow_at[part])
        for side in range(2):
            send(
                block,
                block,
                two_send.at[part, side],
                two_recv.at[part, side],
                neighbours[narrow_axis[part], side],
            )
    for part in range(2):
        spread(part, 0)
    for step in (1, 3, 2):
        source = plus(y, 4 - step)
        arrive(
            layer(rows, z, source),
            y_row_send.at[step],
            y_row_recv.at[step],
            device(x, source, z, core),
        )
        spread_z(4 - step)
    share_z(z, 0)
    for part in range(2):
        for side in range(2):
            step = 3 if side == 0 else 1
            near = plus(narrow_at[part], step)
            target = neighbours[narrow_axis[part], side]
            arrive(
                chunk(rows, part, wide_at[part], near),
                two_send.at[part, side],
                two_recv.at[part, side],
                target,
            )
            block = chunk(rows, part, wide_at[part], near, 4 * side, 4)
            send(
                block,
                block,
                relay_two_send.at[part, side],
                relay_two_recv.at[part, side],
                target,
            )
            spread(part, step)
    send_notes()

    def ring(hop):
        for step in (0, 3, 1, 2):
            for side in range(2):
                if hop == 4 and (step in (0, 3)) != (side == 0):
                    continue
                block = layer(rows, behind(side, hop), plus(y, step))
                sem = (side, hop - 1, step)
                arrive(block, ring_send.at[sem], ring_recv.at[sem], along_z[side])
                if hop < 3 or (hop == 3 and (step in (0, 3)) == (side == 0)):
                    sem = (side, hop, step)
                    send(block, block, ring_send.at[sem], ring_recv.at[sem], along_z[side])
        if hop < 4:
            for side in range(2):
                share_z(behind(side, hop), 2 * hop - 1 + side)
        else:
            share_z(behind(0, 4), 7)

    def near(step):
        for part in range(2):
            narrow = plus(narrow_at[part], step)
            for side in range(2):
                wide = plus(wide_at[part], 3 if side == 0 else 1)
                target = neighbours[wide_axis[part], side]
                sem = (part, side, step)
                block = chunk(rows, part, wide, narrow)
                arrive(block, three_send.at[sem], three_recv.at[sem], target)
                if (step in (0, 3)) == (side == 0):
                    send(
                        block,
                        block,
                        relay_three_send.at[part, step],
                        relay_three_recv.at[part, step],
                        target,
                    )
                share(part, wide, narrow, step, 1 + side)

    near(0)
    ring(1)
    for part in range(2):
        far = plus(narrow_at[part], 2)
        for side in range(2):
            arrive(
                chunk(rows, part, wide_at[part], far, 4 * side, 4),
                relay_two_send.at[part, side],
                relay_two_recv.at[part, side],
                neighbours[narrow_axis[part], side],
            )
        spread(part, 2)
    near(3)
    near(1)
    ring(2)
    near(2)
    ring(3)
    ring(4)
    for step in (0, 3, 1, 2):
        for part in range(2):
            side = 0 if step in (0, 3) else 1
            wide, narrow = plus(wide_at[part], 2), plus(narrow_at[part], step)
            arrive(
                chunk(rows, part, wide, narrow),
                relay_three_send.at[part, step],
                relay_three_recv.at[part, step],
                neighbours[wide_axis[part], side],
            )
            share(part, wide, narrow, step, 3)
    for hop in range(8):
        source = z if hop == 0 else behind(0, 4) if hop == 7 else behind((hop - 1) % 2, (hop + 1) // 2)
        arrive(
            rows.at[:, 1 - core, :, source, :, pl.ds(*PARTS[2])],
            share_z_send.at[hop],
            share_z_recv.at[hop],
            other_core,
        )
    for part in range(2):
        first_lane, lanes = PARTS[part]
        for step in range(4):
            for hop in range(4):
                wide = plus(wide_at[part], (0, 3, 1, 2)[hop])
                narrow = plus(narrow_at[part], step)
                at_x, at_y = (wide, narrow) if part == 0 else (narrow, wide)
                block = rows.at[
                    lax.rem(at_y, 2) * 4 + at_x,
                    1 - core,
                    at_y // 2,
                    :,
                    :,
                    pl.ds(first_lane, lanes),
                ]
                sem = (part, step, hop)
                arrive(block, share_send.at[sem], share_recv.at[sem], other_core)

    for fetch in fetches[1:]:
        fetch.wait()

    @pl.loop(1, N_EXP)
    def _(step):
        source = lax.rem(e + step, N_EXP)
        spot = lax.rem(source, 2) * 16 + lax.rem(source // 2, 2) * 8 + source // 4
        remote(
            notes.at[source], noted.at[spot], note_send.at[source], note_recv.at[spot], (c, source)
        ).wait_recv()

    note = jnp.broadcast_to(noted[...], (N_EXP, ROWS, 128)).reshape(N_EXP * ROWS, 128)
    lane = lax.broadcasted_iota(jnp.int32, (N_EXP * ROWS, 128), 1)
    beam = row_index(N_EXP * ROWS) & 15
    routed = jnp.sum(jnp.where(lane == beam, note, 0.0), axis=-1, keepdims=True)
    scale = jnp.sum(jnp.where(lane == beam + 16, note, 0.0), axis=-1, keepdims=True)
    total = jnp.zeros((512, 256), F32)
    for k in range(N_CTX):
        total = total + dot(rows[k].reshape(512, COLS), both[k])
    total = total * scale
    gate, up = total[:, :128], total[:, 128:]
    silu = gate / (1.0 + jnp.exp(-gate))
    hidden[...] = (silu * up * routed).astype(BF16).reshape(2, 256, 128)

    def add(ref, *others):
        value = ref[...].astype(F32)
        for other in others:
            value = value + other[...].astype(F32)
        ref[...] = value.astype(BF16)

    def landed(ref, part, *index):
        return ref.at[(part, *index, slice(None), slice(None), pl.ds(0, PARTS[part][1]))]

    def piece(ref, part):
        return ref.at[:, :, :, pl.ds(*PARTS[part])]

    blocks = [
        peer(*k) for k in ((0, 2), (1, 2), (0, 1), (0, 3), (0, 0), (1, 1), (1, 3), (1, 0))
    ]

    def product(part, k, half):
        first_lane, lanes = PARTS[part]
        at = pl.ds(pl.multiple_of(k * COLS + first_lane, 128), lanes)
        return dot(hidden[half], down[:, at])

    def other(part):
        for k in blocks:
            block = piece(sums.at[k, 1 - core], part)
            block[...] = (
                product(part, k, 1 - core).astype(BF16).reshape(2, 8, ROWS, PARTS[part][1])
            )
            send(
                block,
                piece(from_core.at[k], part),
                cross_send.at[part, k],
                cross_recv.at[part, k],
                other_core,
            )

    def own(part, after):
        for number, k in enumerate(blocks):
            value = product(part, k, core).reshape(2, 8, ROWS, PARTS[part][1])
            block = piece(from_core.at[k], part)
            arrive(block, cross_send.at[part, k], cross_recv.at[part, k], other_core)
            piece(sums.at[k, core], part)[...] = (value + block[...].astype(F32)).astype(BF16)
            if number in after:
                after[number]()

    def far_send(part):
        wide = plus(wide_at[part], 2)
        for side in range(2):
            for k in range(2):
                step = HALVES[side][k]
                sem = (part, side, k)
                send(
                    chunk(sums, part, wide, plus(narrow_at[part], step)),
                    landed(half_one, *sem),
                    half_one_send.at[sem],
                    half_one_recv.at[sem],
                    neighbours[wide_axis[part], side],
                )

    def wide_send(part, side, step):
        wide = plus(wide_at[part], 1 if side == 0 else 3)
        sem = (part, side, step)
        send(
            chunk(sums, part, wide, plus(narrow_at[part], step)),
            landed(whole_one, *sem),
            whole_one_send.at[sem],
            whole_one_recv.at[sem],
            neighbours[wide_axis[part], side],
        )

    def near_send(part):
        for k in range(2):
            for side in range(2):
                wide_send(part, side, HALVES[1 - side][k])

    def near_add(part):
        for k in range(2):
            for side in range(2):
                wide = plus(wide_at[part], 1 if side == 0 else 3)
                step = HALVES[side][k]
                sem = (part, side, k)
                block = landed(half_one, *sem)
                arrive(
                    block,
                    half_one_send.at[sem],
                    half_one_recv.at[sem],
                    neighbours[wide_axis[part], side],
                )
                add(chunk(sums, part, wide, plus(narrow_at[part], step)), block)
                wide_send(part, side, step)

    def ahead(side, hop):
        return lax.rem(z + (hop if side == 0 else 8 - hop), 8)

    def ring_send_sum(hop, side, step):
        sem = (side, hop - 1, step)
        send(
            layer(sums, ahead(side, hop), plus(y, step)),
            ring_sums.at[sem],
            ring_sum_send.at[sem],
            ring_sum_recv.at[sem],
            along_z[side],
        )

    def ring_start():
        for k in range(2):
            for side in range(2):
                ring_send_sum(4, side, HALVES[side][k])
        for k in range(2):
            for side in range(2):
                ring_send_sum(3, side, HALVES[1 - side][k])

    def ring_sum(hop):
        for step in (2, 1, 3, 0):
            for side in range(2):
                if hop == 3 and step not in HALVES[side]:
                    continue
                sem = (side, hop, step)
                arrive(
                    ring_sums.at[sem],
                    ring_sum_send.at[sem],
                    ring_sum_recv.at[sem],
                    along_z[side],
                )
                if hop:
                    add(layer(sums, ahead(side, hop), plus(y, step)), ring_sums.at[sem])
                    ring_send_sum(hop, side, step)
            if hop == 0:
                add(
                    layer(sums, z, plus(y, step)),
                    ring_sums.at[0, 0, step],
                    ring_sums.at[1, 0, step],
                )
                if step:
                    send(
                        layer(sums, z, plus(y, step)),
                        y_sums.at[step],
                        y_sum_send.at[step],
                        y_sum_recv.at[step],
                        device(x, plus(y, step), z, core),
                    )

    def narrow_send(part, side):
        near = plus(narrow_at[part], 1 if side == 0 else 3)
        sem = (part, side)
        send(
            chunk(sums, part, wide_at[part], near),
            landed(whole_two, *sem),
            whole_two_send.at[sem],
            whole_two_recv.at[sem],
            neighbours[narrow_axis[part], side],
        )

    def wide_add(part, step):
        narrow = plus(narrow_at[part], step)
        for side in range(2):
            sem = (part, side, step)
            arrive(
                landed(whole_one, *sem),
                whole_one_send.at[sem],
                whole_one_recv.at[sem],
                neighbours[wide_axis[part], side],
            )
        add(
            chunk(sums, part, wide_at[part], narrow),
            landed(whole_one, part, 0, step),
            landed(whole_one, part, 1, step),
        )
        if step == 2:
            for side in range(2):
                sem = (part, side)
                send(
                    chunk(sums, part, wide_at[part], narrow, 4 * side, 4),
                    landed(half_two, *sem),
                    half_two_send.at[sem],
                    half_two_recv.at[sem],
                    neighbours[narrow_axis[part], side],
                )

    def narrow_add(part):
        for side in range(2):
            near = plus(narrow_at[part], 1 if side == 0 else 3)
            sem = (part, side)
            arrive(
                landed(half_two, *sem),
                half_two_send.at[sem],
                half_two_recv.at[sem],
                neighbours[narrow_axis[part], side],
            )
            add(
                chunk(sums, part, wide_at[part], near, 4 * side, 4), landed(half_two, *sem)
            )
            narrow_send(part, side)

    def narrow_end(part):
        for side in range(2):
            sem = (part, side)
            arrive(
                landed(whole_two, *sem),
                whole_two_send.at[sem],
                whole_two_recv.at[sem],
                neighbours[narrow_axis[part], side],
            )
        add(
            chunk(sums, part, wide_at[part], narrow_at[part]),
            landed(whole_two, part, 0),
            landed(whole_two, part, 1),
        )
        for step in (4, 3, 5, 2, 6, 1, 7):
            to = lax.rem(z + step, 8)
            send(
                sums.at[c, core, y_hi, to, :, pl.ds(*PARTS[part])],
                last.at[z, :, pl.ds(*PARTS[part])],
                last_send.at[part, to],
                last_recv.at[part, z],
                device(x, y, to, core),
            )

    other(0)
    other(2)
    own(0, {1: lambda: far_send(0)})
    near_send(0)
    own(2, {})
    ring_start()
    other(1)
    near_add(0)
    own(1, {4: lambda: far_send(1)})
    near_send(1)
    ring_sum(3)
    near_add(1)
    ring_sum(2)
    wide_add(0, 2)
    wide_add(1, 2)
    ring_sum(1)
    for step in (1, 3):
        for part in (1, 0):
            wide_add(part, step)
    ring_sum(0)
    narrow_add(1)
    narrow_add(0)
    for part in (1, 0):
        wide_add(part, 0)
    for step in (2, 1, 3):
        arrive(
            y_sums.at[step],
            y_sum_send.at[step],
            y_sum_recv.at[step],
            device(x, plus(y, 4 - step), z, core),
        )
    add(layer(sums, z, y), *(y_sums.at[step] for step in (1, 2, 3)))
    for step in (2, 1, 3):
        send(
            sums.at[y_lo * 4 + plus(x, step), core, y_hi, z, :, pl.ds(*PARTS[2])],
            x_sums.at[step],
            x_sum_send.at[step],
            x_sum_recv.at[step],
            device(plus(x, step), y, z, core),
        )
    narrow_end(1)
    narrow_end(0)
    for step in (1, 3, 2):
        arrive(
            x_sums.at[step],
            x_sum_send.at[step],
            x_sum_recv.at[step],
            device(plus(x, 4 - step), y, z, core),
        )

    def finish(part, value):
        lanes = pl.ds(*PARTS[part])
        value = value + state[:, lanes] + sums[c, core, y_hi, z, :, lanes].astype(F32)
        out_ref[:, lanes] = value.astype(BF16)

    finish(2, sum(x_sums[step].astype(F32) for step in (1, 2, 3)))
    for part in (1, 0):
        value = jnp.zeros((ROWS, PARTS[part][1]), F32)
        for step in range(1, 8):
            source = lax.rem(z + step, 8)
            block = last.at[source, :, pl.ds(*PARTS[part])]
            arrive(
                block,
                last_send.at[part, source],
                last_recv.at[part, source],
                device(x, y, source, core),
            )
            value = value + block[...].astype(F32)
        finish(part, value)

    for copy in sent:
        copy.wait_send()

    @pl.loop(1, N_EXP)
    def _(step):
        head_copy(step).wait_send()
        note_copy(step).wait_send()


VMEM = pl.BlockSpec(memory_space=pltpu.VMEM)
SMEM = pl.BlockSpec(memory_space=pltpu.SMEM)
ANY = pl.BlockSpec(memory_space=pl.ANY)
DMA = pltpu.SemaphoreType.DMA


def per_device(
    queries,
    prompt_cache,
    new_latent,
    parents,
    lengths,
    value_weight,
    output_weight,
    residual,
    norm_gain,
    expert_ids,
    expert_weights,
    expert_gate,
    expert_up,
    expert_down,
):
    key_width = queries.shape[3]
    pairs = [(N_CTX,), (N_CTX,), (N_EXP,), (N_CTX,), (2,), (8,), (8,), (N_CTX,), (N_EXP,)]
    pairs += [(8,), (4,), (4,), (2, 2), (2, 2), (2, 2, 4), (2, 4), (2, 4, 4)]
    pairs += [(2, 4, 4), (8,), (3, 8), (2, 2, 2), (2, 2, 4), (2, 2)]
    pairs += [(2, 2), (2, 4, 4), (4,), (4,), (2, 8)]
    out = pl.pallas_call(
        layer_kernel,
        out_shape=jax.ShapeDtypeStruct((ROWS, COLS), BF16),
        in_specs=[SMEM, SMEM] + [VMEM] * 6 + [ANY, VMEM, VMEM, ANY, ANY, ANY],
        out_specs=VMEM,
        scratch_shapes=[
            pltpu.VMEM((N_CTX, 128, LAT), BF16),
            pltpu.VMEM((N_CTX, 8, 128), F32),
            pltpu.VMEM((N_CTX, 128, LAT), BF16),
            pltpu.VMEM((N_CTX, 8, 128), F32),
            pltpu.VMEM((3, 512, 512), BF16),
            pltpu.VMEM((N_EXP, ROWS, 128), BF16),
            pltpu.VMEM((N_EXP, ROWS, 128), BF16),
            pltpu.VMEM((256, COLS), BF16),
            pltpu.VMEM((N_CTX, 64, 256), BF16),
            pltpu.VMEM((2, 256, 256), BF16),
            pltpu.VMEM((2, 8, ROWS, COLS), BF16),
            pltpu.VMEM((2, 8, ROWS, COLS), BF16),
            pltpu.VMEM((2, 8, ROWS, COLS), BF16),
            pltpu.VMEM((8, ROWS, COLS), BF16),
            pltpu.VMEM((8, ROWS, COLS), BF16),
            pltpu.VMEM((N_CTX, ROWS, 128), F32),
            pltpu.VMEM((ROWS, COLS), F32),
            pltpu.VMEM((N_EXP, 1, 128), F32),
            pltpu.VMEM((N_EXP, 1, 128), F32),
            pltpu.VMEM((N_CTX, 2, 2, 8, ROWS, COLS), BF16),
            pltpu.VMEM((N_CTX, 2, 2, 8, ROWS, COLS), BF16),
            pltpu.VMEM((N_CTX, 2, 8, ROWS, COLS), BF16),
            pltpu.VMEM((2, 2, 2, 8, ROWS, 384), BF16),
            pltpu.VMEM((2, 2, 4, 8, ROWS, 384), BF16),
            pltpu.VMEM((2, 2, 4, ROWS, 384), BF16),
            pltpu.VMEM((2, 2, 8, ROWS, 384), BF16),
            pltpu.VMEM((2, 4, 4, 4, ROWS, 256), BF16),
            pltpu.VMEM((4, 4, ROWS, 256), BF16),
            pltpu.VMEM((4, ROWS, 256), BF16),
            pltpu.VMEM((8, ROWS, COLS), BF16),
            pltpu.VMEM((2, 256, 128), BF16),
            pltpu.VMEM((N_CTX, COLS, 256), BF16),
            pltpu.VMEM((128, N_CTX * COLS), BF16),
            DMA((4,)),
        ]
        + [DMA(shape) for shape in pairs for _ in range(2)],
        compiler_params=pltpu.CompilerParams(
            collective_id=0, has_side_effects=True, vmem_limit_bytes=VMEM_LIMIT
        ),
        name="layer",
    )(
        lengths,
        parents.reshape(8),
        queries.reshape(N_CTX, 128, key_width),
        prompt_cache[0].T,
        new_latent.reshape(ROWS, key_width),
        expert_ids.reshape(ROWS, 8),
        expert_weights.reshape(ROWS, 8),
        value_weight,
        output_weight,
        residual.reshape(ROWS, N_CTX * COLS),
        norm_gain.reshape(N_CTX, COLS),
        expert_gate.reshape(N_CTX, COLS, 128),
        expert_up.reshape(N_CTX, COLS, 128),
        expert_down[0],
    )
    return out.reshape(2, 8, COLS)


def solution(mesh):
    in_specs = (
        P(None, "exp", None, None),
        P("exp", "ctx", None),
        P(None, "exp", None),
        P("exp", None),
        P("exp"),
        P("exp", None, None),
        P("exp", None),
        P(None, "exp", None),
        P(),
        P(None, "exp", None),
        P(None, "exp", None),
        P("exp", None, "ctx"),
        P("exp", None, "ctx"),
        P("exp", "ctx", None),
    )
    out_specs = P(None, "exp", "ctx")
    return jax.shard_map(
        per_device, mesh=mesh, in_specs=in_specs, out_specs=out_specs, check_vma=False
    )
```

```python
import functools

import jax
import jax.numpy as jnp
from jax import lax
from jax.experimental import pallas as pl
from jax.experimental.pallas import tpu as pltpu
from jax.sharding import PartitionSpec as P

SCALE = 0.07216878364870322
NEGATIVE = -1e30
BF16 = jnp.bfloat16
F32 = jnp.float32
N_CTX = 8
N_EXP = 32
ROWS = 16
MINE = 2
HEADS = 64
LAT = 512
COLS = 896
PARTS = ((0, 384), (384, 256), (640, 256))
HALVES = ((2, 1), (3, 0))
VMEM_LIMIT = 56 * 1024 * 1024


def coordinates():
    c, e = lax.axis_index("ctx"), lax.axis_index("exp")
    x, y_lo = lax.rem(c, 4), c // 4
    z, y_hi, core = e // 4, lax.rem(e // 2, 2), lax.rem(e, 2)
    return c, e, x, y_hi * 2 + y_lo, z, core


def device(x, y, z, core):
    return (lax.rem(y, 2) * 4 + x, z * 4 + (y // 2) * 2 + core)


def greet(barrier, target):
    pl.semaphore_signal(
        barrier, inc=1, device_id=target, device_id_type=pl.DeviceIdType.MESH
    )


def remote(source, target_ref, send_sem, recv_sem, target):
    return pltpu.make_async_remote_copy(
        src_ref=source,
        dst_ref=target_ref,
        send_sem=send_sem,
        recv_sem=recv_sem,
        device_id=target,
        device_id_type=pl.DeviceIdType.MESH,
    )


def one_hot(wanted, columns):
    return jnp.where(
        lax.broadcasted_iota(jnp.int32, (wanted.shape[0], columns), 1) == wanted, 1.0, 0.0
    ).astype(BF16)


def row_index(count):
    return lax.broadcasted_iota(jnp.int32, (count, 1), 0)


def dot(a, b):
    return jnp.dot(a, b, preferred_element_type=F32)


def dot_t(a, b):
    return lax.dot_general(a, b, (((1,), (1,)), ((), ())), preferred_element_type=F32)


def layer_kernel(
    length_ref,
    parents_ref,
    q_ref,
    cache_ref,
    new_ref,
    ids_ref,
    gates_ref,
    wv_ref,
    wo_ref,
    residual_ref,
    gain_ref,
    gate_ref,
    up_ref,
    down_ref,
    out_ref,
    part,
    stat,
    got,
    got_stat,
    orders,
    heads,
    by_head,
    wo_cols,
    values,
    ordered,
    crossing,
    crossed,
    shares,
    from_y,
    from_z,
    squares,
    state,
    notes,
    noted,
    rows,
    sums,
    from_core,
    half_one,
    whole_one,
    half_two,
    whole_two,
    ring_sums,
    y_sums,
    x_sums,
    last,
    hidden,
    both,
    down,
    weight_sems,
    part_send,
    part_recv,
    stat_send,
    stat_recv,
    head_send,
    head_recv,
    value_send,
    value_recv,
    crossing_send,
    crossing_recv,
    y_send,
    y_recv,
    zsum_send,
    zsum_recv,
    square_send,
    square_recv,
    note_send,
    note_recv,
    z_send,
    z_recv,
    x_send,
    x_recv,
    y_row_send,
    y_row_recv,
    two_send,
    two_recv,
    relay_two_send,
    relay_two_recv,
    three_send,
    three_recv,
    relay_three_send,
    relay_three_recv,
    ring_send,
    ring_recv,
    share_send,
    share_recv,
    cross_send,
    cross_recv,
    half_one_send,
    half_one_recv,
    whole_one_send,
    whole_one_recv,
    half_two_send,
    half_two_recv,
    whole_two_send,
    whole_two_recv,
    ring_sum_send,
    ring_sum_recv,
    y_sum_send,
    y_sum_recv,
    x_sum_send,
    x_sum_recv,
    last_send,
    last_recv,
):
    c, e, x, y, z, core = coordinates()
    y_hi, y_lo = y // 2, lax.rem(y, 2)

    def plus(a, k):
        return lax.rem(a + k, 4)

    u, v = x + core * (y - x), y + core * (x - y)

    def at_xy(at_u, at_v):
        return at_u + core * (at_v - at_u), at_v + core * (at_u - at_v)

    neighbours = {
        ("u", 0): device(*at_xy(plus(u, 1), v), z, core),
        ("u", 1): device(*at_xy(plus(u, 3), v), z, core),
        ("v", 0): device(*at_xy(u, plus(v, 1)), z, core),
        ("v", 1): device(*at_xy(u, plus(v, 3)), z, core),
    }
    other_core = device(x, y, z, 1 - core)
    wide_axis, narrow_axis = ("u", "v"), ("v", "u")
    wide_at, narrow_at = (u, v), (v, u)

    barrier = pltpu.get_barrier_semaphore()
    for step in range(1, N_CTX):
        greet(barrier, (lax.rem(c + step, N_CTX), e))

    @pl.loop(1, N_EXP)
    def _(step):
        greet(barrier, (c, lax.rem(e + step, N_EXP)))

    greet(barrier, device(x, 3 - y, z, core))

    columns = pl.ds(pl.multiple_of(c * COLS, 128), COLS)
    fetches = [
        pltpu.make_async_copy(wo_ref.at[:, columns], wo_cols, weight_sems.at[0]),
        pltpu.make_async_copy(gate_ref, both.at[:, :, pl.ds(0, 128)], weight_sems.at[1]),
        pltpu.make_async_copy(up_ref, both.at[:, :, pl.ds(128, 128)], weight_sems.at[2]),
        pltpu.make_async_copy(down_ref, down, weight_sems.at[3]),
    ]
    for fetch in fetches:
        fetch.start()

    sent = []

    def taken():
        copies = list(sent)
        sent.clear()
        return copies

    def drain(copies):
        for copy in copies:
            copy.wait_send()

    def send(source, target_ref, send_sem, recv_sem, target):
        copy = remote(source, target_ref, send_sem, recv_sem, target)
        copy.start()
        sent.append(copy)

    def arrive(ref, send_sem, recv_sem, target):
        remote(ref, ref, send_sem, recv_sem, target).wait_recv()

    length = length_ref[0]
    positions = cache_ref.shape[1]
    live = (
        c * positions + lax.broadcasted_iota(jnp.int32, (1, positions), 1)
    ) < length
    wide_lane = lax.broadcasted_iota(jnp.int32, (128, 128), 1)

    def partial(target, sums_ref, stats_ref):
        scores = dot(q_ref[target], cache_ref[...]) * SCALE
        scores = jnp.where(live, scores, NEGATIVE)
        top = jnp.max(scores, axis=-1, keepdims=True)
        weights = jnp.where(live, jnp.exp(scores - top), 0.0)
        total = jnp.sum(weights, axis=-1, keepdims=True)
        sums_ref[...] = dot_t(weights.astype(BF16), cache_ref[:LAT, :]).astype(BF16)
        stats_ref[...] = jnp.where(
            wide_lane == 0, top, jnp.where(wide_lane == 1, total, 0.0)
        ).T[:8]

    def peer(flip, step):
        return lax.rem(y_lo + flip, 2) * 4 + plus(x, step)

    def send_partial(target):
        where = (target, e)
        send(part.at[target], got.at[c], part_send.at[target], part_recv.at[c], where)
        send(stat.at[target], got_stat.at[c], stat_send.at[target], stat_recv.at[c], where)

    peers = [peer(*k) for k in ((1, 2), (0, 2), (1, 1), (0, 1), (1, 3), (0, 3), (1, 0))]
    early = 4
    for target in peers[:early]:
        partial(target, part.at[target], stat.at[target])
    pl.semaphore_wait(barrier, N_CTX - 1 + N_EXP - 1 + 1)
    for target in peers[:early]:
        send_partial(target)
    for target in peers[early:]:
        partial(target, part.at[target], stat.at[target])
        send_partial(target)
    partial(c, got.at[c], got_stat.at[c])

    row = row_index(512)
    orders[0] = one_hot(
        ((row >> 2) & 3) * 128 + ((row >> 1) & 1) * HEADS + (row >> 4) * 2 + (row & 1), 512
    )
    orders[1] = one_hot(
        ((row >> 1) & 31) * 16 + ((row >> 6) & 3) * 4 + (row & 1) * 2 + (row >> 8), 512
    )
    orders[2] = one_hot(
        ((row >> 1) & 7) * 64
        + ((row >> 4) & 7) * 8
        + ((row >> 7) & 1) * 4
        + (row >> 8) * 2
        + (row & 1),
        512,
    )

    row = row_index(128)
    base = lax.rem(c, 4) * MINE
    wanted = jnp.where(
        row == 0,
        c * MINE,
        jnp.where(
            row == 1,
            c * MINE + 1,
            jnp.where(
                row == 2, parents_ref[base], jnp.where(row == 3, parents_ref[base + 1], -1)
            ),
        ),
    )
    keys = dot(one_hot(wanted, ROWS), new_ref[...]).astype(BF16)
    scores = dot_t(q_ref[c], keys) * SCALE
    second = jnp.where(row >= HEADS, 1, 0)
    tail_at = jnp.where(c >= 4, second + 2, -1)
    valid = (wide_lane == second) | (wide_lane == tail_at)
    scores = jnp.where(valid, scores, NEGATIVE)
    top = jnp.max(scores, axis=-1, keepdims=True)
    weights = jnp.where(valid, jnp.exp(scores - top), 0.0)
    own_total = jnp.sum(weights, axis=-1, keepdims=True)
    own_sum = dot(weights.astype(BF16), keys[:, :LAT])

    lane = lax.broadcasted_iota(jnp.int32, (ROWS, 128), 1)
    dense = jnp.zeros((ROWS, 128), F32)
    for k in range(8):
        dense = jnp.where(lane == ids_ref[:, k : k + 1], gates_ref[:, k : k + 1], dense)

    for source in peers:
        where = (source, e)
        arrive(got_stat.at[source], stat_send.at[source], stat_recv.at[source], where)
    stats = got_stat[...].reshape(N_CTX * 8, 128).T
    peak = top
    for source in range(N_CTX):
        peak = jnp.maximum(peak, stats[:, 8 * source : 8 * source + 1])
    factor = jnp.exp(top - peak)
    total = own_total * factor
    summed = own_sum * factor
    for source in range(N_CTX):
        factor = jnp.exp(stats[:, 8 * source : 8 * source + 1] - peak)
        total = total + stats[:, 8 * source + 1 : 8 * source + 2] * factor
    for source in peers:
        arrive(got.at[source], part_send.at[source], part_recv.at[source], (source, e))
    for source in range(N_CTX):
        factor = jnp.exp(stats[:, 8 * source : 8 * source + 1] - peak)
        summed = summed + got[source].astype(F32) * factor
    attended = (summed / total).astype(BF16)
    stacked = jnp.concatenate([attended[:, 128 * k : 128 * k + 128] for k in range(4)], axis=0)
    heads[...] = dot(orders[0], stacked).astype(BF16).reshape(N_EXP, ROWS, 128)

    def head_copy(step):
        target = lax.rem(e + step, N_EXP)
        return remote(heads.at[target], by_head.at[e], head_send, head_recv, (c, target))

    others = pl.ds(0, N_EXP - 1)
    any_peer = (c, lax.rem(e + 1, N_EXP))
    all_heads = remote(heads.at[others], by_head.at[others], head_send, head_recv, any_peer)

    @pl.loop(1, N_EXP)
    def _(step):
        head_copy(step).start()

    by_head[e] = heads[e]

    all_heads.wait_recv()
    latents = dot(orders[1], by_head[...].reshape(512, 128)).astype(BF16)
    halves = []
    for parity in range(2):
        value = jnp.zeros((64, 128), F32)
        for quarter in range(4):
            at = (parity * 4 + quarter) * 64
            value = value + dot(
                latents[at : at + 64], wv_ref[parity, 128 * quarter : 128 * quarter + 128, :]
            )
        halves.append(value.astype(BF16))
    values[c] = jnp.concatenate(halves, axis=1)

    for target in peers:
        send(values.at[c], values.at[c], value_send.at[target], value_recv.at[c], (target, e))
    for source in peers:
        arrive(values.at[source], value_send.at[source], value_recv.at[source], (source, e))
    ordered[...] = dot(orders[2], values[...].reshape(512, 256)).astype(BF16).reshape(2, 256, 256)
    fetches[0].wait()
    crossing[...] = dot(ordered[1 - core], wo_cols[...]).astype(BF16).reshape(2, 8, ROWS, COLS)
    for half in (1, 0):
        at = lax.rem(y_hi + half, 2)
        send(
            crossing.at[at],
            crossed.at[at],
            crossing_send.at[at],
            crossing_recv.at[at],
            other_core,
        )
    other_y = device(x, plus(y, 2), z, core)
    for half in (1, 0):
        at = lax.rem(y_hi + half, 2)
        own = dot(ordered[core, pl.ds(pl.multiple_of(at * 128, 128), 128)], wo_cols[...])
        arrive(crossed.at[at], crossing_send.at[at], crossing_recv.at[at], other_core)
        own = own + crossed[at].reshape(128, COLS).astype(F32)
        shares[at] = own.astype(BF16).reshape(8, ROWS, COLS)
        if half:
            for step in (4, 3, 5, 2, 6, 1, 7, 0):
                to = lax.rem(z + step, 8)
                send(shares.at[at, to], from_y.at[to], y_send.at[to], y_recv.at[to], other_y)
    for step in (4, 3, 5, 2, 6, 1, 7, 0):
        to = lax.rem(z + step, 8)
        arrive(from_y.at[to], y_send.at[to], y_recv.at[to], other_y)
        both_y = shares[y_hi, to].astype(F32) + from_y[to].astype(F32)
        if step:
            shares[y_hi, to] = both_y.astype(BF16)
            send(
                shares.at[y_hi, to],
                from_z.at[z],
                zsum_send.at[to],
                zsum_recv.at[z],
                device(x, y, to, core),
            )
    value = residual_ref[:, columns].astype(F32) + both_y
    for step in range(1, 8):
        source = lax.rem(z + step, 8)
        arrive(
            from_z.at[source],
            zsum_send.at[source],
            zsum_recv.at[source],
            device(x, y, source, core),
        )
        value = value + from_z[source].astype(F32)
    state[...] = value
    rows[c, core, y_hi, z] = (value * gain_ref[:, columns]).astype(BF16)
    squares[c] = jnp.broadcast_to(jnp.sum(value * value, axis=-1, keepdims=True), (ROWS, 128))
    for target in peers:
        send(squares.at[c], squares.at[c], square_send.at[target], square_recv.at[c], (target, e))

    def note_copy(step):
        target = lax.rem(e + step, N_EXP)
        spot = core * 16 + y_hi * 8 + z
        return remote(notes.at[target], noted.at[spot], note_send, note_recv, (c, target))

    all_notes = remote(notes.at[others], noted.at[others], note_send, note_recv, any_peer)

    def send_notes():
        for source in peers:
            arrive(squares.at[source], square_send.at[source], square_recv.at[source], (source, e))
        mean = jnp.sum(squares[...], axis=0) * (1.0 / (N_CTX * COLS))
        scale = lax.rsqrt(mean + 1e-06)
        block = jnp.concatenate([dense, scale, jnp.zeros((96, 128), F32)], axis=0).T
        notes[...] = block[:N_EXP].reshape(N_EXP, 1, 128)
        noted[core * 16 + y_hi * 8 + z] = notes[e]

        @pl.loop(1, N_EXP)
        def _(step):
            note_copy(step).start()

    def chunk(ref, part, wide, narrow, start=0, count=8):
        at_x, at_y = at_xy(wide, narrow) if part == 0 else at_xy(narrow, wide)
        first_lane, lanes = PARTS[part]
        return ref.at[
            lax.rem(at_y, 2) * 4 + at_x,
            core,
            at_y // 2,
            pl.ds(start, count),
            :,
            pl.ds(first_lane, lanes),
        ]

    def layer(ref, at_z, at_y):
        return ref.at[pl.ds(lax.rem(at_y, 2) * 4, 4), core, at_y // 2, at_z, :, pl.ds(*PARTS[2])]

    along_z = (device(x, y, lax.rem(z + 1, 8), core), device(x, y, lax.rem(z + 7, 8), core))

    def behind(side, hop):
        return lax.rem(z + (8 - hop if side == 0 else hop), 8)

    for step in (4, 3, 5, 2, 6, 1, 7):
        to = lax.rem(z + step, 8)
        block = rows.at[c, core, y_hi, z, :, pl.ds(0, PARTS[2][0])]
        send(block, block, z_send.at[to], z_recv.at[z], device(x, y, to, core))
    block = rows.at[c, core, y_hi, z, :, pl.ds(*PARTS[2])]
    for step in (2, 1, 3):
        send(
            block,
            block,
            x_send.at[step],
            x_recv.at[step],
            device(plus(x, step), y, z, core),
        )

    def share(part, wide, narrow):
        block = chunk(rows, part, wide, narrow)
        remote(block, block, share_send.at[part], share_recv.at[part], other_core).start()

    def spread(part, step):
        narrow = plus(narrow_at[part], step)
        block = chunk(rows, part, wide_at[part], narrow)
        for side in range(2):
            sem = (part, side, step)
            send(
                block,
                block,
                three_send.at[sem],
                three_recv.at[sem],
                neighbours[wide_axis[part], side],
            )
        share(part, wide_at[part], narrow)

    def spread_z(step):
        block = layer(rows, z, plus(y, step))
        for side in range(2):
            sem = (side, 0, step)
            send(block, block, ring_send.at[sem], ring_recv.at[sem], along_z[side])

    def share_z(at_z):
        block = rows.at[:, core, :, at_z, :, pl.ds(*PARTS[2])]
        remote(block, block, share_send.at[2], share_recv.at[2], other_core).start()

    for step in (1, 3, 2):
        source = plus(x, 4 - step)
        arrive(
            rows.at[y_lo * 4 + source, core, y_hi, z, :, pl.ds(*PARTS[2])],
            x_send.at[step],
            x_recv.at[step],
            device(source, y, z, core),
        )
    block = layer(rows, z, y)
    for step in (2, 1, 3):
        send(
            block,
            block,
            y_row_send.at[step],
            y_row_recv.at[step],
            device(x, plus(y, step), z, core),
        )
    spread_z(0)
    for step in range(1, 8):
        source = lax.rem(z + step, 8)
        arrive(
            rows.at[c, core, y_hi, source, :, pl.ds(0, PARTS[2][0])],
            z_send.at[source],
            z_recv.at[source],
            device(x, y, source, core),
        )
    for part in range(2):
        block = chunk(rows, part, wide_at[part], narrow_at[part])
        for side in range(2):
            send(
                block,
                block,
                two_send.at[part, side],
                two_recv.at[part, side],
                neighbours[narrow_axis[part], side],
            )
    for part in range(2):
        spread(part, 0)
    for step in (1, 3, 2):
        source = plus(y, 4 - step)
        arrive(
            layer(rows, z, source),
            y_row_send.at[step],
            y_row_recv.at[step],
            device(x, source, z, core),
        )
        spread_z(4 - step)
    share_z(z)
    for part in range(2):
        for side in range(2):
            step = 3 if side == 0 else 1
            near = plus(narrow_at[part], step)
            target = neighbours[narrow_axis[part], side]
            arrive(
                chunk(rows, part, wide_at[part], near),
                two_send.at[part, side],
                two_recv.at[part, side],
                target,
            )
            block = chunk(rows, part, wide_at[part], near, 4 * side, 4)
            send(
                block,
                block,
                relay_two_send.at[part, side],
                relay_two_recv.at[part, side],
                target,
            )
            spread(part, step)
    send_notes()

    def ring(hop):
        for step in (0, 3, 1, 2):
            for side in range(2):
                if hop == 4 and (step in (0, 3)) != (side == 0):
                    continue
                block = layer(rows, behind(side, hop), plus(y, step))
                sem = (side, hop - 1, step)
                arrive(block, ring_send.at[sem], ring_recv.at[sem], along_z[side])
                if hop < 3 or (hop == 3 and (step in (0, 3)) == (side == 0)):
                    sem = (side, hop, step)
                    send(block, block, ring_send.at[sem], ring_recv.at[sem], along_z[side])
        if hop < 4:
            for side in range(2):
                share_z(behind(side, hop))
        else:
            share_z(behind(0, 4))

    def near(step):
        for part in range(2):
            narrow = plus(narrow_at[part], step)
            for side in range(2):
                wide = plus(wide_at[part], 3 if side == 0 else 1)
                target = neighbours[wide_axis[part], side]
                sem = (part, side, step)
                block = chunk(rows, part, wide, narrow)
                arrive(block, three_send.at[sem], three_recv.at[sem], target)
                if (step in (0, 3)) == (side == 0):
                    send(
                        block,
                        block,
                        relay_three_send.at[part, step],
                        relay_three_recv.at[part, step],
                        target,
                    )
                share(part, wide, narrow)

    near(0)
    ring(1)
    for part in range(2):
        far = plus(narrow_at[part], 2)
        for side in range(2):
            arrive(
                chunk(rows, part, wide_at[part], far, 4 * side, 4),
                relay_two_send.at[part, side],
                relay_two_recv.at[part, side],
                neighbours[narrow_axis[part], side],
            )
        spread(part, 2)
    near(3)
    near(1)
    ring(2)
    near(2)
    ring(3)
    ring(4)
    for step in (0, 3, 1, 2):
        for part in range(2):
            side = 0 if step in (0, 3) else 1
            wide, narrow = plus(wide_at[part], 2), plus(narrow_at[part], step)
            arrive(
                chunk(rows, part, wide, narrow),
                relay_three_send.at[part, step],
                relay_three_recv.at[part, step],
                neighbours[wide_axis[part], side],
            )
            share(part, wide, narrow)
    shared = []
    for part in range(3):
        lanes = pl.ds(*PARTS[part])
        shared.append(
            remote(
                rows.at[:, core, :, :, :, lanes],
                rows.at[:, 1 - core, :, :, :, lanes],
                share_send.at[part],
                share_recv.at[part],
                other_core,
            )
        )
        shared[part].wait_recv()

    for fetch in fetches[1:]:
        fetch.wait()

    all_notes.wait_recv()
    note = jnp.broadcast_to(noted[...], (N_EXP, ROWS, 128)).reshape(N_EXP * ROWS, 128)
    lane = lax.broadcasted_iota(jnp.int32, (N_EXP * ROWS, 128), 1)
    beam = row_index(N_EXP * ROWS) & 15
    routed = jnp.sum(jnp.where(lane == beam, note, 0.0), axis=-1, keepdims=True)
    scale = jnp.sum(jnp.where(lane == beam + 16, note, 0.0), axis=-1, keepdims=True)
    total = jnp.zeros((512, 256), F32)
    for k in range(N_CTX):
        total = total + dot(rows[k].reshape(512, COLS), both[k])
    total = total * scale
    gate, up = total[:, :128], total[:, 128:]
    silu = gate / (1.0 + jnp.exp(-gate))
    hidden[...] = (silu * up * routed).astype(BF16).reshape(2, 256, 128)

    def add(ref, *others):
        value = ref[...].astype(F32)
        for other in others:
            value = value + other[...].astype(F32)
        ref[...] = value.astype(BF16)

    def landed(ref, part, *index):
        return ref.at[(part, *index, slice(None), slice(None), pl.ds(0, PARTS[part][1]))]

    def piece(ref, part):
        return ref.at[:, :, :, pl.ds(*PARTS[part])]

    by_x = [peer(*k) for k in ((0, 2), (1, 2), (0, 1), (0, 3), (0, 0), (1, 1), (1, 3), (1, 0))]
    by_y = [peer(*k) for k in ((0, 2), (0, 1), (0, 3), (0, 0), (1, 2), (1, 1), (1, 3), (1, 0))]

    def blocks(part, half):
        by_u, by_v = (by_x, by_y) if part == 0 else (by_y, by_x)
        return [k + half * (l - k) for k, l in zip(by_u, by_v)]

    def product(part, k, half):
        first_lane, lanes = PARTS[part]
        at = pl.ds(pl.multiple_of(k * COLS + first_lane, 128), lanes)
        return dot(hidden[half], down[:, at])

    def other(part):
        for k in blocks(part, 1 - core):
            block = piece(sums.at[k, 1 - core], part)
            block[...] = (
                product(part, k, 1 - core).astype(BF16).reshape(2, 8, ROWS, PARTS[part][1])
            )
            send(
                block,
                piece(from_core.at[k], part),
                cross_send.at[part, k],
                cross_recv.at[part, k],
                other_core,
            )

    def own(part, after):
        for number, k in enumerate(blocks(part, core)):
            value = product(part, k, core).reshape(2, 8, ROWS, PARTS[part][1])
            block = piece(from_core.at[k], part)
            arrive(block, cross_send.at[part, k], cross_recv.at[part, k], other_core)
            piece(sums.at[k, core], part)[...] = (value + block[...].astype(F32)).astype(BF16)
            if number in after:
                after[number]()

    def far_send(part):
        wide = plus(wide_at[part], 2)
        for side in range(2):
            for k in range(2):
                step = HALVES[side][k]
                sem = (part, side, k)
                send(
                    chunk(sums, part, wide, plus(narrow_at[part], step)),
                    landed(half_one, *sem),
                    half_one_send.at[sem],
                    half_one_recv.at[sem],
                    neighbours[wide_axis[part], side],
                )

    def wide_send(part, side, step):
        wide = plus(wide_at[part], 1 if side == 0 else 3)
        sem = (part, side, step)
        send(
            chunk(sums, part, wide, plus(narrow_at[part], step)),
            landed(whole_one, *sem),
            whole_one_send.at[sem],
            whole_one_recv.at[sem],
            neighbours[wide_axis[part], side],
        )

    def near_send(part):
        for k in range(2):
            for side in range(2):
                wide_send(part, side, HALVES[1 - side][k])

    def near_add(part):
        for k in range(2):
            for side in range(2):
                wide = plus(wide_at[part], 1 if side == 0 else 3)
                step = HALVES[side][k]
                sem = (part, side, k)
                block = landed(half_one, *sem)
                arrive(
                    block,
                    half_one_send.at[sem],
                    half_one_recv.at[sem],
                    neighbours[wide_axis[part], side],
                )
                add(chunk(sums, part, wide, plus(narrow_at[part], step)), block)
                wide_send(part, side, step)

    def ahead(side, hop):
        return lax.rem(z + (hop if side == 0 else 8 - hop), 8)

    def ring_send_sum(hop, side, step):
        sem = (side, hop - 1, step)
        send(
            layer(sums, ahead(side, hop), plus(y, step)),
            ring_sums.at[sem],
            ring_sum_send.at[sem],
            ring_sum_recv.at[sem],
            along_z[side],
        )

    def ring_start():
        for k in range(2):
            for side in range(2):
                ring_send_sum(4, side, HALVES[side][k])
        for k in range(2):
            for side in range(2):
                ring_send_sum(3, side, HALVES[1 - side][k])

    def ring_sum(hop):
        for step in (2, 1, 3, 0):
            for side in range(2):
                if hop == 3 and step not in HALVES[side]:
                    continue
                sem = (side, hop, step)
                arrive(
                    ring_sums.at[sem],
                    ring_sum_send.at[sem],
                    ring_sum_recv.at[sem],
                    along_z[side],
                )
                if hop:
                    add(layer(sums, ahead(side, hop), plus(y, step)), ring_sums.at[sem])
                    ring_send_sum(hop, side, step)
            if hop == 0:
                add(
                    layer(sums, z, plus(y, step)),
                    ring_sums.at[0, 0, step],
                    ring_sums.at[1, 0, step],
                )
                if step:
                    send(
                        layer(sums, z, plus(y, step)),
                        y_sums.at[step],
                        y_sum_send.at[step],
                        y_sum_recv.at[step],
                        device(x, plus(y, step), z, core),
                    )

    def narrow_send(part, side):
        near = plus(narrow_at[part], 1 if side == 0 else 3)
        sem = (part, side)
        send(
            chunk(sums, part, wide_at[part], near),
            landed(whole_two, *sem),
            whole_two_send.at[sem],
            whole_two_recv.at[sem],
            neighbours[narrow_axis[part], side],
        )

    def wide_add(part, step):
        narrow = plus(narrow_at[part], step)
        for side in range(2):
            sem = (part, side, step)
            arrive(
                landed(whole_one, *sem),
                whole_one_send.at[sem],
                whole_one_recv.at[sem],
                neighbours[wide_axis[part], side],
            )
        add(
            chunk(sums, part, wide_at[part], narrow),
            landed(whole_one, part, 0, step),
            landed(whole_one, part, 1, step),
        )
        if step == 2:
            for side in range(2):
                sem = (part, side)
                send(
                    chunk(sums, part, wide_at[part], narrow, 4 * side, 4),
                    landed(half_two, *sem),
                    half_two_send.at[sem],
                    half_two_recv.at[sem],
                    neighbours[narrow_axis[part], side],
                )

    def narrow_add(part):
        for side in range(2):
            near = plus(narrow_at[part], 1 if side == 0 else 3)
            sem = (part, side)
            arrive(
                landed(half_two, *sem),
                half_two_send.at[sem],
                half_two_recv.at[sem],
                neighbours[narrow_axis[part], side],
            )
            add(
                chunk(sums, part, wide_at[part], near, 4 * side, 4), landed(half_two, *sem)
            )
            narrow_send(part, side)

    def narrow_end(part):
        for side in range(2):
            sem = (part, side)
            arrive(
                landed(whole_two, *sem),
                whole_two_send.at[sem],
                whole_two_recv.at[sem],
                neighbours[narrow_axis[part], side],
            )
        add(
            chunk(sums, part, wide_at[part], narrow_at[part]),
            landed(whole_two, part, 0),
            landed(whole_two, part, 1),
        )
        for step in (4, 3, 5, 2, 6, 1, 7):
            to = lax.rem(z + step, 8)
            send(
                sums.at[c, core, y_hi, to, :, pl.ds(*PARTS[part])],
                last.at[z, :, pl.ds(*PARTS[part])],
                last_send.at[part, to],
                last_recv.at[part, z],
                device(x, y, to, core),
            )

    earlier = taken()
    other(0)
    own(0, {3: lambda: far_send(0)})
    near_send(0)
    other(2)
    own(2, {})
    ring_start()
    other(1)
    near_add(0)
    own(1, {3: lambda: far_send(1)})
    near_send(1)
    ring_sum(3)
    near_add(1)
    ring_sum(2)
    drain(earlier)
    all_heads.wait_send()
    all_notes.wait_send()
    for copy in shared:
        copy.wait_send()
    wide_add(0, 2)
    ring_sum(1)
    wide_add(1, 2)
    for step in (1, 3):
        for part in range(2):
            wide_add(part, step)
    ring_sum(0)
    narrow_add(0)
    narrow_add(1)
    for part in range(2):
        wide_add(part, 0)
    for step in (2, 1, 3):
        arrive(
            y_sums.at[step],
            y_sum_send.at[step],
            y_sum_recv.at[step],
            device(x, plus(y, 4 - step), z, core),
        )
    add(layer(sums, z, y), *(y_sums.at[step] for step in (1, 2, 3)))
    for step in (2, 1, 3):
        send(
            sums.at[y_lo * 4 + plus(x, step), core, y_hi, z, :, pl.ds(*PARTS[2])],
            x_sums.at[step],
            x_sum_send.at[step],
            x_sum_recv.at[step],
            device(plus(x, step), y, z, core),
        )
    earlier = taken()
    narrow_end(0)
    narrow_end(1)
    drain(earlier)
    for step in (1, 3, 2):
        arrive(
            x_sums.at[step],
            x_sum_send.at[step],
            x_sum_recv.at[step],
            device(plus(x, 4 - step), y, z, core),
        )

    def finish(part, value):
        lanes = pl.ds(*PARTS[part])
        value = value + state[:, lanes] + sums[c, core, y_hi, z, :, lanes].astype(F32)
        out_ref[:, lanes] = value.astype(BF16)

    finish(2, sum(x_sums[step].astype(F32) for step in (1, 2, 3)))
    for part in range(2):
        value = jnp.zeros((ROWS, PARTS[part][1]), F32)
        for step in range(1, 8):
            source = lax.rem(z + step, 8)
            block = last.at[source, :, pl.ds(*PARTS[part])]
            arrive(
                block,
                last_send.at[part, source],
                last_recv.at[part, source],
                device(x, y, source, core),
            )
            value = value + block[...].astype(F32)
        finish(part, value)

    drain(sent)


VMEM = pl.BlockSpec(memory_space=pltpu.VMEM)
SMEM = pl.BlockSpec(memory_space=pltpu.SMEM)
ANY = pl.BlockSpec(memory_space=pl.ANY)
DMA = pltpu.SemaphoreType.DMA


def per_device(
    queries,
    prompt_cache,
    new_latent,
    parents,
    lengths,
    value_weight,
    output_weight,
    residual,
    norm_gain,
    expert_ids,
    expert_weights,
    expert_gate,
    expert_up,
    expert_down,
):
    key_width = queries.shape[3]
    pairs = [(N_CTX,), (N_CTX,), None, (N_CTX,), (2,), (8,), (8,), (N_CTX,), None]
    pairs += [(8,), (4,), (4,), (2, 2), (2, 2), (2, 2, 4), (2, 4), (2, 4, 4), (3,)]
    pairs += [(3, 8), (2, 2, 2), (2, 2, 4), (2, 2), (2, 2), (2, 4, 4), (4,), (4,), (2, 8)]
    out = pl.pallas_call(
        layer_kernel,
        out_shape=jax.ShapeDtypeStruct((ROWS, COLS), BF16),
        in_specs=[SMEM, SMEM] + [VMEM] * 6 + [ANY, VMEM, VMEM, ANY, ANY, ANY],
        out_specs=VMEM,
        scratch_shapes=[
            pltpu.VMEM((N_CTX, 128, LAT), BF16),
            pltpu.VMEM((N_CTX, 8, 128), F32),
            pltpu.VMEM((N_CTX, 128, LAT), BF16),
            pltpu.VMEM((N_CTX, 8, 128), F32),
            pltpu.VMEM((3, 512, 512), BF16),
            pltpu.VMEM((N_EXP, ROWS, 128), BF16),
            pltpu.VMEM((N_EXP, ROWS, 128), BF16),
            pltpu.VMEM((256, COLS), BF16),
            pltpu.VMEM((N_CTX, 64, 256), BF16),
            pltpu.VMEM((2, 256, 256), BF16),
            pltpu.VMEM((2, 8, ROWS, COLS), BF16),
            pltpu.VMEM((2, 8, ROWS, COLS), BF16),
            pltpu.VMEM((2, 8, ROWS, COLS), BF16),
            pltpu.VMEM((8, ROWS, COLS), BF16),
            pltpu.VMEM((8, ROWS, COLS), BF16),
            pltpu.VMEM((N_CTX, ROWS, 128), F32),
            pltpu.VMEM((ROWS, COLS), F32),
            pltpu.VMEM((N_EXP, 1, 128), F32),
            pltpu.VMEM((N_EXP, 1, 128), F32),
            pltpu.VMEM((N_CTX, 2, 2, 8, ROWS, COLS), BF16),
            pltpu.VMEM((N_CTX, 2, 2, 8, ROWS, COLS), BF16),
            pltpu.VMEM((N_CTX, 2, 8, ROWS, COLS), BF16),
            pltpu.VMEM((2, 2, 2, 8, ROWS, 384), BF16),
            pltpu.VMEM((2, 2, 4, 8, ROWS, 384), BF16),
            pltpu.VMEM((2, 2, 4, ROWS, 384), BF16),
            pltpu.VMEM((2, 2, 8, ROWS, 384), BF16),
            pltpu.VMEM((2, 4, 4, 4, ROWS, 256), BF16),
            pltpu.VMEM((4, 4, ROWS, 256), BF16),
            pltpu.VMEM((4, ROWS, 256), BF16),
            pltpu.VMEM((8, ROWS, COLS), BF16),
            pltpu.VMEM((2, 256, 128), BF16),
            pltpu.VMEM((N_CTX, COLS, 256), BF16),
            pltpu.VMEM((128, N_CTX * COLS), BF16),
            DMA((4,)),
        ]
        + [DMA(shape) if shape else DMA for shape in pairs for _ in range(2)],
        compiler_params=pltpu.CompilerParams(
            collective_id=0, has_side_effects=True, vmem_limit_bytes=VMEM_LIMIT
        ),
        name="layer",
    )(
        lengths,
        parents.reshape(8),
        queries.reshape(N_CTX, 128, key_width),
        prompt_cache[0].T,
        new_latent.reshape(ROWS, key_width),
        expert_ids.reshape(ROWS, 8),
        expert_weights.reshape(ROWS, 8),
        value_weight,
        output_weight,
        residual.reshape(ROWS, N_CTX * COLS),
        norm_gain.reshape(1, N_CTX * COLS),
        expert_gate.reshape(N_CTX, COLS, 128),
        expert_up.reshape(N_CTX, COLS, 128),
        expert_down[0],
    )
    return out.reshape(2, 8, COLS)


def solution(mesh):
    in_specs = (
        P(None, "exp", None, None),
        P("exp", "ctx", None),
        P(None, "exp", None),
        P("exp", None),
        P("exp"),
        P("exp", None, None),
        P("exp", None),
        P(None, "exp", None),
        P(),
        P(None, "exp", None),
        P(None, "exp", None),
        P("exp", None, "ctx"),
        P("exp", None, "ctx"),
        P("exp", "ctx", None),
    )
    out_specs = P(None, "exp", "ctx")
    return jax.shard_map(
        per_device, mesh=mesh, in_specs=in_specs, out_specs=out_specs, check_vma=False
    )
```

```python
import functools

import jax
import jax.numpy as jnp
from jax import lax
from jax.experimental import pallas as pl
from jax.experimental.pallas import tpu as pltpu
from jax.sharding import PartitionSpec as P

SCALE = 0.07216878364870322
NEGATIVE = -1e30
BF16 = jnp.bfloat16
F32 = jnp.float32
N_CTX = 8
N_EXP = 32
ROWS = 16
MINE = 2
HEADS = 64
LAT = 512
COLS = 896
PARTS = ((0, 384), (384, 256), (640, 256))
HALVES = ((2, 1), (3, 0))
VMEM_LIMIT = 56 * 1024 * 1024


def coordinates():
    c, e = lax.axis_index("ctx"), lax.axis_index("exp")
    x, y_lo = lax.rem(c, 4), c // 4
    z, y_hi, core = e // 4, lax.rem(e // 2, 2), lax.rem(e, 2)
    return c, e, x, y_hi * 2 + y_lo, z, core


def device(x, y, z, core):
    return (lax.rem(y, 2) * 4 + x, z * 4 + (y // 2) * 2 + core)


def greet(barrier, target):
    pl.semaphore_signal(
        barrier, inc=1, device_id=target, device_id_type=pl.DeviceIdType.MESH
    )


def remote(source, target_ref, send_sem, recv_sem, target):
    return pltpu.make_async_remote_copy(
        src_ref=source,
        dst_ref=target_ref,
        send_sem=send_sem,
        recv_sem=recv_sem,
        device_id=target,
        device_id_type=pl.DeviceIdType.MESH,
    )


def one_hot(wanted, columns):
    return jnp.where(
        lax.broadcasted_iota(jnp.int32, (wanted.shape[0], columns), 1) == wanted, 1.0, 0.0
    ).astype(BF16)


def row_index(count):
    return lax.broadcasted_iota(jnp.int32, (count, 1), 0)


def dot(a, b):
    return jnp.dot(a, b, preferred_element_type=F32)


def dot_t(a, b):
    return lax.dot_general(a, b, (((1,), (1,)), ((), ())), preferred_element_type=F32)


def layer_kernel(
    length_ref,
    parents_ref,
    q_hbm,
    cache_hbm,
    new_ref,
    ids_ref,
    gates_ref,
    wv_hbm,
    wo_ref,
    residual_hbm,
    gain_ref,
    gate_ref,
    up_ref,
    down_ref,
    out_ref,
    q_ref,
    cache_ref,
    wv_ref,
    residual_ref,
    wo_other,
    part,
    stat,
    got,
    got_stat,
    orders,
    heads,
    by_head,
    wo_cols,
    values,
    ordered,
    met,
    shares,
    from_y,
    from_z,
    squares,
    state,
    notes,
    noted,
    rows,
    sums,
    half_one,
    whole_one,
    half_two,
    whole_two,
    ring_sums,
    y_sums,
    x_sums,
    last,
    scales,
    crossing_hidden,
    hidden,
    both,
    down,
    input_sems,
    weight_sems,
    part_send,
    part_recv,
    stat_send,
    stat_recv,
    head_send,
    head_recv,
    value_send,
    value_recv,
    crossing_send,
    crossing_recv,
    y_send,
    y_recv,
    zsum_send,
    zsum_recv,
    square_send,
    square_recv,
    note_send,
    note_recv,
    z_send,
    z_recv,
    x_send,
    x_recv,
    y_row_send,
    y_row_recv,
    two_send,
    two_recv,
    relay_two_send,
    relay_two_recv,
    three_send,
    three_recv,
    relay_three_send,
    relay_three_recv,
    ring_send,
    ring_recv,
    share_send,
    share_recv,
    pair_send,
    pair_recv,
    hidden_send,
    hidden_recv,
    half_one_send,
    half_one_recv,
    whole_one_send,
    whole_one_recv,
    half_two_send,
    half_two_recv,
    whole_two_send,
    whole_two_recv,
    ring_sum_send,
    ring_sum_recv,
    y_sum_send,
    y_sum_recv,
    x_sum_send,
    x_sum_recv,
    last_send,
    last_recv,
):
    c, e, x, y, z, core = coordinates()
    y_hi, y_lo = y // 2, lax.rem(y, 2)

    def plus(a, k):
        return lax.rem(a + k, 4)

    u, v = x + core * (y - x), y + core * (x - y)

    def at_xy(at_u, at_v):
        return at_u + core * (at_v - at_u), at_v + core * (at_u - at_v)

    neighbours = {
        ("u", 0): device(*at_xy(plus(u, 1), v), z, core),
        ("u", 1): device(*at_xy(plus(u, 3), v), z, core),
        ("v", 0): device(*at_xy(u, plus(v, 1)), z, core),
        ("v", 1): device(*at_xy(u, plus(v, 3)), z, core),
    }
    other_core = device(x, y, z, 1 - core)
    wide_axis, narrow_axis = ("u", "v"), ("v", "u")
    wide_at, narrow_at = (u, v), (v, u)

    inputs = [
        pltpu.make_async_copy(cache_hbm, cache_ref, input_sems.at[0]),
        pltpu.make_async_copy(q_hbm, q_ref, input_sems.at[1]),
    ]
    for fetch in inputs:
        fetch.start()
    barrier = pltpu.get_barrier_semaphore()
    for step in range(1, N_CTX):
        greet(barrier, (lax.rem(c + step, N_CTX), e))

    @pl.loop(1, N_EXP)
    def _(step):
        greet(barrier, (c, lax.rem(e + step, N_EXP)))

    greet(barrier, device(x, 3 - y, z, core))

    columns = pl.ds(pl.multiple_of(c * COLS, 128), COLS)
    fetches = [
        pltpu.make_async_copy(wo_ref.at[:, columns], wo_cols, weight_sems.at[0]),
        pltpu.make_async_copy(gate_ref, both.at[:, :, pl.ds(0, 128)], weight_sems.at[1]),
        pltpu.make_async_copy(up_ref, both.at[:, :, pl.ds(128, 128)], weight_sems.at[2]),
        pltpu.make_async_copy(
            down_ref, down.at[pl.ds(pl.multiple_of(core * 128, 128), 128)], weight_sems.at[3]
        ),
        pltpu.make_async_copy(wv_hbm, wv_ref, weight_sems.at[4]),
        pltpu.make_async_copy(residual_hbm.at[:, columns], residual_ref, weight_sems.at[5]),
    ]
    for fetch in fetches:
        fetch.start()

    sent = []

    def taken():
        copies = list(sent)
        sent.clear()
        return copies

    def drain(copies):
        for copy in copies:
            copy.wait_send()

    def send(source, target_ref, send_sem, recv_sem, target):
        copy = remote(source, target_ref, send_sem, recv_sem, target)
        copy.start()
        sent.append(copy)

    def arrive(ref, send_sem, recv_sem, target):
        remote(ref, ref, send_sem, recv_sem, target).wait_recv()

    length = length_ref[0]
    positions = cache_ref.shape[1]
    live = (
        c * positions + lax.broadcasted_iota(jnp.int32, (1, positions), 1)
    ) < length
    wide_lane = lax.broadcasted_iota(jnp.int32, (128, 128), 1)

    def partial(target, sums_ref, stats_ref):
        scores = dot(q_ref[target], cache_ref[...]) * SCALE
        scores = jnp.where(live, scores, NEGATIVE)
        top = jnp.max(scores, axis=-1, keepdims=True)
        weights = jnp.where(live, jnp.exp(scores - top), 0.0)
        total = jnp.sum(weights, axis=-1, keepdims=True)
        sums_ref[...] = dot_t(weights.astype(BF16), cache_ref[:LAT, :]).astype(BF16)
        stats_ref[...] = jnp.where(
            wide_lane == 0, top, jnp.where(wide_lane == 1, total, 0.0)
        ).T[:8]

    def peer(flip, step):
        return lax.rem(y_lo + flip, 2) * 4 + plus(x, step)

    def send_partial(target):
        where = (target, e)
        send(part.at[target], got.at[c], part_send.at[target], part_recv.at[c], where)
        send(stat.at[target], got_stat.at[c], stat_send.at[target], stat_recv.at[c], where)

    peers = [peer(*k) for k in ((1, 2), (0, 2), (1, 1), (0, 1), (1, 3), (0, 3), (1, 0))]
    for fetch in inputs:
        fetch.wait()
    early = 4
    for target in peers[:early]:
        partial(target, part.at[target], stat.at[target])
    pl.semaphore_wait(barrier, N_CTX - 1 + N_EXP - 1 + 1)
    for target in peers[:early]:
        send_partial(target)
    for target in peers[early:]:
        partial(target, part.at[target], stat.at[target])
        send_partial(target)
    send(wo_ref.at[:, columns], wo_other, pair_send.at[0], pair_recv.at[0], other_core)
    own_down = down.at[pl.ds(pl.multiple_of(core * 128, 128), 128)]
    send(down_ref, own_down, pair_send.at[1], pair_recv.at[1], other_core)
    partial(c, got.at[c], got_stat.at[c])

    row = row_index(512)
    orders[0] = one_hot(
        ((row >> 2) & 3) * 128 + ((row >> 1) & 1) * HEADS + (row >> 4) * 2 + (row & 1), 512
    )
    orders[1] = one_hot(
        ((row >> 1) & 31) * 16 + ((row >> 6) & 3) * 4 + (row & 1) * 2 + (row >> 8), 512
    )
    orders[2] = one_hot(
        ((row >> 1) & 7) * 64
        + ((row >> 4) & 7) * 8
        + ((row >> 7) & 1) * 4
        + (row >> 8) * 2
        + (row & 1),
        512,
    )

    row = row_index(128)
    base = lax.rem(c, 4) * MINE
    wanted = jnp.where(
        row == 0,
        c * MINE,
        jnp.where(
            row == 1,
            c * MINE + 1,
            jnp.where(
                row == 2, parents_ref[base], jnp.where(row == 3, parents_ref[base + 1], -1)
            ),
        ),
    )
    keys = dot(one_hot(wanted, ROWS), new_ref[...]).astype(BF16)
    scores = dot_t(q_ref[c], keys) * SCALE
    second = jnp.where(row >= HEADS, 1, 0)
    tail_at = jnp.where(c >= 4, second + 2, -1)
    valid = (wide_lane == second) | (wide_lane == tail_at)
    scores = jnp.where(valid, scores, NEGATIVE)
    top = jnp.max(scores, axis=-1, keepdims=True)
    weights = jnp.where(valid, jnp.exp(scores - top), 0.0)
    own_total = jnp.sum(weights, axis=-1, keepdims=True)
    own_sum = dot(weights.astype(BF16), keys[:, :LAT])

    lane = lax.broadcasted_iota(jnp.int32, (ROWS, 128), 1)
    dense = jnp.zeros((ROWS, 128), F32)
    for k in range(8):
        dense = jnp.where(lane == ids_ref[:, k : k + 1], gates_ref[:, k : k + 1], dense)

    for source in peers:
        where = (source, e)
        arrive(got_stat.at[source], stat_send.at[source], stat_recv.at[source], where)
    stats = got_stat[...].reshape(N_CTX * 8, 128).T
    peak = top
    for source in range(N_CTX):
        peak = jnp.maximum(peak, stats[:, 8 * source : 8 * source + 1])
    factor = jnp.exp(top - peak)
    total = own_total * factor
    summed = own_sum * factor
    for source in range(N_CTX):
        factor = jnp.exp(stats[:, 8 * source : 8 * source + 1] - peak)
        total = total + stats[:, 8 * source + 1 : 8 * source + 2] * factor
    for source in peers:
        arrive(got.at[source], part_send.at[source], part_recv.at[source], (source, e))
    for source in range(N_CTX):
        factor = jnp.exp(stats[:, 8 * source : 8 * source + 1] - peak)
        summed = summed + got[source].astype(F32) * factor
    attended = (summed / total).astype(BF16)
    stacked = jnp.concatenate([attended[:, 128 * k : 128 * k + 128] for k in range(4)], axis=0)
    heads[...] = dot(orders[0], stacked).astype(BF16).reshape(N_EXP, ROWS, 128)

    def head_copy(step):
        target = lax.rem(e + step, N_EXP)
        return remote(heads.at[target], by_head.at[e], head_send, head_recv, (c, target))

    others = pl.ds(0, N_EXP - 1)
    any_peer = (c, lax.rem(e + 1, N_EXP))
    all_heads = remote(heads.at[others], by_head.at[others], head_send, head_recv, any_peer)

    @pl.loop(1, N_EXP)
    def _(step):
        head_copy(step).start()

    by_head[e] = heads[e]

    all_heads.wait_recv()
    fetches[4].wait()
    latents = dot(orders[1], by_head[...].reshape(512, 128)).astype(BF16)
    halves = []
    for parity in range(2):
        value = jnp.zeros((64, 128), F32)
        for quarter in range(4):
            at = (parity * 4 + quarter) * 64
            value = value + dot(
                latents[at : at + 64], wv_ref[parity, 128 * quarter : 128 * quarter + 128, :]
            )
        halves.append(value.astype(BF16))
    values[c] = jnp.concatenate(halves, axis=1)

    for target in peers:
        send(values.at[c], values.at[c], value_send.at[target], value_recv.at[c], (target, e))
    for source in peers:
        arrive(values.at[source], value_send.at[source], value_recv.at[source], (source, e))
    ordered[...] = dot(orders[2], values[...].reshape(512, 256)).astype(BF16).reshape(2, 256, 256)
    send(ordered.at[1 - core], met, crossing_send, crossing_recv, other_core)
    fetches[0].wait()
    arrive(wo_other, pair_send.at[0], pair_recv.at[0], other_core)
    other_y = device(x, plus(y, 2), z, core)
    for half in (1, 0):
        at = lax.rem(y_hi + half, 2)
        near_rows = pl.ds(pl.multiple_of(at * 128, 128), 128)
        own = dot(ordered[core, near_rows], wo_cols[...])
        if half:
            arrive(met, crossing_send, crossing_recv, other_core)
        own = own + dot(met[near_rows], wo_other[...])
        shares[at] = own.astype(BF16).reshape(8, ROWS, COLS)
        if half:
            for step in (4, 3, 5, 2, 6, 1, 7, 0):
                to = lax.rem(z + step, 8)
                send(shares.at[at, to], from_y.at[to], y_send.at[to], y_recv.at[to], other_y)
    for step in (4, 3, 5, 2, 6, 1, 7, 0):
        to = lax.rem(z + step, 8)
        arrive(from_y.at[to], y_send.at[to], y_recv.at[to], other_y)
        both_y = shares[y_hi, to].astype(F32) + from_y[to].astype(F32)
        if step:
            shares[y_hi, to] = both_y.astype(BF16)
            send(
                shares.at[y_hi, to],
                from_z.at[z],
                zsum_send.at[to],
                zsum_recv.at[z],
                device(x, y, to, core),
            )
    fetches[5].wait()
    value = residual_ref[...].astype(F32) + both_y
    for step in range(1, 8):
        source = lax.rem(z + step, 8)
        arrive(
            from_z.at[source],
            zsum_send.at[source],
            zsum_recv.at[source],
            device(x, y, source, core),
        )
        value = value + from_z[source].astype(F32)
    state[...] = value
    rows[c, core, y_hi, z] = (value * gain_ref[:, columns]).astype(BF16)
    squares[c] = jnp.broadcast_to(jnp.sum(value * value, axis=-1, keepdims=True), (ROWS, 128))
    for target in peers:
        send(squares.at[c], squares.at[c], square_send.at[target], square_recv.at[c], (target, e))

    def note_copy(step):
        target = lax.rem(e + step, N_EXP)
        spot = core * 16 + y_hi * 8 + z
        return remote(notes.at[target], noted.at[spot], note_send, note_recv, (c, target))

    all_notes = remote(notes.at[others], noted.at[others], note_send, note_recv, any_peer)

    def send_notes():
        for source in peers:
            arrive(squares.at[source], square_send.at[source], square_recv.at[source], (source, e))
        mean = jnp.sum(squares[...], axis=0) * (1.0 / (N_CTX * COLS))
        scale = lax.rsqrt(mean + 1e-06)
        block = jnp.concatenate([dense, scale, jnp.zeros((96, 128), F32)], axis=0).T
        notes[...] = block[:N_EXP].reshape(N_EXP, 1, 128)
        noted[core * 16 + y_hi * 8 + z] = notes[e]

        @pl.loop(1, N_EXP)
        def _(step):
            note_copy(step).start()

    def chunk(ref, part, wide, narrow, start=0, count=8):
        at_x, at_y = at_xy(wide, narrow) if part == 0 else at_xy(narrow, wide)
        first_lane, lanes = PARTS[part]
        at = (lax.rem(at_y, 2) * 4 + at_x,) + ((core,) if ref is rows else ())
        return ref.at[at + (at_y // 2, pl.ds(start, count), slice(None), pl.ds(first_lane, lanes))]

    def layer(ref, at_z, at_y):
        at = (pl.ds(lax.rem(at_y, 2) * 4, 4),) + ((core,) if ref is rows else ())
        return ref.at[at + (at_y // 2, at_z, slice(None), pl.ds(*PARTS[2]))]

    along_z = (device(x, y, lax.rem(z + 1, 8), core), device(x, y, lax.rem(z + 7, 8), core))

    def behind(side, hop):
        return lax.rem(z + (8 - hop if side == 0 else hop), 8)

    for step in (4, 3, 5, 2, 6, 1, 7):
        to = lax.rem(z + step, 8)
        block = rows.at[c, core, y_hi, z, :, pl.ds(0, PARTS[2][0])]
        send(block, block, z_send.at[to], z_recv.at[z], device(x, y, to, core))
    block = rows.at[c, core, y_hi, z, :, pl.ds(*PARTS[2])]
    for step in (2, 1, 3):
        send(
            block,
            block,
            x_send.at[step],
            x_recv.at[step],
            device(plus(x, step), y, z, core),
        )

    def share(part, wide, narrow):
        block = chunk(rows, part, wide, narrow)
        remote(block, block, share_send.at[part], share_recv.at[part], other_core).start()

    def spread(part, step):
        narrow = plus(narrow_at[part], step)
        block = chunk(rows, part, wide_at[part], narrow)
        for side in range(2):
            sem = (part, side, step)
            send(
                block,
                block,
                three_send.at[sem],
                three_recv.at[sem],
                neighbours[wide_axis[part], side],
            )
        share(part, wide_at[part], narrow)

    def spread_z(step):
        block = layer(rows, z, plus(y, step))
        for side in range(2):
            sem = (side, 0, step)
            send(block, block, ring_send.at[sem], ring_recv.at[sem], along_z[side])

    def share_z(at_z):
        block = rows.at[:, core, :, at_z, :, pl.ds(*PARTS[2])]
        remote(block, block, share_send.at[2], share_recv.at[2], other_core).start()

    for step in (1, 3, 2):
        source = plus(x, 4 - step)
        arrive(
            rows.at[y_lo * 4 + source, core, y_hi, z, :, pl.ds(*PARTS[2])],
            x_send.at[step],
            x_recv.at[step],
            device(source, y, z, core),
        )
    block = layer(rows, z, y)
    for step in (2, 1, 3):
        send(
            block,
            block,
            y_row_send.at[step],
            y_row_recv.at[step],
            device(x, plus(y, step), z, core),
        )
    spread_z(0)
    for step in range(1, 8):
        source = lax.rem(z + step, 8)
        arrive(
            rows.at[c, core, y_hi, source, :, pl.ds(0, PARTS[2][0])],
            z_send.at[source],
            z_recv.at[source],
            device(x, y, source, core),
        )
    for part in range(2):
        block = chunk(rows, part, wide_at[part], narrow_at[part])
        for side in range(2):
            send(
                block,
                block,
                two_send.at[part, side],
                two_recv.at[part, side],
                neighbours[narrow_axis[part], side],
            )
    for part in range(2):
        spread(part, 0)
    for step in (1, 3, 2):
        source = plus(y, 4 - step)
        arrive(
            layer(rows, z, source),
            y_row_send.at[step],
            y_row_recv.at[step],
            device(x, source, z, core),
        )
        spread_z(4 - step)
    share_z(z)
    for part in range(2):
        for side in range(2):
            step = 3 if side == 0 else 1
            near = plus(narrow_at[part], step)
            target = neighbours[narrow_axis[part], side]
            arrive(
                chunk(rows, part, wide_at[part], near),
                two_send.at[part, side],
                two_recv.at[part, side],
                target,
            )
            block = chunk(rows, part, wide_at[part], near, 4 * side, 4)
            send(
                block,
                block,
                relay_two_send.at[part, side],
                relay_two_recv.at[part, side],
                target,
            )
            spread(part, step)
    send_notes()

    def ring(hop):
        for step in (0, 3, 1, 2):
            for side in range(2):
                if hop == 4 and (step in (0, 3)) != (side == 0):
                    continue
                block = layer(rows, behind(side, hop), plus(y, step))
                sem = (side, hop - 1, step)
                arrive(block, ring_send.at[sem], ring_recv.at[sem], along_z[side])
                if hop < 3 or (hop == 3 and (step in (0, 3)) == (side == 0)):
                    sem = (side, hop, step)
                    send(block, block, ring_send.at[sem], ring_recv.at[sem], along_z[side])
        if hop < 4:
            for side in range(2):
                share_z(behind(side, hop))
        else:
            share_z(behind(0, 4))

    def near(step):
        for part in range(2):
            narrow = plus(narrow_at[part], step)
            for side in range(2):
                wide = plus(wide_at[part], 3 if side == 0 else 1)
                target = neighbours[wide_axis[part], side]
                sem = (part, side, step)
                block = chunk(rows, part, wide, narrow)
                arrive(block, three_send.at[sem], three_recv.at[sem], target)
                if (step in (0, 3)) == (side == 0):
                    send(
                        block,
                        block,
                        relay_three_send.at[part, step],
                        relay_three_recv.at[part, step],
                        target,
                    )
                share(part, wide, narrow)

    near(0)
    ring(1)
    for part in range(2):
        far = plus(narrow_at[part], 2)
        for side in range(2):
            arrive(
                chunk(rows, part, wide_at[part], far, 4 * side, 4),
                relay_two_send.at[part, side],
                relay_two_recv.at[part, side],
                neighbours[narrow_axis[part], side],
            )
        spread(part, 2)
    near(3)
    near(1)
    ring(2)
    near(2)
    ring(3)
    ring(4)
    for step in (0, 3, 1, 2):
        for part in range(2):
            side = 0 if step in (0, 3) else 1
            wide, narrow = plus(wide_at[part], 2), plus(narrow_at[part], step)
            arrive(
                chunk(rows, part, wide, narrow),
                relay_three_send.at[part, step],
                relay_three_recv.at[part, step],
                neighbours[wide_axis[part], side],
            )
            share(part, wide, narrow)
    shared = []
    for part in range(3):
        lanes = pl.ds(*PARTS[part])
        shared.append(
            remote(
                rows.at[:, core, :, :, :, lanes],
                rows.at[:, 1 - core, :, :, :, lanes],
                share_send.at[part],
                share_recv.at[part],
                other_core,
            )
        )
        shared[part].wait_recv()

    for fetch in fetches[1:4]:
        fetch.wait()

    all_notes.wait_recv()
    note = jnp.broadcast_to(noted[...], (N_EXP, ROWS, 128)).reshape(N_EXP * ROWS, 128)
    lane = lax.broadcasted_iota(jnp.int32, (N_EXP * ROWS, 128), 1)
    beam = row_index(N_EXP * ROWS) & 15
    routed = jnp.sum(jnp.where(lane == beam, note, 0.0), axis=-1, keepdims=True)
    scale = jnp.sum(jnp.where(lane == beam + 16, note, 0.0), axis=-1, keepdims=True)
    def hide(half):
        total = jnp.zeros((256, 256), F32)
        for k in range(N_CTX):
            total = total + dot(rows[k, half].reshape(256, COLS), both[k])
        rows_at = pl.ds(pl.multiple_of(half * 256, 256), 256)
        total = total * scales[rows_at, :1]
        gate, up = total[:, :128], total[:, 128:]
        silu = gate / (1.0 + jnp.exp(-gate))
        return (silu * up * scales[rows_at, 1:2]).astype(BF16)

    def lanes_of(half):
        return pl.ds(pl.multiple_of(half * 128, 128), 128)

    scales[...] = jnp.where(lane == 0, scale, routed)
    crossing_hidden[...] = hide(1 - core)
    send(
        crossing_hidden,
        hidden.at[:, lanes_of(core)],
        hidden_send,
        hidden_recv,
        other_core,
    )
    hidden[:, lanes_of(core)] = hide(core)
    other_lanes = hidden.at[:, lanes_of(1 - core)]
    arrive(other_lanes, hidden_send, hidden_recv, other_core)
    other_down = down.at[pl.ds(pl.multiple_of((1 - core) * 128, 128), 128)]
    arrive(other_down, pair_send.at[1], pair_recv.at[1], other_core)

    def add(ref, *others):
        value = ref[...].astype(F32)
        for other in others:
            value = value + other[...].astype(F32)
        ref[...] = value.astype(BF16)

    def landed(ref, part, *index):
        return ref.at[(part, *index, slice(None), slice(None), pl.ds(0, PARTS[part][1]))]

    def piece(ref, part):
        return ref.at[:, :, :, pl.ds(*PARTS[part])]

    by_x = [peer(*k) for k in ((0, 2), (1, 2), (0, 1), (0, 3), (0, 0), (1, 1), (1, 3), (1, 0))]
    by_y = [peer(*k) for k in ((0, 2), (0, 1), (0, 3), (0, 0), (1, 2), (1, 1), (1, 3), (1, 0))]

    def blocks(part):
        by_u, by_v = (by_x, by_y) if part == 0 else (by_y, by_x)
        return [k + core * (l - k) for k, l in zip(by_u, by_v)]

    def product(part, k):
        first_lane, lanes = PARTS[part]
        at = pl.ds(pl.multiple_of(k * COLS + first_lane, 128), lanes)
        return dot(hidden[...], down[:, at]).astype(BF16).reshape(2, 8, ROWS, lanes)

    def own(part, after):
        for number, k in enumerate(blocks(part)):
            piece(sums.at[k], part)[...] = product(part, k)
            if number in after:
                after[number]()

    def far_send(part):
        wide = plus(wide_at[part], 2)
        for side in range(2):
            for k in range(2):
                step = HALVES[side][k]
                sem = (part, side, k)
                send(
                    chunk(sums, part, wide, plus(narrow_at[part], step)),
                    landed(half_one, *sem),
                    half_one_send.at[sem],
                    half_one_recv.at[sem],
                    neighbours[wide_axis[part], side],
                )

    def wide_send(part, side, step):
        wide = plus(wide_at[part], 1 if side == 0 else 3)
        sem = (part, side, step)
        send(
            chunk(sums, part, wide, plus(narrow_at[part], step)),
            landed(whole_one, *sem),
            whole_one_send.at[sem],
            whole_one_recv.at[sem],
            neighbours[wide_axis[part], side],
        )

    def near_send(part):
        for k in range(2):
            for side in range(2):
                wide_send(part, side, HALVES[1 - side][k])

    def near_add(part):
        for k in range(2):
            for side in range(2):
                wide = plus(wide_at[part], 1 if side == 0 else 3)
                step = HALVES[side][k]
                sem = (part, side, k)
                block = landed(half_one, *sem)
                arrive(
                    block,
                    half_one_send.at[sem],
                    half_one_recv.at[sem],
                    neighbours[wide_axis[part], side],
                )
                add(chunk(sums, part, wide, plus(narrow_at[part], step)), block)
                wide_send(part, side, step)

    def ahead(side, hop):
        return lax.rem(z + (hop if side == 0 else 8 - hop), 8)

    def ring_send_sum(hop, side, step):
        sem = (side, hop - 1, step)
        send(
            layer(sums, ahead(side, hop), plus(y, step)),
            ring_sums.at[sem],
            ring_sum_send.at[sem],
            ring_sum_recv.at[sem],
            along_z[side],
        )

    def ring_start():
        for k in range(2):
            for side in range(2):
                ring_send_sum(4, side, HALVES[side][k])
        for k in range(2):
            for side in range(2):
                ring_send_sum(3, side, HALVES[1 - side][k])

    def ring_sum(hop):
        for step in (2, 1, 3, 0):
            for side in range(2):
                if hop == 3 and step not in HALVES[side]:
                    continue
                sem = (side, hop, step)
                arrive(
                    ring_sums.at[sem],
                    ring_sum_send.at[sem],
                    ring_sum_recv.at[sem],
                    along_z[side],
                )
                if hop:
                    add(layer(sums, ahead(side, hop), plus(y, step)), ring_sums.at[sem])
                    ring_send_sum(hop, side, step)
            if hop == 0:
                add(
                    layer(sums, z, plus(y, step)),
                    ring_sums.at[0, 0, step],
                    ring_sums.at[1, 0, step],
                )
                if step:
                    send(
                        layer(sums, z, plus(y, step)),
                        y_sums.at[step],
                        y_sum_send.at[step],
                        y_sum_recv.at[step],
                        device(x, plus(y, step), z, core),
                    )

    def narrow_send(part, side):
        near = plus(narrow_at[part], 1 if side == 0 else 3)
        sem = (part, side)
        send(
            chunk(sums, part, wide_at[part], near),
            landed(whole_two, *sem),
            whole_two_send.at[sem],
            whole_two_recv.at[sem],
            neighbours[narrow_axis[part], side],
        )

    def wide_add(part, step):
        narrow = plus(narrow_at[part], step)
        for side in range(2):
            sem = (part, side, step)
            arrive(
                landed(whole_one, *sem),
                whole_one_send.at[sem],
                whole_one_recv.at[sem],
                neighbours[wide_axis[part], side],
            )
        add(
            chunk(sums, part, wide_at[part], narrow),
            landed(whole_one, part, 0, step),
            landed(whole_one, part, 1, step),
        )
        if step == 2:
            for side in range(2):
                sem = (part, side)
                send(
                    chunk(sums, part, wide_at[part], narrow, 4 * side, 4),
                    landed(half_two, *sem),
                    half_two_send.at[sem],
                    half_two_recv.at[sem],
                    neighbours[narrow_axis[part], side],
                )

    def narrow_add(part):
        for side in range(2):
            near = plus(narrow_at[part], 1 if side == 0 else 3)
            sem = (part, side)
            arrive(
                landed(half_two, *sem),
                half_two_send.at[sem],
                half_two_recv.at[sem],
                neighbours[narrow_axis[part], side],
            )
            add(
                chunk(sums, part, wide_at[part], near, 4 * side, 4), landed(half_two, *sem)
            )
            narrow_send(part, side)

    def narrow_end(part):
        for side in range(2):
            sem = (part, side)
            arrive(
                landed(whole_two, *sem),
                whole_two_send.at[sem],
                whole_two_recv.at[sem],
                neighbours[narrow_axis[part], side],
            )
        add(
            chunk(sums, part, wide_at[part], narrow_at[part]),
            landed(whole_two, part, 0),
            landed(whole_two, part, 1),
        )
        for step in (4, 3, 5, 2, 6, 1, 7):
            to = lax.rem(z + step, 8)
            send(
                sums.at[c, y_hi, to, :, pl.ds(*PARTS[part])],
                last.at[z, :, pl.ds(*PARTS[part])],
                last_send.at[part, to],
                last_recv.at[part, z],
                device(x, y, to, core),
            )

    earlier = taken()
    own(0, {3: lambda: far_send(0)})
    near_send(0)
    own(2, {})
    ring_start()
    own(1, {3: lambda: far_send(1)})
    near_send(1)
    near_add(0)
    ring_sum(3)
    near_add(1)
    ring_sum(2)
    drain(earlier)
    all_heads.wait_send()
    all_notes.wait_send()
    for copy in shared:
        copy.wait_send()
    wide_add(0, 2)
    ring_sum(1)
    wide_add(1, 2)
    for step in (1, 3):
        for part in range(2):
            wide_add(part, step)
    narrow_add(0)
    narrow_add(1)
    ring_sum(0)
    for part in range(2):
        wide_add(part, 0)
    for step in (2, 1, 3):
        arrive(
            y_sums.at[step],
            y_sum_send.at[step],
            y_sum_recv.at[step],
            device(x, plus(y, 4 - step), z, core),
        )
    add(layer(sums, z, y), *(y_sums.at[step] for step in (1, 2, 3)))
    for step in (2, 1, 3):
        send(
            sums.at[y_lo * 4 + plus(x, step), y_hi, z, :, pl.ds(*PARTS[2])],
            x_sums.at[step],
            x_sum_send.at[step],
            x_sum_recv.at[step],
            device(plus(x, step), y, z, core),
        )
    earlier = taken()
    narrow_end(0)
    narrow_end(1)
    drain(earlier)
    for step in (1, 3, 2):
        arrive(
            x_sums.at[step],
            x_sum_send.at[step],
            x_sum_recv.at[step],
            device(plus(x, 4 - step), y, z, core),
        )

    def finish(part, value):
        lanes = pl.ds(*PARTS[part])
        value = value + state[:, lanes] + sums[c, y_hi, z, :, lanes].astype(F32)
        out_ref[:, lanes] = value.astype(BF16)

    finish(2, sum(x_sums[step].astype(F32) for step in (1, 2, 3)))
    for part in range(2):
        value = jnp.zeros((ROWS, PARTS[part][1]), F32)
        for step in range(1, 8):
            source = lax.rem(z + step, 8)
            block = last.at[source, :, pl.ds(*PARTS[part])]
            arrive(
                block,
                last_send.at[part, source],
                last_recv.at[part, source],
                device(x, y, source, core),
            )
            value = value + block[...].astype(F32)
        finish(part, value)

    drain(sent)


VMEM = pl.BlockSpec(memory_space=pltpu.VMEM)
SMEM = pl.BlockSpec(memory_space=pltpu.SMEM)
ANY = pl.BlockSpec(memory_space=pl.ANY)
DMA = pltpu.SemaphoreType.DMA


def per_device(
    queries,
    prompt_cache,
    new_latent,
    parents,
    lengths,
    value_weight,
    output_weight,
    residual,
    norm_gain,
    expert_ids,
    expert_weights,
    expert_gate,
    expert_up,
    expert_down,
):
    key_width = queries.shape[3]
    pairs = [(N_CTX,), (N_CTX,), None, (N_CTX,), None, (8,), (8,), (N_CTX,), None]
    pairs += [(8,), (4,), (4,), (2, 2), (2, 2), (2, 2, 4), (2, 4), (2, 4, 4), (3,)]
    pairs += [(2,), None, (2, 2, 2), (2, 2, 4), (2, 2), (2, 2), (2, 4, 4), (4,), (4,), (2, 8)]
    out = pl.pallas_call(
        layer_kernel,
        out_shape=jax.ShapeDtypeStruct((ROWS, COLS), BF16),
        in_specs=[SMEM, SMEM, ANY, ANY, VMEM, VMEM, VMEM, ANY, ANY, ANY, VMEM, ANY, ANY, ANY],
        out_specs=VMEM,
        scratch_shapes=[
            pltpu.VMEM((N_CTX, 128, key_width), BF16),
            pltpu.VMEM((key_width, prompt_cache.shape[1]), BF16),
            pltpu.VMEM(value_weight.shape, BF16),
            pltpu.VMEM((ROWS, COLS), BF16),
            pltpu.VMEM((256, COLS), BF16),
            pltpu.VMEM((N_CTX, 128, LAT), BF16),
            pltpu.VMEM((N_CTX, 8, 128), F32),
            pltpu.VMEM((N_CTX, 128, LAT), BF16),
            pltpu.VMEM((N_CTX, 8, 128), F32),
            pltpu.VMEM((3, 512, 512), BF16),
            pltpu.VMEM((N_EXP, ROWS, 128), BF16),
            pltpu.VMEM((N_EXP, ROWS, 128), BF16),
            pltpu.VMEM((256, COLS), BF16),
            pltpu.VMEM((N_CTX, 64, 256), BF16),
            pltpu.VMEM((2, 256, 256), BF16),
            pltpu.VMEM((256, 256), BF16),
            pltpu.VMEM((2, 8, ROWS, COLS), BF16),
            pltpu.VMEM((8, ROWS, COLS), BF16),
            pltpu.VMEM((8, ROWS, COLS), BF16),
            pltpu.VMEM((N_CTX, ROWS, 128), F32),
            pltpu.VMEM((ROWS, COLS), F32),
            pltpu.VMEM((N_EXP, 1, 128), F32),
            pltpu.VMEM((N_EXP, 1, 128), F32),
            pltpu.VMEM((N_CTX, 2, 2, 8, ROWS, COLS), BF16),
            pltpu.VMEM((N_CTX, 2, 8, ROWS, COLS), BF16),
            pltpu.VMEM((2, 2, 2, 8, ROWS, 384), BF16),
            pltpu.VMEM((2, 2, 4, 8, ROWS, 384), BF16),
            pltpu.VMEM((2, 2, 4, ROWS, 384), BF16),
            pltpu.VMEM((2, 2, 8, ROWS, 384), BF16),
            pltpu.VMEM((2, 4, 4, 4, ROWS, 256), BF16),
            pltpu.VMEM((4, 4, ROWS, 256), BF16),
            pltpu.VMEM((4, ROWS, 256), BF16),
            pltpu.VMEM((8, ROWS, COLS), BF16),
            pltpu.VMEM((512, 128), F32),
            pltpu.VMEM((256, 128), BF16),
            pltpu.VMEM((256, 256), BF16),
            pltpu.VMEM((N_CTX, COLS, 256), BF16),
            pltpu.VMEM((256, N_CTX * COLS), BF16),
            DMA((2,)),
            DMA((6,)),
        ]
        + [DMA(shape) if shape else DMA for shape in pairs for _ in range(2)],
        compiler_params=pltpu.CompilerParams(
            collective_id=0, has_side_effects=True, vmem_limit_bytes=VMEM_LIMIT
        ),
        name="layer",
    )(
        lengths,
        parents.reshape(8),
        queries.reshape(N_CTX, 128, key_width),
        prompt_cache[0].T,
        new_latent.reshape(ROWS, key_width),
        expert_ids.reshape(ROWS, 8),
        expert_weights.reshape(ROWS, 8),
        value_weight,
        output_weight,
        residual.reshape(ROWS, N_CTX * COLS),
        norm_gain.reshape(1, N_CTX * COLS),
        expert_gate.reshape(N_CTX, COLS, 128),
        expert_up.reshape(N_CTX, COLS, 128),
        expert_down[0],
    )
    return out.reshape(2, 8, COLS)


def solution(mesh):
    in_specs = (
        P(None, "exp", None, None),
        P("exp", "ctx", None),
        P(None, "exp", None),
        P("exp", None),
        P("exp"),
        P("exp", None, None),
        P("exp", None),
        P(None, "exp", None),
        P(),
        P(None, "exp", None),
        P(None, "exp", None),
        P("exp", None, "ctx"),
        P("exp", None, "ctx"),
        P("exp", "ctx", None),
    )
    out_specs = P(None, "exp", "ctx")
    return jax.shard_map(
        per_device, mesh=mesh, in_specs=in_specs, out_specs=out_specs, check_vma=False
    )
```

```python
import functools

import jax
import jax.numpy as jnp
from jax import lax
from jax.experimental import pallas as pl
from jax.experimental.pallas import tpu as pltpu
from jax.sharding import PartitionSpec as P

SCALE = 0.07216878364870322
NEGATIVE = -1e30
BF16 = jnp.bfloat16
F32 = jnp.float32
N_CTX = 8
N_EXP = 32
ROWS = 16
MINE = 2
HEADS = 64
LAT = 512
COLS = 896
PARTS = ((0, 384), (384, 256), (640, 256))
HALVES = ((2, 1), (3, 0))
VMEM_LIMIT = 56 * 1024 * 1024


def coordinates():
    c, e = lax.axis_index("ctx"), lax.axis_index("exp")
    x, y_lo = lax.rem(c, 4), c // 4
    z, y_hi, core = e // 4, lax.rem(e // 2, 2), lax.rem(e, 2)
    return c, e, x, y_hi * 2 + y_lo, z, core


def device(x, y, z, core):
    return (lax.rem(y, 2) * 4 + x, z * 4 + (y // 2) * 2 + core)


def greet(barrier, target):
    pl.semaphore_signal(
        barrier, inc=1, device_id=target, device_id_type=pl.DeviceIdType.MESH
    )


def remote(source, target_ref, send_sem, recv_sem, target):
    return pltpu.make_async_remote_copy(
        src_ref=source,
        dst_ref=target_ref,
        send_sem=send_sem,
        recv_sem=recv_sem,
        device_id=target,
        device_id_type=pl.DeviceIdType.MESH,
    )


def one_hot(wanted, columns):
    return jnp.where(
        lax.broadcasted_iota(jnp.int32, (wanted.shape[0], columns), 1) == wanted, 1.0, 0.0
    ).astype(BF16)


def row_index(count):
    return lax.broadcasted_iota(jnp.int32, (count, 1), 0)


def dot(a, b):
    return jnp.dot(a, b, preferred_element_type=F32)


def dot_t(a, b):
    return lax.dot_general(a, b, (((1,), (1,)), ((), ())), preferred_element_type=F32)


def layer_kernel(
    length_ref,
    parents_ref,
    q_hbm,
    cache_hbm,
    new_ref,
    ids_ref,
    gates_ref,
    wv_hbm,
    wo_ref,
    residual_hbm,
    gain_ref,
    gate_ref,
    up_ref,
    down_ref,
    out_ref,
    q_ref,
    cache_ref,
    wv_ref,
    residual_ref,
    wo_other,
    part,
    stat,
    got,
    got_stat,
    orders,
    heads,
    by_head,
    wo_cols,
    values,
    ordered,
    met,
    shares,
    from_y,
    from_z,
    squares,
    state,
    notes,
    noted,
    rows,
    sums,
    half_one,
    whole_one,
    whole_two,
    ring_sums,
    xy_sums,
    last,
    scales,
    crossing_hidden,
    hidden,
    both,
    down,
    input_sems,
    weight_sems,
    part_send,
    part_recv,
    stat_send,
    stat_recv,
    head_send,
    head_recv,
    value_send,
    value_recv,
    crossing_send,
    crossing_recv,
    y_send,
    y_recv,
    zsum_send,
    zsum_recv,
    square_send,
    square_recv,
    note_send,
    note_recv,
    z_send,
    z_recv,
    xy_send,
    xy_recv,
    two_send,
    two_recv,
    three_send,
    three_recv,
    relay_three_send,
    relay_three_recv,
    ring_send,
    ring_recv,
    share_send,
    share_recv,
    pair_send,
    pair_recv,
    hidden_send,
    hidden_recv,
    half_one_send,
    half_one_recv,
    whole_one_send,
    whole_one_recv,
    whole_two_send,
    whole_two_recv,
    ring_sum_send,
    ring_sum_recv,
    xy_sum_send,
    xy_sum_recv,
    last_send,
    last_recv,
):
    c, e, x, y, z, core = coordinates()
    y_hi, y_lo = y // 2, lax.rem(y, 2)

    def plus(a, k):
        return lax.rem(a + k, 4)

    u, v = x + core * (y - x), y + core * (x - y)

    def at_xy(at_u, at_v):
        return at_u + core * (at_v - at_u), at_v + core * (at_u - at_v)

    neighbours = {
        ("u", 0): device(*at_xy(plus(u, 1), v), z, core),
        ("u", 1): device(*at_xy(plus(u, 3), v), z, core),
        ("v", 0): device(*at_xy(u, plus(v, 1)), z, core),
        ("v", 1): device(*at_xy(u, plus(v, 3)), z, core),
        ("u", 2): device(*at_xy(plus(u, 2), v), z, core),
        ("v", 2): device(*at_xy(u, plus(v, 2)), z, core),
    }
    other_core = device(x, y, z, 1 - core)
    wide_axis, narrow_axis = ("u", "v"), ("v", "u")
    wide_at, narrow_at = (u, v), (v, u)

    inputs = [
        pltpu.make_async_copy(cache_hbm, cache_ref, input_sems.at[0]),
        pltpu.make_async_copy(q_hbm, q_ref, input_sems.at[1]),
    ]
    for fetch in inputs:
        fetch.start()
    barrier = pltpu.get_barrier_semaphore()
    for step in range(1, N_CTX):
        greet(barrier, (lax.rem(c + step, N_CTX), e))

    @pl.loop(1, N_EXP)
    def _(step):
        greet(barrier, (c, lax.rem(e + step, N_EXP)))

    for step in range(1, N_CTX):
        greet(barrier, (lax.rem(c + step, N_CTX), e + 2 - 4 * y_hi))

    columns = pl.ds(pl.multiple_of(c * COLS, 128), COLS)
    fetches = [
        pltpu.make_async_copy(wo_ref.at[:, columns], wo_cols, weight_sems.at[0]),
        pltpu.make_async_copy(gate_ref, both.at[:, :, pl.ds(0, 128)], weight_sems.at[1]),
        pltpu.make_async_copy(up_ref, both.at[:, :, pl.ds(128, 128)], weight_sems.at[2]),
        pltpu.make_async_copy(
            down_ref, down.at[pl.ds(pl.multiple_of(core * 128, 128), 128)], weight_sems.at[3]
        ),
        pltpu.make_async_copy(wv_hbm, wv_ref, weight_sems.at[4]),
        pltpu.make_async_copy(residual_hbm.at[:, columns], residual_ref, weight_sems.at[5]),
    ]
    for fetch in fetches:
        fetch.start()

    sent = []

    def taken():
        copies = list(sent)
        sent.clear()
        return copies

    def drain(copies):
        for copy in copies:
            copy.wait_send()

    def send(source, target_ref, send_sem, recv_sem, target):
        copy = remote(source, target_ref, send_sem, recv_sem, target)
        copy.start()
        sent.append(copy)

    def arrive(ref, send_sem, recv_sem, target):
        remote(ref, ref, send_sem, recv_sem, target).wait_recv()

    length = length_ref[0]
    positions = cache_ref.shape[1]
    live = (
        c * positions + lax.broadcasted_iota(jnp.int32, (1, positions), 1)
    ) < length
    wide_lane = lax.broadcasted_iota(jnp.int32, (128, 128), 1)

    def partial(target, sums_ref, stats_ref):
        scores = dot(q_ref[target], cache_ref[...]) * SCALE
        scores = jnp.where(live, scores, NEGATIVE)
        top = jnp.max(scores, axis=-1, keepdims=True)
        weights = jnp.where(live, jnp.exp(scores - top), 0.0)
        total = jnp.sum(weights, axis=-1, keepdims=True)
        sums_ref[...] = dot_t(weights.astype(BF16), cache_ref[:LAT, :]).astype(BF16)
        stats_ref[...] = jnp.where(
            wide_lane == 0, top, jnp.where(wide_lane == 1, total, 0.0)
        ).T[:8]

    def peer(flip, step):
        return lax.rem(y_lo + flip, 2) * 4 + plus(x, step)

    def send_partial(target):
        where = (target, e)
        send(part.at[target], got.at[c], part_send.at[target], part_recv.at[c], where)
        send(stat.at[target], got_stat.at[c], stat_send.at[target], stat_recv.at[c], where)

    peers = [peer(*k) for k in ((1, 2), (0, 2), (1, 1), (0, 1), (1, 3), (0, 3), (1, 0))]
    for fetch in inputs:
        fetch.wait()
    early = 4
    for target in peers[:early]:
        partial(target, part.at[target], stat.at[target])
    pl.semaphore_wait(barrier, 2 * (N_CTX - 1) + N_EXP - 1)
    for target in peers[:early]:
        send_partial(target)
    for target in peers[early:]:
        partial(target, part.at[target], stat.at[target])
        send_partial(target)
    send(wo_ref.at[:, columns], wo_other, pair_send.at[0], pair_recv.at[0], other_core)
    own_down = down.at[pl.ds(pl.multiple_of(core * 128, 128), 128)]
    send(down_ref, own_down, pair_send.at[1], pair_recv.at[1], other_core)
    partial(c, got.at[c], got_stat.at[c])

    row = row_index(512)
    orders[0] = one_hot(
        ((row >> 2) & 3) * 128 + ((row >> 1) & 1) * HEADS + (row >> 4) * 2 + (row & 1), 512
    )
    orders[1] = one_hot(
        ((row >> 1) & 31) * 16 + ((row >> 6) & 3) * 4 + (row & 1) * 2 + (row >> 8), 512
    )
    orders[2] = one_hot(
        ((row >> 1) & 7) * 64
        + ((row >> 4) & 7) * 8
        + ((row >> 7) & 1) * 4
        + (row >> 8) * 2
        + (row & 1),
        512,
    )

    row = row_index(128)
    base = lax.rem(c, 4) * MINE
    wanted = jnp.where(
        row == 0,
        c * MINE,
        jnp.where(
            row == 1,
            c * MINE + 1,
            jnp.where(
                row == 2, parents_ref[base], jnp.where(row == 3, parents_ref[base + 1], -1)
            ),
        ),
    )
    keys = dot(one_hot(wanted, ROWS), new_ref[...]).astype(BF16)
    scores = dot_t(q_ref[c], keys) * SCALE
    second = jnp.where(row >= HEADS, 1, 0)
    tail_at = jnp.where(c >= 4, second + 2, -1)
    valid = (wide_lane == second) | (wide_lane == tail_at)
    scores = jnp.where(valid, scores, NEGATIVE)
    top = jnp.max(scores, axis=-1, keepdims=True)
    weights = jnp.where(valid, jnp.exp(scores - top), 0.0)
    own_total = jnp.sum(weights, axis=-1, keepdims=True)
    own_sum = dot(weights.astype(BF16), keys[:, :LAT])

    lane = lax.broadcasted_iota(jnp.int32, (ROWS, 128), 1)
    dense = jnp.zeros((ROWS, 128), F32)
    for k in range(8):
        dense = jnp.where(lane == ids_ref[:, k : k + 1], gates_ref[:, k : k + 1], dense)

    for source in peers:
        where = (source, e)
        arrive(got_stat.at[source], stat_send.at[source], stat_recv.at[source], where)
    stats = got_stat[...].reshape(N_CTX * 8, 128).T
    peak = top
    for source in range(N_CTX):
        peak = jnp.maximum(peak, stats[:, 8 * source : 8 * source + 1])
    factor = jnp.exp(top - peak)
    total = own_total * factor
    summed = own_sum * factor
    for source in range(N_CTX):
        factor = jnp.exp(stats[:, 8 * source : 8 * source + 1] - peak)
        total = total + stats[:, 8 * source + 1 : 8 * source + 2] * factor
    for source in peers:
        arrive(got.at[source], part_send.at[source], part_recv.at[source], (source, e))
    for source in range(N_CTX):
        factor = jnp.exp(stats[:, 8 * source : 8 * source + 1] - peak)
        summed = summed + got[source].astype(F32) * factor
    attended = (summed / total).astype(BF16)
    stacked = jnp.concatenate([attended[:, 128 * k : 128 * k + 128] for k in range(4)], axis=0)
    heads[...] = dot(orders[0], stacked).astype(BF16).reshape(N_EXP, ROWS, 128)

    def head_copy(step):
        target = lax.rem(e + step, N_EXP)
        return remote(heads.at[target], by_head.at[e], head_send, head_recv, (c, target))

    others = pl.ds(0, N_EXP - 1)
    any_peer = (c, lax.rem(e + 1, N_EXP))
    all_heads = remote(heads.at[others], by_head.at[others], head_send, head_recv, any_peer)

    @pl.loop(1, N_EXP)
    def _(step):
        head_copy(step).start()

    by_head[e] = heads[e]

    all_heads.wait_recv()
    fetches[4].wait()
    latents = dot(orders[1], by_head[...].reshape(512, 128)).astype(BF16)
    halves = []
    for parity in range(2):
        value = jnp.zeros((64, 128), F32)
        for quarter in range(4):
            at = (parity * 4 + quarter) * 64
            value = value + dot(
                latents[at : at + 64], wv_ref[parity, 128 * quarter : 128 * quarter + 128, :]
            )
        halves.append(value.astype(BF16))
    values[c] = jnp.concatenate(halves, axis=1)

    for target in peers:
        send(values.at[c], values.at[c], value_send.at[target], value_recv.at[c], (target, e))
    for source in peers:
        arrive(values.at[source], value_send.at[source], value_recv.at[source], (source, e))
    ordered[...] = dot(orders[2], values[...].reshape(512, 256)).astype(BF16).reshape(2, 256, 256)
    send(ordered.at[1 - core], met, crossing_send, crossing_recv, other_core)
    fetches[0].wait()
    arrive(wo_other, pair_send.at[0], pair_recv.at[0], other_core)
    other_y = device(x, plus(y, 2), z, core)
    for half in (1, 0):
        at = lax.rem(y_hi + half, 2)
        near_rows = pl.ds(pl.multiple_of(at * 128, 128), 128)
        own = dot(ordered[core, near_rows], wo_cols[...])
        if half:
            arrive(met, crossing_send, crossing_recv, other_core)
        own = own + dot(met[near_rows], wo_other[...])
        shares[at] = own.astype(BF16).reshape(8, ROWS, COLS)
        if half:
            for step in (4, 3, 5, 2, 6, 1, 7, 0):
                to = lax.rem(z + step, 8)
                send(shares.at[at, to], from_y.at[to], y_send.at[to], y_recv.at[to], other_y)
    for step in (4, 3, 5, 2, 6, 1, 7, 0):
        to = lax.rem(z + step, 8)
        arrive(from_y.at[to], y_send.at[to], y_recv.at[to], other_y)
        both_y = shares[y_hi, to].astype(F32) + from_y[to].astype(F32)
        if step:
            shares[y_hi, to] = both_y.astype(BF16)
            send(
                shares.at[y_hi, to],
                from_z.at[z],
                zsum_send.at[to],
                zsum_recv.at[z],
                device(x, y, to, core),
            )
    fetches[5].wait()
    value = residual_ref[...].astype(F32) + both_y
    for step in range(1, 8):
        source = lax.rem(z + step, 8)
        arrive(
            from_z.at[source],
            zsum_send.at[source],
            zsum_recv.at[source],
            device(x, y, source, core),
        )
        value = value + from_z[source].astype(F32)
    state[...] = value
    rows[c, core, y_hi, z] = (value * gain_ref[:, columns]).astype(BF16)
    squares[c] = jnp.broadcast_to(jnp.sum(value * value, axis=-1, keepdims=True), (ROWS, 128))
    for target in peers:
        send(squares.at[c], squares.at[c], square_send.at[target], square_recv.at[c], (target, e))

    def note_copy(step):
        target = lax.rem(e + step, N_EXP)
        spot = core * 16 + y_hi * 8 + z
        return remote(notes.at[target], noted.at[spot], note_send, note_recv, (c, target))

    all_notes = remote(notes.at[others], noted.at[others], note_send, note_recv, any_peer)

    def send_notes():
        for source in peers:
            arrive(squares.at[source], square_send.at[source], square_recv.at[source], (source, e))
        mean = jnp.sum(squares[...], axis=0) * (1.0 / (N_CTX * COLS))
        scale = lax.rsqrt(mean + 1e-06)
        block = jnp.concatenate([dense, scale, jnp.zeros((96, 128), F32)], axis=0).T
        notes[...] = block[:N_EXP].reshape(N_EXP, 1, 128)
        noted[core * 16 + y_hi * 8 + z] = notes[e]

        @pl.loop(1, N_EXP)
        def _(step):
            note_copy(step).start()

    def chunk(ref, part, wide, narrow, start=0, count=8):
        at_x, at_y = at_xy(wide, narrow) if part == 0 else at_xy(narrow, wide)
        first_lane, lanes = PARTS[part]
        at = (lax.rem(at_y, 2) * 4 + at_x,) + ((core,) if ref is rows else ())
        return ref.at[at + (at_y // 2, pl.ds(start, count), slice(None), pl.ds(first_lane, lanes))]

    def layer(ref, at_z, at_y):
        at = (pl.ds(lax.rem(at_y, 2) * 4, 4),) + ((core,) if ref is rows else ())
        return ref.at[at + (at_y // 2, at_z, slice(None), pl.ds(*PARTS[2]))]

    along_z = (device(x, y, lax.rem(z + 1, 8), core), device(x, y, lax.rem(z + 7, 8), core))

    def behind(side, hop):
        return lax.rem(z + (8 - hop if side == 0 else hop), 8)

    for step in (4, 3, 5, 2, 6, 1, 7):
        to = lax.rem(z + step, 8)
        block = rows.at[c, core, y_hi, z, :, pl.ds(0, PARTS[2][0])]
        send(block, block, z_send.at[to], z_recv.at[z], device(x, y, to, core))
    block = rows.at[c, core, y_hi, z, :, pl.ds(*PARTS[2])]
    for dy in range(4):
        for dx in range(4):
            if dx or dy:
                send(
                    block,
                    block,
                    xy_send.at[4 * dy + dx],
                    xy_recv.at[4 * dy + dx],
                    device(plus(x, dx), plus(y, dy), z, core),
                )

    def share(part, wide, narrow):
        block = chunk(rows, part, wide, narrow)
        remote(block, block, share_send.at[part], share_recv.at[part], other_core).start()

    def spread(part, step):
        narrow = plus(narrow_at[part], step)
        block = chunk(rows, part, wide_at[part], narrow)
        for side in range(2):
            sem = (part, side, step)
            send(
                block,
                block,
                three_send.at[sem],
                three_recv.at[sem],
                neighbours[wide_axis[part], side],
            )
        share(part, wide_at[part], narrow)

    def spread_z(step):
        block = layer(rows, z, plus(y, step))
        for side in range(2):
            sem = (side, 0, step)
            send(block, block, ring_send.at[sem], ring_recv.at[sem], along_z[side])

    def share_z(at_z):
        block = rows.at[:, core, :, at_z, :, pl.ds(*PARTS[2])]
        remote(block, block, share_send.at[2], share_recv.at[2], other_core).start()

    def arrive_plane(dy):
        for dx in range(4):
            if dx or dy:
                at_x, at_y = plus(x, 4 - dx), plus(y, 4 - dy)
                arrive(
                    rows.at[
                        lax.rem(at_y, 2) * 4 + at_x, core, at_y // 2, z, :, pl.ds(*PARTS[2])
                    ],
                    xy_send.at[4 * dy + dx],
                    xy_recv.at[4 * dy + dx],
                    device(at_x, at_y, z, core),
                )

    arrive_plane(0)
    spread_z(0)
    for step in range(1, 8):
        source = lax.rem(z + step, 8)
        arrive(
            rows.at[c, core, y_hi, source, :, pl.ds(0, PARTS[2][0])],
            z_send.at[source],
            z_recv.at[source],
            device(x, y, source, core),
        )
    for part in range(2):
        block = chunk(rows, part, wide_at[part], narrow_at[part])
        for side in range(3):
            send(
                block,
                block,
                two_send.at[part, side],
                two_recv.at[part, side],
                neighbours[narrow_axis[part], side],
            )
    for part in range(2):
        spread(part, 0)
    for dy in (1, 3, 2):
        arrive_plane(dy)
        spread_z(4 - dy)
    share_z(z)

    def arrive_narrow(side):
        step = (3, 1, 2)[side]
        for part in range(2):
            arrive(
                chunk(rows, part, wide_at[part], plus(narrow_at[part], step)),
                two_send.at[part, side],
                two_recv.at[part, side],
                neighbours[narrow_axis[part], side],
            )
            spread(part, step)

    arrive_narrow(0)
    arrive_narrow(1)
    send_notes()

    def ring(hop):
        for step in (0, 3, 1, 2):
            for side in range(2):
                if hop == 4 and (step in (0, 3)) != (side == 0):
                    continue
                block = layer(rows, behind(side, hop), plus(y, step))
                sem = (side, hop - 1, step)
                arrive(block, ring_send.at[sem], ring_recv.at[sem], along_z[side])
                if hop < 3 or (hop == 3 and (step in (0, 3)) == (side == 0)):
                    sem = (side, hop, step)
                    send(block, block, ring_send.at[sem], ring_recv.at[sem], along_z[side])
        if hop < 4:
            for side in range(2):
                share_z(behind(side, hop))
        else:
            share_z(behind(0, 4))

    def near(step):
        for part in range(2):
            narrow = plus(narrow_at[part], step)
            for side in range(2):
                wide = plus(wide_at[part], 3 if side == 0 else 1)
                target = neighbours[wide_axis[part], side]
                sem = (part, side, step)
                block = chunk(rows, part, wide, narrow)
                arrive(block, three_send.at[sem], three_recv.at[sem], target)
                if (step in (0, 3)) == (side == 0):
                    send(
                        block,
                        block,
                        relay_three_send.at[part, step],
                        relay_three_recv.at[part, step],
                        target,
                    )
                share(part, wide, narrow)

    near(0)
    ring(1)
    arrive_narrow(2)
    near(3)
    near(1)
    ring(2)
    near(2)
    ring(3)
    ring(4)
    for step in (0, 3, 1, 2):
        for part in range(2):
            side = 0 if step in (0, 3) else 1
            wide, narrow = plus(wide_at[part], 2), plus(narrow_at[part], step)
            arrive(
                chunk(rows, part, wide, narrow),
                relay_three_send.at[part, step],
                relay_three_recv.at[part, step],
                neighbours[wide_axis[part], side],
            )
            share(part, wide, narrow)
    shared = []
    for part in range(3):
        lanes = pl.ds(*PARTS[part])
        shared.append(
            remote(
                rows.at[:, core, :, :, :, lanes],
                rows.at[:, 1 - core, :, :, :, lanes],
                share_send.at[part],
                share_recv.at[part],
                other_core,
            )
        )
        shared[part].wait_recv()

    for fetch in fetches[1:4]:
        fetch.wait()

    all_notes.wait_recv()
    note = jnp.broadcast_to(noted[...], (N_EXP, ROWS, 128)).reshape(N_EXP * ROWS, 128)
    lane = lax.broadcasted_iota(jnp.int32, (N_EXP * ROWS, 128), 1)
    beam = row_index(N_EXP * ROWS) & 15
    routed = jnp.sum(jnp.where(lane == beam, note, 0.0), axis=-1, keepdims=True)
    scale = jnp.sum(jnp.where(lane == beam + 16, note, 0.0), axis=-1, keepdims=True)
    def hide(half):
        total = jnp.zeros((256, 256), F32)
        for k in range(N_CTX):
            total = total + dot(rows[k, half].reshape(256, COLS), both[k])
        rows_at = pl.ds(pl.multiple_of(half * 256, 256), 256)
        total = total * scales[rows_at, :1]
        gate, up = total[:, :128], total[:, 128:]
        silu = gate / (1.0 + jnp.exp(-gate))
        return (silu * up * scales[rows_at, 1:2]).astype(BF16)

    def lanes_of(half):
        return pl.ds(pl.multiple_of(half * 128, 128), 128)

    scales[...] = jnp.where(lane == 0, scale, routed)
    crossing_hidden[...] = hide(1 - core)
    send(
        crossing_hidden,
        hidden.at[:, lanes_of(core)],
        hidden_send,
        hidden_recv,
        other_core,
    )
    hidden[:, lanes_of(core)] = hide(core)
    other_lanes = hidden.at[:, lanes_of(1 - core)]
    arrive(other_lanes, hidden_send, hidden_recv, other_core)
    other_down = down.at[pl.ds(pl.multiple_of((1 - core) * 128, 128), 128)]
    arrive(other_down, pair_send.at[1], pair_recv.at[1], other_core)

    def add(ref, *others):
        value = ref[...].astype(F32)
        for other in others:
            value = value + other[...].astype(F32)
        ref[...] = value.astype(BF16)

    def landed(ref, part, *index):
        return ref.at[(part, *index, slice(None), slice(None), pl.ds(0, PARTS[part][1]))]

    def piece(ref, part):
        return ref.at[:, :, :, pl.ds(*PARTS[part])]

    by_x = [peer(*k) for k in ((0, 2), (1, 2), (0, 1), (0, 3), (0, 0), (1, 1), (1, 3), (1, 0))]
    by_y = [peer(*k) for k in ((0, 2), (0, 1), (0, 3), (0, 0), (1, 2), (1, 1), (1, 3), (1, 0))]

    def blocks(part):
        by_u, by_v = (by_x, by_y) if part == 0 else (by_y, by_x)
        return [k + core * (l - k) for k, l in zip(by_u, by_v)]

    def product(part, k):
        first_lane, lanes = PARTS[part]
        at = pl.ds(pl.multiple_of(k * COLS + first_lane, 128), lanes)
        return dot(hidden[...], down[:, at]).astype(BF16).reshape(2, 8, ROWS, lanes)

    def own(part, after):
        for number, k in enumerate(blocks(part)):
            piece(sums.at[k], part)[...] = product(part, k)
            if number in after:
                after[number]()

    def far_send(part):
        wide = plus(wide_at[part], 2)
        for side in range(2):
            for k in range(2):
                step = HALVES[side][k]
                sem = (part, side, k)
                send(
                    chunk(sums, part, wide, plus(narrow_at[part], step)),
                    landed(half_one, *sem),
                    half_one_send.at[sem],
                    half_one_recv.at[sem],
                    neighbours[wide_axis[part], side],
                )

    def wide_send(part, side, step):
        wide = plus(wide_at[part], 1 if side == 0 else 3)
        sem = (part, side, step)
        send(
            chunk(sums, part, wide, plus(narrow_at[part], step)),
            landed(whole_one, *sem),
            whole_one_send.at[sem],
            whole_one_recv.at[sem],
            neighbours[wide_axis[part], side],
        )

    def near_send(part):
        for k in range(2):
            for side in range(2):
                wide_send(part, side, HALVES[1 - side][k])

    def near_add(part):
        for k in range(2):
            for side in range(2):
                wide = plus(wide_at[part], 1 if side == 0 else 3)
                step = HALVES[side][k]
                sem = (part, side, k)
                block = landed(half_one, *sem)
                arrive(
                    block,
                    half_one_send.at[sem],
                    half_one_recv.at[sem],
                    neighbours[wide_axis[part], side],
                )
                add(chunk(sums, part, wide, plus(narrow_at[part], step)), block)
                wide_send(part, side, step)

    def ahead(side, hop):
        return lax.rem(z + (hop if side == 0 else 8 - hop), 8)

    def ring_send_sum(hop, side, step):
        sem = (side, hop - 1, step)
        send(
            layer(sums, ahead(side, hop), plus(y, step)),
            ring_sums.at[sem],
            ring_sum_send.at[sem],
            ring_sum_recv.at[sem],
            along_z[side],
        )

    def ring_start():
        for k in range(2):
            for side in range(2):
                ring_send_sum(4, side, HALVES[side][k])
        for k in range(2):
            for side in range(2):
                ring_send_sum(3, side, HALVES[1 - side][k])

    def ring_sum(hop):
        for step in (2, 1, 3, 0):
            for side in range(2):
                if hop == 3 and step not in HALVES[side]:
                    continue
                sem = (side, hop, step)
                arrive(
                    ring_sums.at[sem],
                    ring_sum_send.at[sem],
                    ring_sum_recv.at[sem],
                    along_z[side],
                )
                if hop:
                    add(layer(sums, ahead(side, hop), plus(y, step)), ring_sums.at[sem])
                    ring_send_sum(hop, side, step)
            if hop == 0:
                add(
                    layer(sums, z, plus(y, step)),
                    ring_sums.at[0, 0, step],
                    ring_sums.at[1, 0, step],
                )
                at_y = plus(y, step)
                for dx in range(4):
                    if dx or step:
                        send(
                            sums.at[
                                lax.rem(at_y, 2) * 4 + plus(x, dx),
                                at_y // 2,
                                z,
                                :,
                                pl.ds(*PARTS[2]),
                            ],
                            xy_sums.at[4 * step + dx],
                            xy_sum_send.at[4 * step + dx],
                            xy_sum_recv.at[4 * step + dx],
                            device(plus(x, dx), at_y, z, core),
                        )

    def wide_add(part, step):
        narrow = plus(narrow_at[part], step)
        for side in range(2):
            sem = (part, side, step)
            arrive(
                landed(whole_one, *sem),
                whole_one_send.at[sem],
                whole_one_recv.at[sem],
                neighbours[wide_axis[part], side],
            )
        add(
            chunk(sums, part, wide_at[part], narrow),
            landed(whole_one, part, 0, step),
            landed(whole_one, part, 1, step),
        )
        if step:
            send(
                chunk(sums, part, wide_at[part], narrow),
                landed(whole_two, part, step - 1),
                whole_two_send.at[part, step - 1],
                whole_two_recv.at[part, step - 1],
                neighbours[narrow_axis[part], (0, 2, 1)[step - 1]],
            )

    def narrow_end(part):
        blocks_here = [landed(whole_two, part, k) for k in range(3)]
        for k in range(3):
            arrive(
                blocks_here[k],
                whole_two_send.at[part, k],
                whole_two_recv.at[part, k],
                neighbours[narrow_axis[part], k],
            )
        add(chunk(sums, part, wide_at[part], narrow_at[part]), *blocks_here)
        for step in (4, 3, 5, 2, 6, 1, 7):
            to = lax.rem(z + step, 8)
            send(
                sums.at[c, y_hi, to, :, pl.ds(*PARTS[part])],
                last.at[z, :, pl.ds(*PARTS[part])],
                last_send.at[part, to],
                last_recv.at[part, z],
                device(x, y, to, core),
            )

    earlier = taken()
    own(0, {3: lambda: far_send(0)})
    near_send(0)
    own(2, {})
    ring_start()
    own(1, {3: lambda: far_send(1)})
    near_send(1)
    near_add(0)
    ring_sum(3)
    near_add(1)
    ring_sum(2)
    drain(earlier)
    all_heads.wait_send()
    all_notes.wait_send()
    for copy in shared:
        copy.wait_send()
    wide_add(0, 2)
    ring_sum(1)
    wide_add(1, 2)
    for step in (1, 3, 0):
        for part in range(2):
            wide_add(part, step)
    ring_sum(0)
    earlier = taken()
    narrow_end(0)
    narrow_end(1)
    drain(earlier)
    for k in range(1, 16):
        dy, dx = k // 4, k % 4
        arrive(
            xy_sums.at[k],
            xy_sum_send.at[k],
            xy_sum_recv.at[k],
            device(plus(x, 4 - dx), plus(y, 4 - dy), z, core),
        )

    def finish(part, value):
        lanes = pl.ds(*PARTS[part])
        value = value + state[:, lanes] + sums[c, y_hi, z, :, lanes].astype(F32)
        out_ref[:, lanes] = value.astype(BF16)

    finish(2, sum(xy_sums[k].astype(F32) for k in range(1, 16)))
    for part in range(2):
        value = jnp.zeros((ROWS, PARTS[part][1]), F32)
        for step in range(1, 8):
            source = lax.rem(z + step, 8)
            block = last.at[source, :, pl.ds(*PARTS[part])]
            arrive(
                block,
                last_send.at[part, source],
                last_recv.at[part, source],
                device(x, y, source, core),
            )
            value = value + block[...].astype(F32)
        finish(part, value)

    drain(sent)


VMEM = pl.BlockSpec(memory_space=pltpu.VMEM)
SMEM = pl.BlockSpec(memory_space=pltpu.SMEM)
ANY = pl.BlockSpec(memory_space=pl.ANY)
DMA = pltpu.SemaphoreType.DMA


def per_device(
    queries,
    prompt_cache,
    new_latent,
    parents,
    lengths,
    value_weight,
    output_weight,
    residual,
    norm_gain,
    expert_ids,
    expert_weights,
    expert_gate,
    expert_up,
    expert_down,
):
    key_width = queries.shape[3]
    pairs = [(N_CTX,), (N_CTX,), None, (N_CTX,), None, (8,), (8,), (N_CTX,), None]
    pairs += [(8,), (16,), (2, 3), (2, 2, 4), (2, 4), (2, 4, 4), (3,)]
    pairs += [(2,), None, (2, 2, 2), (2, 2, 4), (2, 3), (2, 4, 4), (16,), (2, 8)]
    out = pl.pallas_call(
        layer_kernel,
        out_shape=jax.ShapeDtypeStruct((ROWS, COLS), BF16),
        in_specs=[SMEM, SMEM, ANY, ANY, VMEM, VMEM, VMEM, ANY, ANY, ANY, VMEM, ANY, ANY, ANY],
        out_specs=VMEM,
        scratch_shapes=[
            pltpu.VMEM((N_CTX, 128, key_width), BF16),
            pltpu.VMEM((key_width, prompt_cache.shape[1]), BF16),
            pltpu.VMEM(value_weight.shape, BF16),
            pltpu.VMEM((ROWS, COLS), BF16),
            pltpu.VMEM((256, COLS), BF16),
            pltpu.VMEM((N_CTX, 128, LAT), BF16),
            pltpu.VMEM((N_CTX, 8, 128), F32),
            pltpu.VMEM((N_CTX, 128, LAT), BF16),
            pltpu.VMEM((N_CTX, 8, 128), F32),
            pltpu.VMEM((3, 512, 512), BF16),
            pltpu.VMEM((N_EXP, ROWS, 128), BF16),
            pltpu.VMEM((N_EXP, ROWS, 128), BF16),
            pltpu.VMEM((256, COLS), BF16),
            pltpu.VMEM((N_CTX, 64, 256), BF16),
            pltpu.VMEM((2, 256, 256), BF16),
            pltpu.VMEM((256, 256), BF16),
            pltpu.VMEM((2, 8, ROWS, COLS), BF16),
            pltpu.VMEM((8, ROWS, COLS), BF16),
            pltpu.VMEM((8, ROWS, COLS), BF16),
            pltpu.VMEM((N_CTX, ROWS, 128), F32),
            pltpu.VMEM((ROWS, COLS), F32),
            pltpu.VMEM((N_EXP, 1, 128), F32),
            pltpu.VMEM((N_EXP, 1, 128), F32),
            pltpu.VMEM((N_CTX, 2, 2, 8, ROWS, COLS), BF16),
            pltpu.VMEM((N_CTX, 2, 8, ROWS, COLS), BF16),
            pltpu.VMEM((2, 2, 2, 8, ROWS, 384), BF16),
            pltpu.VMEM((2, 2, 4, 8, ROWS, 384), BF16),
            pltpu.VMEM((2, 3, 8, ROWS, 384), BF16),
            pltpu.VMEM((2, 4, 4, 4, ROWS, 256), BF16),
            pltpu.VMEM((16, ROWS, 256), BF16),
            pltpu.VMEM((8, ROWS, COLS), BF16),
            pltpu.VMEM((512, 128), F32),
            pltpu.VMEM((256, 128), BF16),
            pltpu.VMEM((256, 256), BF16),
            pltpu.VMEM((N_CTX, COLS, 256), BF16),
            pltpu.VMEM((256, N_CTX * COLS), BF16),
            DMA((2,)),
            DMA((6,)),
        ]
        + [DMA(shape) if shape else DMA for shape in pairs for _ in range(2)],
        compiler_params=pltpu.CompilerParams(
            collective_id=0, has_side_effects=True, vmem_limit_bytes=VMEM_LIMIT
        ),
        name="layer",
    )(
        lengths,
        parents.reshape(8),
        queries.reshape(N_CTX, 128, key_width),
        prompt_cache[0].T,
        new_latent.reshape(ROWS, key_width),
        expert_ids.reshape(ROWS, 8),
        expert_weights.reshape(ROWS, 8),
        value_weight,
        output_weight,
        residual.reshape(ROWS, N_CTX * COLS),
        norm_gain.reshape(1, N_CTX * COLS),
        expert_gate.reshape(N_CTX, COLS, 128),
        expert_up.reshape(N_CTX, COLS, 128),
        expert_down[0],
    )
    return out.reshape(2, 8, COLS)


def solution(mesh):
    in_specs = (
        P(None, "exp", None, None),
        P("exp", "ctx", None),
        P(None, "exp", None),
        P("exp", None),
        P("exp"),
        P("exp", None, None),
        P("exp", None),
        P(None, "exp", None),
        P(),
        P(None, "exp", None),
        P(None, "exp", None),
        P("exp", None, "ctx"),
        P("exp", None, "ctx"),
        P("exp", "ctx", None),
    )
    out_specs = P(None, "exp", "ctx")
    return jax.shard_map(
        per_device, mesh=mesh, in_specs=in_specs, out_specs=out_specs, check_vma=False
    )
```

```python
import functools

import jax
import jax.numpy as jnp
from jax import lax
from jax.experimental import pallas as pl
from jax.experimental.pallas import tpu as pltpu
from jax.sharding import PartitionSpec as P

SCALE = 0.07216878364870322
NEGATIVE = -1e30
BF16 = jnp.bfloat16
F32 = jnp.float32
N_CTX = 8
N_EXP = 32
ROWS = 16
MINE = 2
HEADS = 64
LAT = 512
COLS = 896
PARTS = ((0, 384), (384, 256), (640, 256))
HALVES = ((2, 1), (3, 0))
VMEM_LIMIT = 56 * 1024 * 1024


def coordinates():
    c, e = lax.axis_index("ctx"), lax.axis_index("exp")
    x, y_lo = lax.rem(c, 4), c // 4
    z, y_hi, core = e // 4, lax.rem(e // 2, 2), lax.rem(e, 2)
    return c, e, x, y_hi * 2 + y_lo, z, core


def device(x, y, z, core):
    return (lax.rem(y, 2) * 4 + x, z * 4 + (y // 2) * 2 + core)


def greet(barrier, target):
    pl.semaphore_signal(
        barrier, inc=1, device_id=target, device_id_type=pl.DeviceIdType.MESH
    )


def remote(source, target_ref, send_sem, recv_sem, target):
    return pltpu.make_async_remote_copy(
        src_ref=source,
        dst_ref=target_ref,
        send_sem=send_sem,
        recv_sem=recv_sem,
        device_id=target,
        device_id_type=pl.DeviceIdType.MESH,
    )


def one_hot(wanted, columns):
    return jnp.where(
        lax.broadcasted_iota(jnp.int32, (wanted.shape[0], columns), 1) == wanted, 1.0, 0.0
    ).astype(BF16)


def row_index(count):
    return lax.broadcasted_iota(jnp.int32, (count, 1), 0)


def dot(a, b):
    return jnp.dot(a, b, preferred_element_type=F32)


def dot_t(a, b):
    return lax.dot_general(a, b, (((1,), (1,)), ((), ())), preferred_element_type=F32)


def layer_kernel(
    length_ref,
    parents_ref,
    q_hbm,
    cache_hbm,
    new_ref,
    ids_ref,
    gates_ref,
    wv_hbm,
    wo_ref,
    residual_hbm,
    gain_ref,
    gate_ref,
    up_ref,
    down_ref,
    out_ref,
    q_ref,
    cache_ref,
    wv_ref,
    residual_ref,
    wo_other,
    part,
    stat,
    got,
    got_stat,
    orders,
    heads,
    by_head,
    wo_cols,
    values,
    ordered,
    met,
    shares,
    from_y,
    from_z,
    squares,
    state,
    notes,
    noted,
    rows,
    sums,
    half_one,
    whole_one,
    whole_two,
    ring_sums,
    xy_sums,
    last,
    scales,
    crossing_hidden,
    hidden,
    both,
    down,
    input_sems,
    weight_sems,
    part_send,
    part_recv,
    stat_send,
    stat_recv,
    head_send,
    head_recv,
    value_send,
    value_recv,
    crossing_send,
    crossing_recv,
    y_send,
    y_recv,
    zsum_send,
    zsum_recv,
    square_send,
    square_recv,
    note_send,
    note_recv,
    z_send,
    z_recv,
    xy_send,
    xy_recv,
    two_send,
    two_recv,
    three_send,
    three_recv,
    relay_three_send,
    relay_three_recv,
    ring_send,
    ring_recv,
    share_send,
    share_recv,
    pair_send,
    pair_recv,
    hidden_send,
    hidden_recv,
    half_one_send,
    half_one_recv,
    whole_one_send,
    whole_one_recv,
    whole_two_send,
    whole_two_recv,
    ring_sum_send,
    ring_sum_recv,
    xy_sum_send,
    xy_sum_recv,
    last_send,
    last_recv,
):
    c, e, x, y, z, core = coordinates()
    y_hi, y_lo = y // 2, lax.rem(y, 2)

    def plus(a, k):
        return lax.rem(a + k, 4)

    u, v = x + core * (y - x), y + core * (x - y)

    def at_xy(at_u, at_v):
        return at_u + core * (at_v - at_u), at_v + core * (at_u - at_v)

    neighbours = {
        ("u", 0): device(*at_xy(plus(u, 1), v), z, core),
        ("u", 1): device(*at_xy(plus(u, 3), v), z, core),
        ("v", 0): device(*at_xy(u, plus(v, 1)), z, core),
        ("v", 1): device(*at_xy(u, plus(v, 3)), z, core),
        ("u", 2): device(*at_xy(plus(u, 2), v), z, core),
        ("v", 2): device(*at_xy(u, plus(v, 2)), z, core),
    }
    other_core = device(x, y, z, 1 - core)
    wide_axis, narrow_axis = ("u", "v"), ("v", "u")
    wide_at, narrow_at = (u, v), (v, u)

    inputs = [
        pltpu.make_async_copy(cache_hbm, cache_ref, input_sems.at[0]),
        pltpu.make_async_copy(q_hbm, q_ref, input_sems.at[1]),
    ]
    for fetch in inputs:
        fetch.start()
    barrier = pltpu.get_barrier_semaphore()
    for step in range(1, N_CTX):
        greet(barrier, (lax.rem(c + step, N_CTX), e))

    @pl.loop(1, N_EXP)
    def _(step):
        greet(barrier, (c, lax.rem(e + step, N_EXP)))

    for step in range(1, N_CTX):
        greet(barrier, (lax.rem(c + step, N_CTX), e + 2 - 4 * y_hi))

    columns = pl.ds(pl.multiple_of(c * COLS, 128), COLS)
    fetches = [
        pltpu.make_async_copy(wo_ref.at[:, columns], wo_cols, weight_sems.at[0]),
        pltpu.make_async_copy(gate_ref, both.at[:, :, pl.ds(0, 128)], weight_sems.at[1]),
        pltpu.make_async_copy(up_ref, both.at[:, :, pl.ds(128, 128)], weight_sems.at[2]),
        pltpu.make_async_copy(
            down_ref, down.at[pl.ds(pl.multiple_of(core * 128, 128), 128)], weight_sems.at[3]
        ),
        pltpu.make_async_copy(wv_hbm, wv_ref, weight_sems.at[4]),
        pltpu.make_async_copy(residual_hbm.at[:, columns], residual_ref, weight_sems.at[5]),
    ]
    for fetch in fetches:
        fetch.start()

    sent = []

    def taken():
        copies = list(sent)
        sent.clear()
        return copies

    def drain(copies):
        for copy in copies:
            copy.wait_send()

    def send(source, target_ref, send_sem, recv_sem, target):
        copy = remote(source, target_ref, send_sem, recv_sem, target)
        copy.start()
        sent.append(copy)

    def arrive(ref, send_sem, recv_sem, target):
        remote(ref, ref, send_sem, recv_sem, target).wait_recv()

    length = length_ref[0]
    positions = cache_ref.shape[1]
    live = (
        c * positions + lax.broadcasted_iota(jnp.int32, (1, positions), 1)
    ) < length
    wide_lane = lax.broadcasted_iota(jnp.int32, (128, 128), 1)

    def partial(target, sums_ref, stats_ref):
        scores = dot(q_ref[target], cache_ref[...]) * SCALE
        scores = jnp.where(live, scores, NEGATIVE)
        top = jnp.max(scores, axis=-1, keepdims=True)
        weights = jnp.where(live, jnp.exp(scores - top), 0.0)
        total = jnp.sum(weights, axis=-1, keepdims=True)
        sums_ref[...] = dot_t(weights.astype(BF16), cache_ref[:LAT, :]).astype(BF16)
        stats_ref[...] = jnp.where(
            wide_lane == 0, top, jnp.where(wide_lane == 1, total, 0.0)
        ).T[:8]

    def peer(flip, step):
        return lax.rem(y_lo + flip, 2) * 4 + plus(x, step)

    def send_partial(k):
        target = peers[k]
        where = (target, e)
        send(stat.at[target], got_stat.at[k], stat_send.at[k], stat_recv.at[k], where)
        send(part.at[target], got.at[k], part_send.at[k], part_recv.at[k], where)

    peers = [peer(*k) for k in ((1, 2), (0, 2), (1, 1), (0, 1), (1, 3), (0, 3), (1, 0))]
    for fetch in inputs:
        fetch.wait()
    early = 4
    for target in peers[:early]:
        partial(target, part.at[target], stat.at[target])
    pl.semaphore_wait(barrier, 2 * (N_CTX - 1) + N_EXP - 1)
    for k in range(early):
        send_partial(k)
    for k in range(early, N_CTX - 1):
        partial(peers[k], part.at[peers[k]], stat.at[peers[k]])
        send_partial(k)
    send(wo_ref.at[:, columns], wo_other, pair_send.at[0], pair_recv.at[0], other_core)
    own_down = down.at[pl.ds(pl.multiple_of(core * 128, 128), 128)]
    send(down_ref, own_down, pair_send.at[1], pair_recv.at[1], other_core)
    partial(c, got.at[N_CTX - 1], got_stat.at[N_CTX - 1])

    row = row_index(512)
    orders[0] = one_hot(
        ((row >> 2) & 3) * 128 + ((row >> 1) & 1) * HEADS + (row >> 4) * 2 + (row & 1), 512
    )
    orders[1] = one_hot(
        ((row >> 1) & 31) * 16 + ((row >> 6) & 3) * 4 + (row & 1) * 2 + (row >> 8), 512
    )
    orders[2] = one_hot(
        ((row >> 1) & 7) * 64
        + ((row >> 4) & 7) * 8
        + ((row >> 7) & 1) * 4
        + (row >> 8) * 2
        + (row & 1),
        512,
    )

    row = row_index(128)
    base = lax.rem(c, 4) * MINE
    wanted = jnp.where(
        row == 0,
        c * MINE,
        jnp.where(
            row == 1,
            c * MINE + 1,
            jnp.where(
                row == 2, parents_ref[base], jnp.where(row == 3, parents_ref[base + 1], -1)
            ),
        ),
    )
    keys = dot(one_hot(wanted, ROWS), new_ref[...]).astype(BF16)
    scores = dot_t(q_ref[c], keys) * SCALE
    second = jnp.where(row >= HEADS, 1, 0)
    tail_at = jnp.where(c >= 4, second + 2, -1)
    valid = (wide_lane == second) | (wide_lane == tail_at)
    scores = jnp.where(valid, scores, NEGATIVE)
    top = jnp.max(scores, axis=-1, keepdims=True)
    weights = jnp.where(valid, jnp.exp(scores - top), 0.0)
    own_total = jnp.sum(weights, axis=-1, keepdims=True)
    own_sum = dot(weights.astype(BF16), keys[:, :LAT])

    lane = lax.broadcasted_iota(jnp.int32, (ROWS, 128), 1)
    dense = jnp.zeros((ROWS, 128), F32)
    for k in range(8):
        dense = jnp.where(lane == ids_ref[:, k : k + 1], gates_ref[:, k : k + 1], dense)

    for k in range(N_CTX - 1):
        arrive(got_stat.at[k], stat_send.at[k], stat_recv.at[k], (peers[k], e))
    stats = got_stat[...].reshape(N_CTX * 8, 128).T
    peak = top
    for source in range(N_CTX):
        peak = jnp.maximum(peak, stats[:, 8 * source : 8 * source + 1])
    factor = jnp.exp(top - peak)
    total = own_total * factor
    summed = own_sum * factor
    for source in range(N_CTX):
        factor = jnp.exp(stats[:, 8 * source : 8 * source + 1] - peak)
        total = total + stats[:, 8 * source + 1 : 8 * source + 2] * factor
    for source in (N_CTX - 1, *range(N_CTX - 1)):
        if source < N_CTX - 1:
            arrive(
                got.at[source], part_send.at[source], part_recv.at[source], (peers[source], e)
            )
        factor = jnp.exp(stats[:, 8 * source : 8 * source + 1] - peak)
        summed = summed + got[source].astype(F32) * factor
    attended = (summed / total).astype(BF16)
    stacked = jnp.concatenate([attended[:, 128 * k : 128 * k + 128] for k in range(4)], axis=0)
    heads[...] = dot(orders[0], stacked).astype(BF16).reshape(N_EXP, ROWS, 128)

    def head_copy(step):
        target = lax.rem(e + step, N_EXP)
        return remote(heads.at[target], by_head.at[e], head_send, head_recv, (c, target))

    others = pl.ds(0, N_EXP - 1)
    any_peer = (c, lax.rem(e + 1, N_EXP))
    all_heads = remote(heads.at[others], by_head.at[others], head_send, head_recv, any_peer)

    @pl.loop(1, N_EXP)
    def _(step):
        head_copy(step).start()

    by_head[e] = heads[e]

    all_heads.wait_recv()
    fetches[4].wait()
    latents = dot(orders[1], by_head[...].reshape(512, 128)).astype(BF16)
    halves = []
    for parity in range(2):
        value = jnp.zeros((64, 128), F32)
        for quarter in range(4):
            at = (parity * 4 + quarter) * 64
            value = value + dot(
                latents[at : at + 64], wv_ref[parity, 128 * quarter : 128 * quarter + 128, :]
            )
        halves.append(value.astype(BF16))
    values[c] = jnp.concatenate(halves, axis=1)

    for target in peers:
        send(values.at[c], values.at[c], value_send.at[target], value_recv.at[c], (target, e))
    for source in peers:
        arrive(values.at[source], value_send.at[source], value_recv.at[source], (source, e))
    ordered[...] = dot(orders[2], values[...].reshape(512, 256)).astype(BF16).reshape(2, 256, 256)
    send(ordered.at[1 - core], met, crossing_send, crossing_recv, other_core)
    fetches[0].wait()
    arrive(wo_other, pair_send.at[0], pair_recv.at[0], other_core)
    other_y = device(x, plus(y, 2), z, core)
    for half in (1, 0):
        at = lax.rem(y_hi + half, 2)
        near_rows = pl.ds(pl.multiple_of(at * 128, 128), 128)
        own = dot(ordered[core, near_rows], wo_cols[...])
        if half:
            arrive(met, crossing_send, crossing_recv, other_core)
        own = own + dot(met[near_rows], wo_other[...])
        shares[at] = own.astype(BF16).reshape(8, ROWS, COLS)
        if half:
            for step in (4, 3, 5, 2, 6, 1, 7, 0):
                to = lax.rem(z + step, 8)
                send(shares.at[at, to], from_y.at[to], y_send.at[to], y_recv.at[to], other_y)
    for step in (4, 3, 5, 2, 6, 1, 7, 0):
        to = lax.rem(z + step, 8)
        arrive(from_y.at[to], y_send.at[to], y_recv.at[to], other_y)
        both_y = shares[y_hi, to].astype(F32) + from_y[to].astype(F32)
        if step:
            shares[y_hi, to] = both_y.astype(BF16)
            send(
                shares.at[y_hi, to],
                from_z.at[z],
                zsum_send.at[to],
                zsum_recv.at[z],
                device(x, y, to, core),
            )
    fetches[5].wait()
    value = residual_ref[...].astype(F32) + both_y
    for step in range(1, 8):
        source = lax.rem(z + step, 8)
        arrive(
            from_z.at[source],
            zsum_send.at[source],
            zsum_recv.at[source],
            device(x, y, source, core),
        )
        value = value + from_z[source].astype(F32)
    state[...] = value
    rows[c, core, y_hi, z] = (value * gain_ref[:, columns]).astype(BF16)
    squares[c] = jnp.broadcast_to(jnp.sum(value * value, axis=-1, keepdims=True), (ROWS, 128))
    for target in peers:
        send(squares.at[c], squares.at[c], square_send.at[target], square_recv.at[c], (target, e))

    def note_copy(step):
        target = lax.rem(e + step, N_EXP)
        spot = core * 16 + y_hi * 8 + z
        return remote(notes.at[target], noted.at[spot], note_send, note_recv, (c, target))

    all_notes = remote(notes.at[others], noted.at[others], note_send, note_recv, any_peer)

    def send_notes():
        for source in peers:
            arrive(squares.at[source], square_send.at[source], square_recv.at[source], (source, e))
        mean = jnp.sum(squares[...], axis=0) * (1.0 / (N_CTX * COLS))
        scale = lax.rsqrt(mean + 1e-06)
        block = jnp.concatenate([dense, scale, jnp.zeros((96, 128), F32)], axis=0).T
        notes[...] = block[:N_EXP].reshape(N_EXP, 1, 128)
        noted[core * 16 + y_hi * 8 + z] = notes[e]

        @pl.loop(1, N_EXP)
        def _(step):
            note_copy(step).start()

    def chunk(ref, part, wide, narrow, start=0, count=8):
        at_x, at_y = at_xy(wide, narrow) if part == 0 else at_xy(narrow, wide)
        first_lane, lanes = PARTS[part]
        at = (lax.rem(at_y, 2) * 4 + at_x,) + ((core,) if ref is rows else ())
        return ref.at[at + (at_y // 2, pl.ds(start, count), slice(None), pl.ds(first_lane, lanes))]

    def layer(ref, at_z, at_y):
        at = (pl.ds(lax.rem(at_y, 2) * 4, 4),) + ((core,) if ref is rows else ())
        return ref.at[at + (at_y // 2, at_z, slice(None), pl.ds(*PARTS[2]))]

    along_z = (device(x, y, lax.rem(z + 1, 8), core), device(x, y, lax.rem(z + 7, 8), core))

    def behind(side, hop):
        return lax.rem(z + (8 - hop if side == 0 else hop), 8)

    for step in (4, 3, 5, 2, 6, 1, 7):
        to = lax.rem(z + step, 8)
        block = rows.at[c, core, y_hi, z, :, pl.ds(0, PARTS[2][0])]
        send(block, block, z_send.at[to], z_recv.at[z], device(x, y, to, core))
    block = rows.at[c, core, y_hi, z, :, pl.ds(*PARTS[2])]
    for dy in range(4):
        for dx in range(4):
            if dx or dy:
                send(
                    block,
                    block,
                    xy_send.at[4 * dy + dx],
                    xy_recv.at[4 * dy + dx],
                    device(plus(x, dx), plus(y, dy), z, core),
                )

    def share(part, wide, narrow):
        block = chunk(rows, part, wide, narrow)
        remote(block, block, share_send.at[part], share_recv.at[part], other_core).start()

    def spread(part, step):
        narrow = plus(narrow_at[part], step)
        block = chunk(rows, part, wide_at[part], narrow)
        for side in range(2):
            sem = (part, side, step)
            send(
                block,
                block,
                three_send.at[sem],
                three_recv.at[sem],
                neighbours[wide_axis[part], side],
            )
        share(part, wide_at[part], narrow)

    def spread_z(step):
        block = layer(rows, z, plus(y, step))
        for side in range(2):
            sem = (side, 0, step)
            send(block, block, ring_send.at[sem], ring_recv.at[sem], along_z[side])

    def share_z(at_z):
        block = rows.at[:, core, :, at_z, :, pl.ds(*PARTS[2])]
        remote(block, block, share_send.at[2], share_recv.at[2], other_core).start()

    def arrive_plane(dy):
        for dx in range(4):
            if dx or dy:
                at_x, at_y = plus(x, 4 - dx), plus(y, 4 - dy)
                arrive(
                    rows.at[
                        lax.rem(at_y, 2) * 4 + at_x, core, at_y // 2, z, :, pl.ds(*PARTS[2])
                    ],
                    xy_send.at[4 * dy + dx],
                    xy_recv.at[4 * dy + dx],
                    device(at_x, at_y, z, core),
                )

    arrive_plane(0)
    spread_z(0)
    for step in range(1, 8):
        source = lax.rem(z + step, 8)
        arrive(
            rows.at[c, core, y_hi, source, :, pl.ds(0, PARTS[2][0])],
            z_send.at[source],
            z_recv.at[source],
            device(x, y, source, core),
        )
    for part in range(2):
        block = chunk(rows, part, wide_at[part], narrow_at[part])
        for side in range(3):
            send(
                block,
                block,
                two_send.at[part, side],
                two_recv.at[part, side],
                neighbours[narrow_axis[part], side],
            )
    for part in range(2):
        spread(part, 0)
    for dy in (1, 3, 2):
        arrive_plane(dy)
        spread_z(4 - dy)
    share_z(z)

    def arrive_narrow(side):
        step = (3, 1, 2)[side]
        for part in range(2):
            arrive(
                chunk(rows, part, wide_at[part], plus(narrow_at[part], step)),
                two_send.at[part, side],
                two_recv.at[part, side],
                neighbours[narrow_axis[part], side],
            )
            spread(part, step)

    arrive_narrow(0)
    arrive_narrow(1)
    send_notes()

    def ring(hop):
        for step in (0, 3, 1, 2):
            for side in range(2):
                if hop == 4 and (step in (0, 3)) != (side == 0):
                    continue
                block = layer(rows, behind(side, hop), plus(y, step))
                sem = (side, hop - 1, step)
                arrive(block, ring_send.at[sem], ring_recv.at[sem], along_z[side])
                if hop < 3 or (hop == 3 and (step in (0, 3)) == (side == 0)):
                    sem = (side, hop, step)
                    send(block, block, ring_send.at[sem], ring_recv.at[sem], along_z[side])
        if hop < 4:
            for side in range(2):
                share_z(behind(side, hop))
        else:
            share_z(behind(0, 4))

    def near(step):
        for part in range(2):
            narrow = plus(narrow_at[part], step)
            for side in range(2):
                wide = plus(wide_at[part], 3 if side == 0 else 1)
                target = neighbours[wide_axis[part], side]
                sem = (part, side, step)
                block = chunk(rows, part, wide, narrow)
                arrive(block, three_send.at[sem], three_recv.at[sem], target)
                if (step in (0, 3)) == (side == 0):
                    send(
                        block,
                        block,
                        relay_three_send.at[part, step],
                        relay_three_recv.at[part, step],
                        target,
                    )
                share(part, wide, narrow)

    near(0)
    ring(1)
    arrive_narrow(2)
    near(3)
    near(1)
    ring(2)
    near(2)
    ring(3)
    ring(4)
    for step in (0, 3, 1, 2):
        for part in range(2):
            side = 0 if step in (0, 3) else 1
            wide, narrow = plus(wide_at[part], 2), plus(narrow_at[part], step)
            arrive(
                chunk(rows, part, wide, narrow),
                relay_three_send.at[part, step],
                relay_three_recv.at[part, step],
                neighbours[wide_axis[part], side],
            )
            share(part, wide, narrow)
    shared = []
    for part in range(3):
        lanes = pl.ds(*PARTS[part])
        shared.append(
            remote(
                rows.at[:, core, :, :, :, lanes],
                rows.at[:, 1 - core, :, :, :, lanes],
                share_send.at[part],
                share_recv.at[part],
                other_core,
            )
        )
        shared[part].wait_recv()

    for fetch in fetches[1:4]:
        fetch.wait()

    all_notes.wait_recv()
    note = jnp.broadcast_to(noted[...], (N_EXP, ROWS, 128)).reshape(N_EXP * ROWS, 128)
    lane = lax.broadcasted_iota(jnp.int32, (N_EXP * ROWS, 128), 1)
    beam = row_index(N_EXP * ROWS) & 15
    routed = jnp.sum(jnp.where(lane == beam, note, 0.0), axis=-1, keepdims=True)
    scale = jnp.sum(jnp.where(lane == beam + 16, note, 0.0), axis=-1, keepdims=True)
    def hide(half):
        total = jnp.zeros((256, 256), F32)
        for k in range(N_CTX):
            total = total + dot(rows[k, half].reshape(256, COLS), both[k])
        rows_at = pl.ds(pl.multiple_of(half * 256, 256), 256)
        total = total * scales[rows_at, :1]
        gate, up = total[:, :128], total[:, 128:]
        silu = gate / (1.0 + jnp.exp(-gate))
        return (silu * up * scales[rows_at, 1:2]).astype(BF16)

    def lanes_of(half):
        return pl.ds(pl.multiple_of(half * 128, 128), 128)

    scales[...] = jnp.where(lane == 0, scale, routed)
    crossing_hidden[...] = hide(1 - core)
    send(
        crossing_hidden,
        hidden.at[:, lanes_of(core)],
        hidden_send,
        hidden_recv,
        other_core,
    )
    hidden[:, lanes_of(core)] = hide(core)
    other_lanes = hidden.at[:, lanes_of(1 - core)]
    arrive(other_lanes, hidden_send, hidden_recv, other_core)
    other_down = down.at[pl.ds(pl.multiple_of((1 - core) * 128, 128), 128)]
    arrive(other_down, pair_send.at[1], pair_recv.at[1], other_core)

    def add(ref, *others):
        value = ref[...].astype(F32)
        for other in others:
            value = value + other[...].astype(F32)
        ref[...] = value.astype(BF16)

    def landed(ref, part, *index):
        return ref.at[(part, *index, slice(None), slice(None), pl.ds(0, PARTS[part][1]))]

    def piece(ref, part):
        return ref.at[:, :, :, pl.ds(*PARTS[part])]

    by_x = [peer(*k) for k in ((0, 2), (1, 2), (0, 1), (0, 3), (0, 0), (1, 1), (1, 3), (1, 0))]
    by_y = [peer(*k) for k in ((0, 2), (0, 1), (0, 3), (0, 0), (1, 2), (1, 1), (1, 3), (1, 0))]

    def blocks(part):
        by_u, by_v = (by_x, by_y) if part == 0 else (by_y, by_x)
        return [k + core * (l - k) for k, l in zip(by_u, by_v)]

    def product(part, k):
        first_lane, lanes = PARTS[part]
        at = pl.ds(pl.multiple_of(k * COLS + first_lane, 128), lanes)
        return dot(hidden[...], down[:, at]).astype(BF16).reshape(2, 8, ROWS, lanes)

    def own(part, after):
        for number, k in enumerate(blocks(part)):
            piece(sums.at[k], part)[...] = product(part, k)
            if number in after:
                after[number]()

    def far_send(part):
        wide = plus(wide_at[part], 2)
        for side in range(2):
            for k in range(2):
                step = HALVES[side][k]
                sem = (part, side, k)
                send(
                    chunk(sums, part, wide, plus(narrow_at[part], step)),
                    landed(half_one, *sem),
                    half_one_send.at[sem],
                    half_one_recv.at[sem],
                    neighbours[wide_axis[part], side],
                )

    def wide_send(part, side, step):
        wide = plus(wide_at[part], 1 if side == 0 else 3)
        sem = (part, side, step)
        send(
            chunk(sums, part, wide, plus(narrow_at[part], step)),
            landed(whole_one, *sem),
            whole_one_send.at[sem],
            whole_one_recv.at[sem],
            neighbours[wide_axis[part], side],
        )

    def near_send(part):
        for k in range(2):
            for side in range(2):
                wide_send(part, side, HALVES[1 - side][k])

    def near_add(part):
        for k in range(2):
            for side in range(2):
                wide = plus(wide_at[part], 1 if side == 0 else 3)
                step = HALVES[side][k]
                sem = (part, side, k)
                block = landed(half_one, *sem)
                arrive(
                    block,
                    half_one_send.at[sem],
                    half_one_recv.at[sem],
                    neighbours[wide_axis[part], side],
                )
                add(chunk(sums, part, wide, plus(narrow_at[part], step)), block)
                wide_send(part, side, step)

    def ahead(side, hop):
        return lax.rem(z + (hop if side == 0 else 8 - hop), 8)

    def ring_send_sum(hop, side, step):
        sem = (side, hop - 1, step)
        send(
            layer(sums, ahead(side, hop), plus(y, step)),
            ring_sums.at[sem],
            ring_sum_send.at[sem],
            ring_sum_recv.at[sem],
            along_z[side],
        )

    def ring_start():
        for k in range(2):
            for side in range(2):
                ring_send_sum(4, side, HALVES[side][k])
        for k in range(2):
            for side in range(2):
                ring_send_sum(3, side, HALVES[1 - side][k])

    def ring_sum(hop):
        for step in (2, 1, 3, 0):
            for side in range(2):
                if hop == 3 and step not in HALVES[side]:
                    continue
                sem = (side, hop, step)
                arrive(
                    ring_sums.at[sem],
                    ring_sum_send.at[sem],
                    ring_sum_recv.at[sem],
                    along_z[side],
                )
                if hop:
                    add(layer(sums, ahead(side, hop), plus(y, step)), ring_sums.at[sem])
                    ring_send_sum(hop, side, step)
            if hop == 0:
                add(
                    layer(sums, z, plus(y, step)),
                    ring_sums.at[0, 0, step],
                    ring_sums.at[1, 0, step],
                )
                at_y = plus(y, step)
                for dx in range(4):
                    if dx or step:
                        send(
                            sums.at[
                                lax.rem(at_y, 2) * 4 + plus(x, dx),
                                at_y // 2,
                                z,
                                :,
                                pl.ds(*PARTS[2]),
                            ],
                            xy_sums.at[4 * step + dx],
                            xy_sum_send.at[4 * step + dx],
                            xy_sum_recv.at[4 * step + dx],
                            device(plus(x, dx), at_y, z, core),
                        )

    def wide_add(part, step):
        narrow = plus(narrow_at[part], step)
        for side in range(2):
            sem = (part, side, step)
            arrive(
                landed(whole_one, *sem),
                whole_one_send.at[sem],
                whole_one_recv.at[sem],
                neighbours[wide_axis[part], side],
            )
        add(
            chunk(sums, part, wide_at[part], narrow),
            landed(whole_one, part, 0, step),
            landed(whole_one, part, 1, step),
        )
        if step:
            send(
                chunk(sums, part, wide_at[part], narrow),
                landed(whole_two, part, step - 1),
                whole_two_send.at[part, step - 1],
                whole_two_recv.at[part, step - 1],
                neighbours[narrow_axis[part], (0, 2, 1)[step - 1]],
            )

    def narrow_end(part):
        blocks_here = [landed(whole_two, part, k) for k in range(3)]
        for k in range(3):
            arrive(
                blocks_here[k],
                whole_two_send.at[part, k],
                whole_two_recv.at[part, k],
                neighbours[narrow_axis[part], k],
            )
        add(chunk(sums, part, wide_at[part], narrow_at[part]), *blocks_here)
        for step in (4, 3, 5, 2, 6, 1, 7):
            to = lax.rem(z + step, 8)
            send(
                sums.at[c, y_hi, to, :, pl.ds(*PARTS[part])],
                last.at[z, :, pl.ds(*PARTS[part])],
                last_send.at[part, to],
                last_recv.at[part, z],
                device(x, y, to, core),
            )

    earlier = taken()
    own(0, {3: lambda: far_send(0)})
    near_send(0)
    own(2, {})
    ring_start()
    own(1, {3: lambda: far_send(1)})
    near_send(1)
    near_add(0)
    ring_sum(3)
    near_add(1)
    ring_sum(2)
    drain(earlier)
    all_heads.wait_send()
    all_notes.wait_send()
    for copy in shared:
        copy.wait_send()
    wide_add(0, 2)
    ring_sum(1)
    wide_add(1, 2)
    for step in (1, 3, 0):
        for part in range(2):
            wide_add(part, step)
    ring_sum(0)
    earlier = taken()
    narrow_end(0)
    narrow_end(1)
    drain(earlier)
    for k in range(1, 16):
        dy, dx = k // 4, k % 4
        arrive(
            xy_sums.at[k],
            xy_sum_send.at[k],
            xy_sum_recv.at[k],
            device(plus(x, 4 - dx), plus(y, 4 - dy), z, core),
        )

    def finish(part, value):
        lanes = pl.ds(*PARTS[part])
        value = value + state[:, lanes] + sums[c, y_hi, z, :, lanes].astype(F32)
        out_ref[:, lanes] = value.astype(BF16)

    finish(2, sum(xy_sums[k].astype(F32) for k in range(1, 16)))
    for part in range(2):
        value = jnp.zeros((ROWS, PARTS[part][1]), F32)
        for step in range(1, 8):
            source = lax.rem(z + step, 8)
            block = last.at[source, :, pl.ds(*PARTS[part])]
            arrive(
                block,
                last_send.at[part, source],
                last_recv.at[part, source],
                device(x, y, source, core),
            )
            value = value + block[...].astype(F32)
        finish(part, value)

    drain(sent)


VMEM = pl.BlockSpec(memory_space=pltpu.VMEM)
SMEM = pl.BlockSpec(memory_space=pltpu.SMEM)
ANY = pl.BlockSpec(memory_space=pl.ANY)
DMA = pltpu.SemaphoreType.DMA


def per_device(
    queries,
    prompt_cache,
    new_latent,
    parents,
    lengths,
    value_weight,
    output_weight,
    residual,
    norm_gain,
    expert_ids,
    expert_weights,
    expert_gate,
    expert_up,
    expert_down,
):
    key_width = queries.shape[3]
    pairs = [(N_CTX,), (N_CTX,), None, (N_CTX,), None, (8,), (8,), (N_CTX,), None]
    pairs += [(8,), (16,), (2, 3), (2, 2, 4), (2, 4), (2, 4, 4), (3,)]
    pairs += [(2,), None, (2, 2, 2), (2, 2, 4), (2, 3), (2, 4, 4), (16,), (2, 8)]
    out = pl.pallas_call(
        layer_kernel,
        out_shape=jax.ShapeDtypeStruct((ROWS, COLS), BF16),
        in_specs=[SMEM, SMEM, ANY, ANY, VMEM, VMEM, VMEM, ANY, ANY, ANY, VMEM, ANY, ANY, ANY],
        out_specs=VMEM,
        scratch_shapes=[
            pltpu.VMEM((N_CTX, 128, key_width), BF16),
            pltpu.VMEM((key_width, prompt_cache.shape[1]), BF16),
            pltpu.VMEM(value_weight.shape, BF16),
            pltpu.VMEM((ROWS, COLS), BF16),
            pltpu.VMEM((256, COLS), BF16),
            pltpu.VMEM((N_CTX, 128, LAT), BF16),
            pltpu.VMEM((N_CTX, 8, 128), F32),
            pltpu.VMEM((N_CTX, 128, LAT), BF16),
            pltpu.VMEM((N_CTX, 8, 128), F32),
            pltpu.VMEM((3, 512, 512), BF16),
            pltpu.VMEM((N_EXP, ROWS, 128), BF16),
            pltpu.VMEM((N_EXP, ROWS, 128), BF16),
            pltpu.VMEM((256, COLS), BF16),
            pltpu.VMEM((N_CTX, 64, 256), BF16),
            pltpu.VMEM((2, 256, 256), BF16),
            pltpu.VMEM((256, 256), BF16),
            pltpu.VMEM((2, 8, ROWS, COLS), BF16),
            pltpu.VMEM((8, ROWS, COLS), BF16),
            pltpu.VMEM((8, ROWS, COLS), BF16),
            pltpu.VMEM((N_CTX, ROWS, 128), F32),
            pltpu.VMEM((ROWS, COLS), F32),
            pltpu.VMEM((N_EXP, 1, 128), F32),
            pltpu.VMEM((N_EXP, 1, 128), F32),
            pltpu.VMEM((N_CTX, 2, 2, 8, ROWS, COLS), BF16),
            pltpu.VMEM((N_CTX, 2, 8, ROWS, COLS), BF16),
            pltpu.VMEM((2, 2, 2, 8, ROWS, 384), BF16),
            pltpu.VMEM((2, 2, 4, 8, ROWS, 384), BF16),
            pltpu.VMEM((2, 3, 8, ROWS, 384), BF16),
            pltpu.VMEM((2, 4, 4, 4, ROWS, 256), BF16),
            pltpu.VMEM((16, ROWS, 256), BF16),
            pltpu.VMEM((8, ROWS, COLS), BF16),
            pltpu.VMEM((512, 128), F32),
            pltpu.VMEM((256, 128), BF16),
            pltpu.VMEM((256, 256), BF16),
            pltpu.VMEM((N_CTX, COLS, 256), BF16),
            pltpu.VMEM((256, N_CTX * COLS), BF16),
            DMA((2,)),
            DMA((6,)),
        ]
        + [DMA(shape) if shape else DMA for shape in pairs for _ in range(2)],
        compiler_params=pltpu.CompilerParams(
            collective_id=0, has_side_effects=True, vmem_limit_bytes=VMEM_LIMIT
        ),
        name="layer",
    )(
        lengths,
        parents.reshape(8),
        queries.reshape(N_CTX, 128, key_width),
        prompt_cache[0].T,
        new_latent.reshape(ROWS, key_width),
        expert_ids.reshape(ROWS, 8),
        expert_weights.reshape(ROWS, 8),
        value_weight,
        output_weight,
        residual.reshape(ROWS, N_CTX * COLS),
        norm_gain.reshape(1, N_CTX * COLS),
        expert_gate.reshape(N_CTX, COLS, 128),
        expert_up.reshape(N_CTX, COLS, 128),
        expert_down[0],
    )
    return out.reshape(2, 8, COLS)


def solution(mesh):
    in_specs = (
        P(None, "exp", None, None),
        P("exp", "ctx", None),
        P(None, "exp", None),
        P("exp", None),
        P("exp"),
        P("exp", None, None),
        P("exp", None),
        P(None, "exp", None),
        P(),
        P(None, "exp", None),
        P(None, "exp", None),
        P("exp", None, "ctx"),
        P("exp", None, "ctx"),
        P("exp", "ctx", None),
    )
    out_specs = P(None, "exp", "ctx")
    return jax.shard_map(
        per_device, mesh=mesh, in_specs=in_specs, out_specs=out_specs, check_vma=False
    )
```

```python
import functools

import jax
import jax.numpy as jnp
from jax import lax
from jax.experimental import pallas as pl
from jax.experimental.pallas import tpu as pltpu
from jax.sharding import PartitionSpec as P

SCALE = 0.07216878364870322
NEGATIVE = -1e30
BF16 = jnp.bfloat16
F32 = jnp.float32
N_CTX = 8
N_EXP = 32
ROWS = 16
MINE = 2
HEADS = 64
LAT = 512
COLS = 896
PARTS = ((0, 384), (384, 256), (640, 256))
HALVES = ((2, 1), (3, 0))
VMEM_LIMIT = 56 * 1024 * 1024


def coordinates():
    c, e = lax.axis_index("ctx"), lax.axis_index("exp")
    x, y_lo = lax.rem(c, 4), c // 4
    z, y_hi, core = e // 4, lax.rem(e // 2, 2), lax.rem(e, 2)
    return c, e, x, y_hi * 2 + y_lo, z, core


def device(x, y, z, core):
    return (lax.rem(y, 2) * 4 + x, z * 4 + (y // 2) * 2 + core)


def greet(barrier, target):
    pl.semaphore_signal(
        barrier, inc=1, device_id=target, device_id_type=pl.DeviceIdType.MESH
    )


def remote(source, target_ref, send_sem, recv_sem, target):
    return pltpu.make_async_remote_copy(
        src_ref=source,
        dst_ref=target_ref,
        send_sem=send_sem,
        recv_sem=recv_sem,
        device_id=target,
        device_id_type=pl.DeviceIdType.MESH,
    )


def one_hot(wanted, columns):
    return jnp.where(
        lax.broadcasted_iota(jnp.int32, (wanted.shape[0], columns), 1) == wanted, 1.0, 0.0
    ).astype(BF16)


def row_index(count):
    return lax.broadcasted_iota(jnp.int32, (count, 1), 0)


def dot(a, b):
    return jnp.dot(a, b, preferred_element_type=F32)


def dot_t(a, b):
    return lax.dot_general(a, b, (((1,), (1,)), ((), ())), preferred_element_type=F32)


def layer_kernel(
    length_ref,
    parents_ref,
    q_hbm,
    cache_hbm,
    new_ref,
    ids_ref,
    gates_ref,
    wv_hbm,
    wo_ref,
    residual_hbm,
    gain_ref,
    gate_ref,
    up_ref,
    down_ref,
    out_ref,
    q_ref,
    cache_ref,
    wv_ref,
    residual_ref,
    wo_other,
    part,
    stat,
    got,
    got_stat,
    orders,
    heads,
    by_head,
    wo_cols,
    values,
    ordered,
    met,
    shares,
    from_y,
    from_z,
    ahead_z,
    summed_z,
    crossed_z,
    squares,
    state,
    notes,
    noted,
    rows,
    sums,
    half_one,
    whole_one,
    whole_two,
    ring_sums,
    xy_sums,
    last,
    scales,
    crossing_hidden,
    hidden,
    both,
    down,
    input_sems,
    weight_sems,
    part_send,
    part_recv,
    stat_send,
    stat_recv,
    head_send,
    head_recv,
    value_send,
    value_recv,
    crossing_send,
    crossing_recv,
    y_send,
    y_recv,
    zsum_send,
    zsum_recv,
    ahead_send,
    ahead_recv,
    cross_z_send,
    cross_z_recv,
    square_send,
    square_recv,
    note_send,
    note_recv,
    z_send,
    z_recv,
    xy_send,
    xy_recv,
    two_send,
    two_recv,
    three_send,
    three_recv,
    relay_three_send,
    relay_three_recv,
    ring_send,
    ring_recv,
    share_send,
    share_recv,
    pair_send,
    pair_recv,
    hidden_send,
    hidden_recv,
    half_one_send,
    half_one_recv,
    whole_one_send,
    whole_one_recv,
    whole_two_send,
    whole_two_recv,
    ring_sum_send,
    ring_sum_recv,
    xy_sum_send,
    xy_sum_recv,
    last_send,
    last_recv,
):
    c, e, x, y, z, core = coordinates()
    y_hi, y_lo = y // 2, lax.rem(y, 2)

    def plus(a, k):
        return lax.rem(a + k, 4)

    u, v = x + core * (y - x), y + core * (x - y)

    def at_xy(at_u, at_v):
        return at_u + core * (at_v - at_u), at_v + core * (at_u - at_v)

    neighbours = {
        ("u", 0): device(*at_xy(plus(u, 1), v), z, core),
        ("u", 1): device(*at_xy(plus(u, 3), v), z, core),
        ("v", 0): device(*at_xy(u, plus(v, 1)), z, core),
        ("v", 1): device(*at_xy(u, plus(v, 3)), z, core),
        ("u", 2): device(*at_xy(plus(u, 2), v), z, core),
        ("v", 2): device(*at_xy(u, plus(v, 2)), z, core),
    }
    other_core = device(x, y, z, 1 - core)
    wide_axis, narrow_axis = ("u", "v"), ("v", "u")
    wide_at, narrow_at = (u, v), (v, u)

    inputs = [
        pltpu.make_async_copy(cache_hbm, cache_ref, input_sems.at[0]),
        pltpu.make_async_copy(q_hbm, q_ref, input_sems.at[1]),
    ]
    for fetch in inputs:
        fetch.start()
    barrier = pltpu.get_barrier_semaphore()
    for step in range(1, N_CTX):
        greet(barrier, (lax.rem(c + step, N_CTX), e))

    @pl.loop(1, N_EXP)
    def _(step):
        greet(barrier, (c, lax.rem(e + step, N_EXP)))

    for step in range(1, N_CTX):
        greet(barrier, (lax.rem(c + step, N_CTX), e + 2 - 4 * y_hi))

    columns = pl.ds(pl.multiple_of(c * COLS, 128), COLS)
    fetches = [
        pltpu.make_async_copy(wo_ref.at[:, columns], wo_cols, weight_sems.at[0]),
        pltpu.make_async_copy(gate_ref, both.at[:, :, pl.ds(0, 128)], weight_sems.at[1]),
        pltpu.make_async_copy(up_ref, both.at[:, :, pl.ds(128, 128)], weight_sems.at[2]),
        pltpu.make_async_copy(
            down_ref, down.at[pl.ds(pl.multiple_of(core * 128, 128), 128)], weight_sems.at[3]
        ),
        pltpu.make_async_copy(wv_hbm, wv_ref, weight_sems.at[4]),
        pltpu.make_async_copy(residual_hbm.at[:, columns], residual_ref, weight_sems.at[5]),
    ]
    for fetch in fetches:
        fetch.start()

    sent = []

    def taken():
        copies = list(sent)
        sent.clear()
        return copies

    def drain(copies):
        for copy in copies:
            copy.wait_send()

    def send(source, target_ref, send_sem, recv_sem, target):
        copy = remote(source, target_ref, send_sem, recv_sem, target)
        copy.start()
        sent.append(copy)

    def arrive(ref, send_sem, recv_sem, target):
        remote(ref, ref, send_sem, recv_sem, target).wait_recv()

    length = length_ref[0]
    positions = cache_ref.shape[1]
    live = (
        c * positions + lax.broadcasted_iota(jnp.int32, (1, positions), 1)
    ) < length
    wide_lane = lax.broadcasted_iota(jnp.int32, (128, 128), 1)

    def partial(target, sums_ref, stats_ref):
        scores = dot(q_ref[target], cache_ref[...]) * SCALE
        scores = jnp.where(live, scores, NEGATIVE)
        top = jnp.max(scores, axis=-1, keepdims=True)
        weights = jnp.where(live, jnp.exp(scores - top), 0.0)
        total = jnp.sum(weights, axis=-1, keepdims=True)
        sums_ref[...] = dot_t(weights.astype(BF16), cache_ref[:LAT, :]).astype(BF16)
        stats_ref[...] = jnp.where(
            wide_lane == 0, top, jnp.where(wide_lane == 1, total, 0.0)
        ).T[:8]

    def peer(flip, step):
        return lax.rem(y_lo + flip, 2) * 4 + plus(x, step)

    def send_partial(k):
        target = peers[k]
        where = (target, e)
        send(stat.at[target], got_stat.at[k], stat_send.at[k], stat_recv.at[k], where)
        send(part.at[target], got.at[k], part_send.at[k], part_recv.at[k], where)

    peers = [peer(*k) for k in ((1, 2), (0, 2), (1, 1), (0, 1), (1, 3), (0, 3), (1, 0))]
    for fetch in inputs:
        fetch.wait()
    early = 4
    for target in peers[:early]:
        partial(target, part.at[target], stat.at[target])
    pl.semaphore_wait(barrier, 2 * (N_CTX - 1) + N_EXP - 1)
    for k in range(early):
        send_partial(k)
    for k in range(early, N_CTX - 1):
        partial(peers[k], part.at[peers[k]], stat.at[peers[k]])
        send_partial(k)
    send(wo_ref.at[:, columns], wo_other, pair_send.at[0], pair_recv.at[0], other_core)
    own_down = down.at[pl.ds(pl.multiple_of(core * 128, 128), 128)]
    send(down_ref, own_down, pair_send.at[1], pair_recv.at[1], other_core)
    partial(c, got.at[N_CTX - 1], got_stat.at[N_CTX - 1])

    row = row_index(512)
    orders[0] = one_hot(
        ((row >> 2) & 3) * 128 + ((row >> 1) & 1) * HEADS + (row >> 4) * 2 + (row & 1), 512
    )
    orders[1] = one_hot(
        ((row >> 1) & 31) * 16 + ((row >> 6) & 3) * 4 + (row & 1) * 2 + (row >> 8), 512
    )
    orders[2] = one_hot(
        ((row >> 1) & 7) * 64
        + ((row >> 4) & 7) * 8
        + ((row >> 7) & 1) * 4
        + (row >> 8) * 2
        + (row & 1),
        512,
    )

    row = row_index(128)
    base = lax.rem(c, 4) * MINE
    wanted = jnp.where(
        row == 0,
        c * MINE,
        jnp.where(
            row == 1,
            c * MINE + 1,
            jnp.where(
                row == 2, parents_ref[base], jnp.where(row == 3, parents_ref[base + 1], -1)
            ),
        ),
    )
    keys = dot(one_hot(wanted, ROWS), new_ref[...]).astype(BF16)
    scores = dot_t(q_ref[c], keys) * SCALE
    second = jnp.where(row >= HEADS, 1, 0)
    tail_at = jnp.where(c >= 4, second + 2, -1)
    valid = (wide_lane == second) | (wide_lane == tail_at)
    scores = jnp.where(valid, scores, NEGATIVE)
    top = jnp.max(scores, axis=-1, keepdims=True)
    weights = jnp.where(valid, jnp.exp(scores - top), 0.0)
    own_total = jnp.sum(weights, axis=-1, keepdims=True)
    own_sum = dot(weights.astype(BF16), keys[:, :LAT])

    lane = lax.broadcasted_iota(jnp.int32, (ROWS, 128), 1)
    dense = jnp.zeros((ROWS, 128), F32)
    for k in range(8):
        dense = jnp.where(lane == ids_ref[:, k : k + 1], gates_ref[:, k : k + 1], dense)

    for k in range(N_CTX - 1):
        arrive(got_stat.at[k], stat_send.at[k], stat_recv.at[k], (peers[k], e))
    stats = got_stat[...].reshape(N_CTX * 8, 128).T
    peak = top
    for source in range(N_CTX):
        peak = jnp.maximum(peak, stats[:, 8 * source : 8 * source + 1])
    factor = jnp.exp(top - peak)
    total = own_total * factor
    summed = own_sum * factor
    for source in range(N_CTX):
        factor = jnp.exp(stats[:, 8 * source : 8 * source + 1] - peak)
        total = total + stats[:, 8 * source + 1 : 8 * source + 2] * factor
    for source in (N_CTX - 1, *range(N_CTX - 1)):
        if source < N_CTX - 1:
            arrive(
                got.at[source], part_send.at[source], part_recv.at[source], (peers[source], e)
            )
        factor = jnp.exp(stats[:, 8 * source : 8 * source + 1] - peak)
        summed = summed + got[source].astype(F32) * factor
    attended = (summed / total).astype(BF16)
    stacked = jnp.concatenate([attended[:, 128 * k : 128 * k + 128] for k in range(4)], axis=0)
    heads[...] = dot(orders[0], stacked).astype(BF16).reshape(N_EXP, ROWS, 128)

    def head_copy(step):
        target = lax.rem(e + step, N_EXP)
        return remote(heads.at[target], by_head.at[e], head_send, head_recv, (c, target))

    others = pl.ds(0, N_EXP - 1)
    any_peer = (c, lax.rem(e + 1, N_EXP))
    all_heads = remote(heads.at[others], by_head.at[others], head_send, head_recv, any_peer)

    @pl.loop(1, N_EXP)
    def _(step):
        head_copy(step).start()

    by_head[e] = heads[e]

    all_heads.wait_recv()
    fetches[4].wait()
    latents = dot(orders[1], by_head[...].reshape(512, 128)).astype(BF16)
    halves = []
    for parity in range(2):
        value = jnp.zeros((64, 128), F32)
        for quarter in range(4):
            at = (parity * 4 + quarter) * 64
            value = value + dot(
                latents[at : at + 64], wv_ref[parity, 128 * quarter : 128 * quarter + 128, :]
            )
        halves.append(value.astype(BF16))
    values[c] = jnp.concatenate(halves, axis=1)

    for target in peers:
        send(values.at[c], values.at[c], value_send.at[target], value_recv.at[c], (target, e))
    for source in peers:
        arrive(values.at[source], value_send.at[source], value_recv.at[source], (source, e))
    ordered[...] = dot(orders[2], values[...].reshape(512, 256)).astype(BF16).reshape(2, 256, 256)
    send(ordered.at[1 - core], met, crossing_send, crossing_recv, other_core)
    fetches[0].wait()
    arrive(wo_other, pair_send.at[0], pair_recv.at[0], other_core)
    other_y = device(x, plus(y, 2), z, core)
    y_first, z_first = pl.ds(0, 512), pl.ds(512, COLS - 512)
    for half in (1, 0):
        at = lax.rem(y_hi + half, 2)
        near_rows = pl.ds(pl.multiple_of(at * 128, 128), 128)
        own = dot(ordered[core, near_rows], wo_cols[...])
        if half:
            arrive(met, crossing_send, crossing_recv, other_core)
        own = own + dot(met[near_rows], wo_other[...])
        shares[at] = own.astype(BF16).reshape(8, ROWS, COLS)
        if half:
            for step in (4, 3, 5, 2, 6, 1, 7, 0):
                to = lax.rem(z + step, 8)
                send(
                    shares.at[at, to, :, y_first],
                    from_y.at[to, :, y_first],
                    y_send.at[to],
                    y_recv.at[to],
                    other_y,
                )
    for step in (4, 3, 5, 2, 6, 1, 7):
        to = lax.rem(z + step, 8)
        send(
            shares.at[:, to, :, z_first],
            ahead_z.at[z],
            ahead_send.at[to],
            ahead_recv.at[z],
            device(x, y, to, core),
        )
    for step in (4, 3, 5, 2, 6, 1, 7, 0):
        to = lax.rem(z + step, 8)
        arrive(from_y.at[to, :, y_first], y_send.at[to], y_recv.at[to], other_y)
        both_y = shares[y_hi, to, :, y_first].astype(F32) + from_y[to, :, y_first].astype(F32)
        if step:
            shares[y_hi, to, :, y_first] = both_y.astype(BF16)
            send(
                shares.at[y_hi, to, :, y_first],
                from_z.at[z, :, y_first],
                zsum_send.at[to],
                zsum_recv.at[z],
                device(x, y, to, core),
            )
    both_z = shares[:, z, :, z_first].astype(F32)
    for step in range(1, 8):
        source = lax.rem(z + step, 8)
        arrive(
            ahead_z.at[source],
            ahead_send.at[source],
            ahead_recv.at[source],
            device(x, y, source, core),
        )
        both_z = both_z + ahead_z[source].astype(F32)
    summed_z[...] = both_z.astype(BF16)
    send(summed_z.at[1 - y_hi], crossed_z, cross_z_send, cross_z_recv, other_y)
    fetches[5].wait()
    value = residual_ref[:, y_first].astype(F32) + both_y
    for step in range(1, 8):
        source = lax.rem(z + step, 8)
        arrive(
            from_z.at[source, :, y_first],
            zsum_send.at[source],
            zsum_recv.at[source],
            device(x, y, source, core),
        )
        value = value + from_z[source, :, y_first].astype(F32)
    state[:, y_first] = value
    arrive(crossed_z, cross_z_send, cross_z_recv, other_y)
    value = residual_ref[:, z_first].astype(F32) + summed_z[y_hi].astype(F32)
    state[:, z_first] = value + crossed_z[...].astype(F32)
    value = state[...]
    rows[c, core, y_hi, z] = (value * gain_ref[:, columns]).astype(BF16)
    squares[c] = jnp.broadcast_to(jnp.sum(value * value, axis=-1, keepdims=True), (ROWS, 128))
    for target in peers:
        send(squares.at[c], squares.at[c], square_send.at[target], square_recv.at[c], (target, e))

    def note_copy(step):
        target = lax.rem(e + step, N_EXP)
        spot = core * 16 + y_hi * 8 + z
        return remote(notes.at[target], noted.at[spot], note_send, note_recv, (c, target))

    all_notes = remote(notes.at[others], noted.at[others], note_send, note_recv, any_peer)

    def send_notes():
        for source in peers:
            arrive(squares.at[source], square_send.at[source], square_recv.at[source], (source, e))
        mean = jnp.sum(squares[...], axis=0) * (1.0 / (N_CTX * COLS))
        scale = lax.rsqrt(mean + 1e-06)
        block = jnp.concatenate([dense, scale, jnp.zeros((96, 128), F32)], axis=0).T
        notes[...] = block[:N_EXP].reshape(N_EXP, 1, 128)
        noted[core * 16 + y_hi * 8 + z] = notes[e]

        @pl.loop(1, N_EXP)
        def _(step):
            note_copy(step).start()

    def chunk(ref, part, wide, narrow, start=0, count=8):
        at_x, at_y = at_xy(wide, narrow) if part == 0 else at_xy(narrow, wide)
        first_lane, lanes = PARTS[part]
        at = (lax.rem(at_y, 2) * 4 + at_x,) + ((core,) if ref is rows else ())
        return ref.at[at + (at_y // 2, pl.ds(start, count), slice(None), pl.ds(first_lane, lanes))]

    def layer(ref, at_z, at_y):
        at = (pl.ds(lax.rem(at_y, 2) * 4, 4),) + ((core,) if ref is rows else ())
        return ref.at[at + (at_y // 2, at_z, slice(None), pl.ds(*PARTS[2]))]

    along_z = (device(x, y, lax.rem(z + 1, 8), core), device(x, y, lax.rem(z + 7, 8), core))

    def behind(side, hop):
        return lax.rem(z + (8 - hop if side == 0 else hop), 8)

    for step in (4, 3, 5, 2, 6, 1, 7):
        to = lax.rem(z + step, 8)
        block = rows.at[c, core, y_hi, z, :, pl.ds(0, PARTS[2][0])]
        send(block, block, z_send.at[to], z_recv.at[z], device(x, y, to, core))
    block = rows.at[c, core, y_hi, z, :, pl.ds(*PARTS[2])]
    for dy in range(4):
        for dx in range(4):
            if dx or dy:
                send(
                    block,
                    block,
                    xy_send.at[4 * dy + dx],
                    xy_recv.at[4 * dy + dx],
                    device(plus(x, dx), plus(y, dy), z, core),
                )

    def share(part, wide, narrow):
        block = chunk(rows, part, wide, narrow)
        remote(block, block, share_send.at[part], share_recv.at[part], other_core).start()

    def spread(part, step):
        narrow = plus(narrow_at[part], step)
        block = chunk(rows, part, wide_at[part], narrow)
        for side in range(2):
            sem = (part, side, step)
            send(
                block,
                block,
                three_send.at[sem],
                three_recv.at[sem],
                neighbours[wide_axis[part], side],
            )
        share(part, wide_at[part], narrow)

    def spread_z(step):
        block = layer(rows, z, plus(y, step))
        for side in range(2):
            sem = (side, 0, step)
            send(block, block, ring_send.at[sem], ring_recv.at[sem], along_z[side])

    def share_z(at_z):
        block = rows.at[:, core, :, at_z, :, pl.ds(*PARTS[2])]
        remote(block, block, share_send.at[2], share_recv.at[2], other_core).start()

    def arrive_plane(dy):
        for dx in range(4):
            if dx or dy:
                at_x, at_y = plus(x, 4 - dx), plus(y, 4 - dy)
                arrive(
                    rows.at[
                        lax.rem(at_y, 2) * 4 + at_x, core, at_y // 2, z, :, pl.ds(*PARTS[2])
                    ],
                    xy_send.at[4 * dy + dx],
                    xy_recv.at[4 * dy + dx],
                    device(at_x, at_y, z, core),
                )

    arrive_plane(0)
    spread_z(0)
    for step in range(1, 8):
        source = lax.rem(z + step, 8)
        arrive(
            rows.at[c, core, y_hi, source, :, pl.ds(0, PARTS[2][0])],
            z_send.at[source],
            z_recv.at[source],
            device(x, y, source, core),
        )
    for part in range(2):
        block = chunk(rows, part, wide_at[part], narrow_at[part])
        for side in range(3):
            send(
                block,
                block,
                two_send.at[part, side],
                two_recv.at[part, side],
                neighbours[narrow_axis[part], side],
            )
    for part in range(2):
        spread(part, 0)
    for dy in (1, 3, 2):
        arrive_plane(dy)
        spread_z(4 - dy)
    share_z(z)

    def arrive_narrow(side):
        step = (3, 1, 2)[side]
        for part in range(2):
            arrive(
                chunk(rows, part, wide_at[part], plus(narrow_at[part], step)),
                two_send.at[part, side],
                two_recv.at[part, side],
                neighbours[narrow_axis[part], side],
            )
            spread(part, step)

    arrive_narrow(0)
    arrive_narrow(1)
    send_notes()

    def ring(hop):
        for step in (0, 3, 1, 2):
            for side in range(2):
                if hop == 4 and (step in (0, 3)) != (side == 0):
                    continue
                block = layer(rows, behind(side, hop), plus(y, step))
                sem = (side, hop - 1, step)
                arrive(block, ring_send.at[sem], ring_recv.at[sem], along_z[side])
                if hop < 3 or (hop == 3 and (step in (0, 3)) == (side == 0)):
                    sem = (side, hop, step)
                    send(block, block, ring_send.at[sem], ring_recv.at[sem], along_z[side])
        if hop < 4:
            for side in range(2):
                share_z(behind(side, hop))
        else:
            share_z(behind(0, 4))

    def near(step):
        for part in range(2):
            narrow = plus(narrow_at[part], step)
            for side in range(2):
                wide = plus(wide_at[part], 3 if side == 0 else 1)
                target = neighbours[wide_axis[part], side]
                sem = (part, side, step)
                block = chunk(rows, part, wide, narrow)
                arrive(block, three_send.at[sem], three_recv.at[sem], target)
                if (step in (0, 3)) == (side == 0):
                    send(
                        block,
                        block,
                        relay_three_send.at[part, step],
                        relay_three_recv.at[part, step],
                        target,
                    )
                share(part, wide, narrow)

    near(0)
    ring(1)
    arrive_narrow(2)
    near(3)
    near(1)
    ring(2)
    near(2)
    ring(3)
    ring(4)
    for step in (0, 3, 1, 2):
        for part in range(2):
            side = 0 if step in (0, 3) else 1
            wide, narrow = plus(wide_at[part], 2), plus(narrow_at[part], step)
            arrive(
                chunk(rows, part, wide, narrow),
                relay_three_send.at[part, step],
                relay_three_recv.at[part, step],
                neighbours[wide_axis[part], side],
            )
            share(part, wide, narrow)
    shared = []
    for part in range(3):
        lanes = pl.ds(*PARTS[part])
        shared.append(
            remote(
                rows.at[:, core, :, :, :, lanes],
                rows.at[:, 1 - core, :, :, :, lanes],
                share_send.at[part],
                share_recv.at[part],
                other_core,
            )
        )
        shared[part].wait_recv()

    for fetch in fetches[1:4]:
        fetch.wait()

    all_notes.wait_recv()
    note = jnp.broadcast_to(noted[...], (N_EXP, ROWS, 128)).reshape(N_EXP * ROWS, 128)
    lane = lax.broadcasted_iota(jnp.int32, (N_EXP * ROWS, 128), 1)
    beam = row_index(N_EXP * ROWS) & 15
    routed = jnp.sum(jnp.where(lane == beam, note, 0.0), axis=-1, keepdims=True)
    scale = jnp.sum(jnp.where(lane == beam + 16, note, 0.0), axis=-1, keepdims=True)
    def hide(half):
        total = jnp.zeros((256, 256), F32)
        for k in range(N_CTX):
            total = total + dot(rows[k, half].reshape(256, COLS), both[k])
        rows_at = pl.ds(pl.multiple_of(half * 256, 256), 256)
        total = total * scales[rows_at, :1]
        gate, up = total[:, :128], total[:, 128:]
        silu = gate / (1.0 + jnp.exp(-gate))
        return (silu * up * scales[rows_at, 1:2]).astype(BF16)

    def lanes_of(half):
        return pl.ds(pl.multiple_of(half * 128, 128), 128)

    scales[...] = jnp.where(lane == 0, scale, routed)
    crossing_hidden[...] = hide(1 - core)
    send(
        crossing_hidden,
        hidden.at[:, lanes_of(core)],
        hidden_send,
        hidden_recv,
        other_core,
    )
    hidden[:, lanes_of(core)] = hide(core)
    other_lanes = hidden.at[:, lanes_of(1 - core)]
    arrive(other_lanes, hidden_send, hidden_recv, other_core)
    other_down = down.at[pl.ds(pl.multiple_of((1 - core) * 128, 128), 128)]
    arrive(other_down, pair_send.at[1], pair_recv.at[1], other_core)

    def add(ref, *others):
        value = ref[...].astype(F32)
        for other in others:
            value = value + other[...].astype(F32)
        ref[...] = value.astype(BF16)

    def landed(ref, part, *index):
        return ref.at[(part, *index, slice(None), slice(None), pl.ds(0, PARTS[part][1]))]

    def piece(ref, part):
        return ref.at[:, :, :, pl.ds(*PARTS[part])]

    by_x = [peer(*k) for k in ((0, 2), (1, 2), (0, 1), (0, 3), (0, 0), (1, 1), (1, 3), (1, 0))]
    by_y = [peer(*k) for k in ((0, 2), (0, 1), (0, 3), (0, 0), (1, 2), (1, 1), (1, 3), (1, 0))]

    def blocks(part):
        by_u, by_v = (by_x, by_y) if part == 0 else (by_y, by_x)
        return [k + core * (l - k) for k, l in zip(by_u, by_v)]

    def product(part, k):
        first_lane, lanes = PARTS[part]
        at = pl.ds(pl.multiple_of(k * COLS + first_lane, 128), lanes)
        return dot(hidden[...], down[:, at]).astype(BF16).reshape(2, 8, ROWS, lanes)

    def own(part, after):
        for number, k in enumerate(blocks(part)):
            piece(sums.at[k], part)[...] = product(part, k)
            if number in after:
                after[number]()

    def far_send(part):
        wide = plus(wide_at[part], 2)
        for side in range(2):
            for k in range(2):
                step = HALVES[side][k]
                sem = (part, side, k)
                send(
                    chunk(sums, part, wide, plus(narrow_at[part], step)),
                    landed(half_one, *sem),
                    half_one_send.at[sem],
                    half_one_recv.at[sem],
                    neighbours[wide_axis[part], side],
                )

    def wide_send(part, side, step):
        wide = plus(wide_at[part], 1 if side == 0 else 3)
        sem = (part, side, step)
        send(
            chunk(sums, part, wide, plus(narrow_at[part], step)),
            landed(whole_one, *sem),
            whole_one_send.at[sem],
            whole_one_recv.at[sem],
            neighbours[wide_axis[part], side],
        )

    def near_send(part):
        for k in range(2):
            for side in range(2):
                wide_send(part, side, HALVES[1 - side][k])

    def near_add(part):
        for k in range(2):
            for side in range(2):
                wide = plus(wide_at[part], 1 if side == 0 else 3)
                step = HALVES[side][k]
                sem = (part, side, k)
                block = landed(half_one, *sem)
                arrive(
                    block,
                    half_one_send.at[sem],
                    half_one_recv.at[sem],
                    neighbours[wide_axis[part], side],
                )
                add(chunk(sums, part, wide, plus(narrow_at[part], step)), block)
                wide_send(part, side, step)

    def ahead(side, hop):
        return lax.rem(z + (hop if side == 0 else 8 - hop), 8)

    def ring_send_sum(hop, side, step):
        sem = (side, hop - 1, step)
        send(
            layer(sums, ahead(side, hop), plus(y, step)),
            ring_sums.at[sem],
            ring_sum_send.at[sem],
            ring_sum_recv.at[sem],
            along_z[side],
        )

    def ring_start():
        for k in range(2):
            for side in range(2):
                ring_send_sum(4, side, HALVES[side][k])
        for k in range(2):
            for side in range(2):
                ring_send_sum(3, side, HALVES[1 - side][k])

    def ring_sum(hop):
        for step in (2, 1, 3, 0):
            for side in range(2):
                if hop == 3 and step not in HALVES[side]:
                    continue
                sem = (side, hop, step)
                arrive(
                    ring_sums.at[sem],
                    ring_sum_send.at[sem],
                    ring_sum_recv.at[sem],
                    along_z[side],
                )
                if hop:
                    add(layer(sums, ahead(side, hop), plus(y, step)), ring_sums.at[sem])
                    ring_send_sum(hop, side, step)
            if hop == 0:
                add(
                    layer(sums, z, plus(y, step)),
                    ring_sums.at[0, 0, step],
                    ring_sums.at[1, 0, step],
                )
                at_y = plus(y, step)
                for dx in range(4):
                    if dx or step:
                        send(
                            sums.at[
                                lax.rem(at_y, 2) * 4 + plus(x, dx),
                                at_y // 2,
                                z,
                                :,
                                pl.ds(*PARTS[2]),
                            ],
                            xy_sums.at[4 * step + dx],
                            xy_sum_send.at[4 * step + dx],
                            xy_sum_recv.at[4 * step + dx],
                            device(plus(x, dx), at_y, z, core),
                        )

    def wide_add(part, step):
        narrow = plus(narrow_at[part], step)
        for side in range(2):
            sem = (part, side, step)
            arrive(
                landed(whole_one, *sem),
                whole_one_send.at[sem],
                whole_one_recv.at[sem],
                neighbours[wide_axis[part], side],
            )
        add(
            chunk(sums, part, wide_at[part], narrow),
            landed(whole_one, part, 0, step),
            landed(whole_one, part, 1, step),
        )
        if step:
            send(
                chunk(sums, part, wide_at[part], narrow),
                landed(whole_two, part, step - 1),
                whole_two_send.at[part, step - 1],
                whole_two_recv.at[part, step - 1],
                neighbours[narrow_axis[part], (0, 2, 1)[step - 1]],
            )

    def narrow_end(part):
        blocks_here = [landed(whole_two, part, k) for k in range(3)]
        for k in range(3):
            arrive(
                blocks_here[k],
                whole_two_send.at[part, k],
                whole_two_recv.at[part, k],
                neighbours[narrow_axis[part], k],
            )
        add(chunk(sums, part, wide_at[part], narrow_at[part]), *blocks_here)
        for step in (4, 3, 5, 2, 6, 1, 7):
            to = lax.rem(z + step, 8)
            send(
                sums.at[c, y_hi, to, :, pl.ds(*PARTS[part])],
                last.at[z, :, pl.ds(*PARTS[part])],
                last_send.at[part, to],
                last_recv.at[part, z],
                device(x, y, to, core),
            )

    earlier = taken()
    own(0, {3: lambda: far_send(0)})
    near_send(0)
    own(2, {})
    ring_start()
    own(1, {3: lambda: far_send(1)})
    near_send(1)
    near_add(0)
    ring_sum(3)
    near_add(1)
    ring_sum(2)
    wide_add(0, 2)
    ring_sum(1)
    drain(earlier)
    all_heads.wait_send()
    all_notes.wait_send()
    for copy in shared:
        copy.wait_send()
    wide_add(1, 2)
    for step in (1, 3, 0):
        for part in range(2):
            wide_add(part, step)
    ring_sum(0)
    earlier = taken()
    narrow_end(0)
    narrow_end(1)
    drain(earlier)
    for k in range(1, 16):
        dy, dx = k // 4, k % 4
        arrive(
            xy_sums.at[k],
            xy_sum_send.at[k],
            xy_sum_recv.at[k],
            device(plus(x, 4 - dx), plus(y, 4 - dy), z, core),
        )

    def finish(part, value):
        lanes = pl.ds(*PARTS[part])
        value = value + state[:, lanes] + sums[c, y_hi, z, :, lanes].astype(F32)
        out_ref[:, lanes] = value.astype(BF16)

    finish(2, sum(xy_sums[k].astype(F32) for k in range(1, 16)))
    for part in range(2):
        value = jnp.zeros((ROWS, PARTS[part][1]), F32)
        for step in range(1, 8):
            source = lax.rem(z + step, 8)
            block = last.at[source, :, pl.ds(*PARTS[part])]
            arrive(
                block,
                last_send.at[part, source],
                last_recv.at[part, source],
                device(x, y, source, core),
            )
            value = value + block[...].astype(F32)
        finish(part, value)

    drain(sent)


VMEM = pl.BlockSpec(memory_space=pltpu.VMEM)
SMEM = pl.BlockSpec(memory_space=pltpu.SMEM)
ANY = pl.BlockSpec(memory_space=pl.ANY)
DMA = pltpu.SemaphoreType.DMA


def per_device(
    queries,
    prompt_cache,
    new_latent,
    parents,
    lengths,
    value_weight,
    output_weight,
    residual,
    norm_gain,
    expert_ids,
    expert_weights,
    expert_gate,
    expert_up,
    expert_down,
):
    key_width = queries.shape[3]
    pairs = [(N_CTX,), (N_CTX,), None, (N_CTX,), None, (8,), (8,), (8,), None, (N_CTX,), None]
    pairs += [(8,), (16,), (2, 3), (2, 2, 4), (2, 4), (2, 4, 4), (3,)]
    pairs += [(2,), None, (2, 2, 2), (2, 2, 4), (2, 3), (2, 4, 4), (16,), (2, 8)]
    out = pl.pallas_call(
        layer_kernel,
        out_shape=jax.ShapeDtypeStruct((ROWS, COLS), BF16),
        in_specs=[SMEM, SMEM, ANY, ANY, VMEM, VMEM, VMEM, ANY, ANY, ANY, VMEM, ANY, ANY, ANY],
        out_specs=VMEM,
        scratch_shapes=[
            pltpu.VMEM((N_CTX, 128, key_width), BF16),
            pltpu.VMEM((key_width, prompt_cache.shape[1]), BF16),
            pltpu.VMEM(value_weight.shape, BF16),
            pltpu.VMEM((ROWS, COLS), BF16),
            pltpu.VMEM((256, COLS), BF16),
            pltpu.VMEM((N_CTX, 128, LAT), BF16),
            pltpu.VMEM((N_CTX, 8, 128), F32),
            pltpu.VMEM((N_CTX, 128, LAT), BF16),
            pltpu.VMEM((N_CTX, 8, 128), F32),
            pltpu.VMEM((3, 512, 512), BF16),
            pltpu.VMEM((N_EXP, ROWS, 128), BF16),
            pltpu.VMEM((N_EXP, ROWS, 128), BF16),
            pltpu.VMEM((256, COLS), BF16),
            pltpu.VMEM((N_CTX, 64, 256), BF16),
            pltpu.VMEM((2, 256, 256), BF16),
            pltpu.VMEM((256, 256), BF16),
            pltpu.VMEM((2, 8, ROWS, COLS), BF16),
            pltpu.VMEM((8, ROWS, COLS), BF16),
            pltpu.VMEM((8, ROWS, COLS), BF16),
            pltpu.VMEM((8, 2, ROWS, COLS - 512), BF16),
            pltpu.VMEM((2, ROWS, COLS - 512), BF16),
            pltpu.VMEM((ROWS, COLS - 512), BF16),
            pltpu.VMEM((N_CTX, ROWS, 128), F32),
            pltpu.VMEM((ROWS, COLS), F32),
            pltpu.VMEM((N_EXP, 1, 128), F32),
            pltpu.VMEM((N_EXP, 1, 128), F32),
            pltpu.VMEM((N_CTX, 2, 2, 8, ROWS, COLS), BF16),
            pltpu.VMEM((N_CTX, 2, 8, ROWS, COLS), BF16),
            pltpu.VMEM((2, 2, 2, 8, ROWS, 384), BF16),
            pltpu.VMEM((2, 2, 4, 8, ROWS, 384), BF16),
            pltpu.VMEM((2, 3, 8, ROWS, 384), BF16),
            pltpu.VMEM((2, 4, 4, 4, ROWS, 256), BF16),
            pltpu.VMEM((16, ROWS, 256), BF16),
            pltpu.VMEM((8, ROWS, COLS), BF16),
            pltpu.VMEM((512, 128), F32),
            pltpu.VMEM((256, 128), BF16),
            pltpu.VMEM((256, 256), BF16),
            pltpu.VMEM((N_CTX, COLS, 256), BF16),
            pltpu.VMEM((256, N_CTX * COLS), BF16),
            DMA((2,)),
            DMA((6,)),
        ]
        + [DMA(shape) if shape else DMA for shape in pairs for _ in range(2)],
        compiler_params=pltpu.CompilerParams(
            collective_id=0, has_side_effects=True, vmem_limit_bytes=VMEM_LIMIT
        ),
        name="layer",
    )(
        lengths,
        parents.reshape(8),
        queries.reshape(N_CTX, 128, key_width),
        prompt_cache[0].T,
        new_latent.reshape(ROWS, key_width),
        expert_ids.reshape(ROWS, 8),
        expert_weights.reshape(ROWS, 8),
        value_weight,
        output_weight,
        residual.reshape(ROWS, N_CTX * COLS),
        norm_gain.reshape(1, N_CTX * COLS),
        expert_gate.reshape(N_CTX, COLS, 128),
        expert_up.reshape(N_CTX, COLS, 128),
        expert_down[0],
    )
    return out.reshape(2, 8, COLS)


def solution(mesh):
    in_specs = (
        P(None, "exp", None, None),
        P("exp", "ctx", None),
        P(None, "exp", None),
        P("exp", None),
        P("exp"),
        P("exp", None, None),
        P("exp", None),
        P(None, "exp", None),
        P(),
        P(None, "exp", None),
        P(None, "exp", None),
        P("exp", None, "ctx"),
        P("exp", None, "ctx"),
        P("exp", "ctx", None),
    )
    out_specs = P(None, "exp", "ctx")
    return jax.shard_map(
        per_device, mesh=mesh, in_specs=in_specs, out_specs=out_specs, check_vma=False
    )
```
